128 devices in a mesh: dom: 32 (over y, x, core), grp: 4 (over z).
Axes of the slice: x: 4, y: 4, z: 4, core: 2. Of those that a mesh axis runs over, the one named last changes fastest.
Arguments:
- encoded: float32 [65536, 1024], P(('dom', 'grp')), may hold values from -6 to 6
- owner_of: int32 [65536], P(('dom', 'grp')), may hold values from 0 to 65535, as said below
- nbr_blocks: int32 [512, 16], P(('dom', 'grp')), may hold values from 0 to 15, as said below
- nbr_count: int32 [512], P(('dom', 'grp')), may hold values from 1 to 16, as said below
- edge_weights: bfloat16 [512, 16, 128, 128], P(('dom', 'grp')), may hold values from 0.01 to 16
Outputs:
- propagated: bfloat16 [65536, 1024], P(('dom', 'grp'))
The draws below stay inside these ranges and needn't reach their ends.
Inputs may be any that keep to these rules, and one draw needn't show every extreme that they name: owner_of is a permutation; the batch rows of each device go to the nodes of every device in equal numbers (512 / the device count to each), where device d owns nodes d * 512 to (d + 1) * 512 - 1. `nbr_blocks`: A partition group is the 2048 nodes of the devices that share a dom index; block g of a group is its nodes g * 128 to (g + 1) * 128 - 1. The first nbr_count[b] entries of row block b are distinct; later entries are padding and are ignored. `nbr_count`: some row block has exactly 16 live blocks.
All inputs are finite; a program needn't handle non-finite values.
Results may differ from the reference program's by a relative error of at most 0.005.
Values may be sent and summed in bfloat16 or wider, within the bound.
No kernel may reach another device: no remote copies, remote signals or barrier semaphores. Data moves between devices by JAX's collectives and lax.ppermute only.
A program may use at most 64 MiB of HBM per device.

```python
import math
import jax
import jax.numpy as jnp
from jax import lax

F = 1024
BLK = 128
DEG_MAX = 16
STEPS = 2
RB_DEV = 4
ROWS_DEV = 512
NODES = 65536
GROUP_BLOCKS = 16
N_GRP = 4


def draw_owner_of(key, part):
    device_total = NODES // ROWS_DEV
    share_rows = ROWS_DEV // device_total
    send_keys = jax.random.split(jax.random.fold_in(key, 11), device_total)
    recv_keys = jax.random.split(jax.random.fold_in(key, 12), device_total)
    slot_table = jax.vmap(lambda kk: jax.random.permutation(kk, ROWS_DEV))(send_keys).astype(jnp.int32)
    arrive_table = jax.vmap(lambda kk: jax.random.permutation(kk, ROWS_DEV))(recv_keys).astype(jnp.int32)
    source = jnp.arange(device_total, dtype=jnp.int32)[:, None]
    target_dev = slot_table // share_rows
    within = slot_table % share_rows
    arrival = source * share_rows + within
    owner_local = arrive_table[target_dev, arrival]
    return (target_dev * ROWS_DEV + owner_local).reshape(NODES).astype(jnp.int32)


def draw_nbr_blocks(key, part):
    block_total = NODES // BLK
    row_keys = jax.random.split(jax.random.fold_in(key, 21), block_total)
    picked = jax.vmap(lambda kk: jax.random.permutation(kk, GROUP_BLOCKS)[:DEG_MAX])(row_keys)
    return picked.astype(jnp.int32)


def draw_nbr_count(key, part):
    block_total = NODES // BLK
    device_total = block_total // RB_DEV
    level = jax.random.randint(jax.random.fold_in(key, 31), (device_total,), 0, 8)
    low_drawn = max(1, DEG_MAX * 3 // 16)
    high_drawn = max(low_drawn, DEG_MAX * 10 // 16)
    low_busy = max(1, DEG_MAX // 2)
    low_full = max(1, DEG_MAX * 3 // 4)
    floor_dev = jnp.where(level == 7, low_full, jnp.where(level == 6, low_busy, low_drawn))
    ceiling_dev = jnp.where(level >= 6, DEG_MAX, high_drawn)
    floor_rows = jnp.repeat(floor_dev, RB_DEV)
    ceiling_rows = jnp.repeat(ceiling_dev, RB_DEV)
    counts = jax.random.randint(jax.random.fold_in(key, 32), (block_total,), floor_rows, ceiling_rows + 1)
    full_row = jax.random.randint(jax.random.fold_in(key, 33), (), 0, block_total)
    counts = jnp.where(jnp.arange(block_total) == full_row, DEG_MAX, counts)
    return counts.astype(jnp.int32)


def draw_edge_weights(key, part):
    block_total = NODES // BLK
    low_log = math.log(0.3)
    high_log = math.log(3.0)
    jitter = jax.random.uniform(jax.random.fold_in(key, 43), (block_total, DEG_MAX, BLK, BLK), jnp.float32, 0.5, 1.5)
    row_factor = jnp.exp(jax.random.uniform(jax.random.fold_in(key, 41), (block_total, DEG_MAX, BLK, 1), jnp.float32, low_log, high_log))
    col_factor = jnp.exp(jax.random.uniform(jax.random.fold_in(key, 42), (block_total, DEG_MAX, 1, BLK), jnp.float32, low_log, high_log))
    return (row_factor * col_factor * jitter).astype(jnp.bfloat16)


def steps_of(key, extent, pieces, low, largest):
    factor_of = 1.0
    for axis_at, blocks in pieces:
        draws = jax.random.uniform(jax.random.fold_in(jax.random.fold_in(key, 6), axis_at), (blocks,), jnp.float32, low / len(pieces), largest / len(pieces))
        factor_of = factor_of * jnp.repeat(jnp.exp(draws), extent[axis_at] // blocks).reshape((-1,) + (1,) * (len(extent) - 1 - axis_at))
    return factor_of


def centred(own_key, extent, width, bound, pieces=(), held_as=jnp.bfloat16):
    values = jax.random.normal(own_key, extent, jnp.float32) * width
    if len(pieces) > 0:
        values = steps_of(own_key, extent, pieces, -0.22, 0.18) * values
    return jnp.clip(values, min=-bound, max=bound).astype(held_as)


def setup_inputs(seed: int = 0) -> dict:
    key_list = jax.random.split(jax.random.key(seed), 6)
    encoded = centred(key_list[0], (NODES, F), 1.0, 6.0, ((0, 128),), jnp.float32)
    owner_of = draw_owner_of(jax.random.fold_in(key_list[5], 71), 0)
    nbr_blocks = draw_nbr_blocks(jax.random.fold_in(key_list[5], 71), 0)
    nbr_count = draw_nbr_count(jax.random.fold_in(key_list[5], 71), 0)
    edge_weights = draw_edge_weights(jax.random.fold_in(key_list[5], 71), 0)
    return {"encoded": encoded, "owner_of": owner_of, "nbr_blocks": nbr_blocks, "nbr_count": nbr_count, "edge_weights": edge_weights}


mix_weight = 0.3

def reference(encoded, owner_of, nbr_blocks, nbr_count, edge_weights):
    node_count, feat_width = encoded.shape
    block_count = node_count // BLK
    base_rows = jnp.zeros((node_count, feat_width), jnp.float32).at[owner_of].set(encoded.astype(jnp.float32))
    group_span = RB_DEV * N_GRP
    offsets = jnp.arange(block_count, dtype=jnp.int32) // group_span * group_span
    target = (nbr_blocks + offsets[:, None]).astype(jnp.int32)
    live_slots = jnp.arange(DEG_MAX, dtype=jnp.int32)[None, :] < nbr_count[:, None]
    row_sums = lax.optimization_barrier(jnp.sum(edge_weights, axis=3, dtype=jnp.float32))
    degree = lax.optimization_barrier(jnp.sum(jnp.where(live_slots[:, :, None], row_sums, jnp.float32(0.0)), axis=1))
    row_scale = lax.rsqrt(degree)[:, :, None]
    base_blocks = base_rows.reshape(block_count, BLK, feat_width)
    hidden = base_rows.astype(jnp.bfloat16).reshape(block_count, BLK, feat_width)
    for step_index in range(STEPS):

        def add_slot(running, slot_index, hidden=hidden):
            columns = jnp.take(hidden, target[:, slot_index], axis=0).astype(jnp.float32)
            weights = edge_weights[:, slot_index].astype(jnp.float32)
            product_term = jnp.einsum('bpq,bqf->bpf', weights, columns)
            keep_slot = live_slots[:, slot_index][:, None, None]
            return (running + jnp.where(keep_slot, product_term, jnp.float32(0.0)), None)
        running, _ = lax.scan(add_slot, jnp.zeros((block_count, BLK, feat_width), jnp.float32), jnp.arange(DEG_MAX, dtype=jnp.int32))
        hidden = (mix_weight * base_blocks + (1.0 - mix_weight) * running * row_scale).astype(jnp.bfloat16)
    return hidden.reshape(node_count, feat_width)
```

```python
import functools

import jax
import jax.numpy as jnp
from jax import lax
from jax.experimental import pallas as pl
from jax.experimental.pallas import tpu as pltpu
from jax.sharding import PartitionSpec as P

AXES = ("dom", "grp")
MIX = 0.3
CHUNKS = 2
VMEM = pl.BlockSpec(memory_space=pltpu.VMEM)
SMEM = pl.BlockSpec(memory_space=pltpu.SMEM)


def kernel_call(body, out_shape, in_specs, flops, moved, scratch=(), limit=40):
    outs = out_shape if isinstance(out_shape, (tuple, list)) else (out_shape,)
    specs = tuple(VMEM for _ in outs)
    return pl.pallas_call(
        body,
        out_shape=out_shape,
        in_specs=in_specs,
        out_specs=specs if isinstance(out_shape, (tuple, list)) else specs[0],
        scratch_shapes=scratch,
        compiler_params=pltpu.CompilerParams(vmem_limit_bytes=limit * 1024 * 1024),
        cost_estimate=pl.CostEstimate(flops=flops, bytes_accessed=moved, transcendentals=0),
    )


def sort_kernel(doms, flip_ref, owner_ref, enc_ref, other_ref, mine_ref):
    rows, width = enc_ref.shape
    half = width // 2
    per = rows // doms
    owner = owner_ref[...]
    group_nodes = rows * 4
    tdom = owner // group_nodes
    place = (owner - tdom * group_nodes).astype(jnp.float32)
    hot = (lax.broadcasted_iota(jnp.int32, (doms, rows), 0) == tdom).astype(jnp.float32)
    before = (
        lax.broadcasted_iota(jnp.int32, (rows, rows), 0)
        < lax.broadcasted_iota(jnp.int32, (rows, rows), 1)
    ).astype(jnp.bfloat16)
    seen = jnp.dot(hot.astype(jnp.bfloat16), before, preferred_element_type=jnp.float32)
    rank = jnp.sum(hot * seen, axis=0, keepdims=True)
    slot = tdom * per + rank.astype(jnp.int32)
    pick = lax.broadcasted_iota(jnp.int32, (rows, rows), 0) == slot
    place_of = jnp.sum(jnp.where(pick, place, 0.0), axis=1, keepdims=True)
    pick = pick.astype(jnp.bfloat16)
    slot_row = lax.broadcasted_iota(jnp.int32, (rows, 1), 0)
    parity = (slot_row // per) % 2
    upper = jnp.where(parity == 0, flip_ref[0], flip_ref[1]) == 1
    moved = jnp.dot(pick, enc_ref[...].astype(jnp.bfloat16), preferred_element_type=jnp.float32)
    low, high = moved[:, :half], moved[:, half:]
    other_ref[:, :half] = jnp.where(upper, low, high).astype(jnp.bfloat16)
    mine_ref[...] = jnp.where(upper, high, low).astype(jnp.bfloat16)
    place_of = place_of.astype(jnp.int32)
    lane = lax.broadcasted_iota(jnp.int32, (rows, 128), 1)
    coded = jnp.where(lane == 0, place_of // 64, jnp.where(lane == 1, place_of % 64, 0))
    other_ref[:, half:] = coded.astype(jnp.float32).astype(jnp.bfloat16)


def place_kernel(arrived_ref, places_ref, rows_ref):
    rows, width = rows_ref.shape
    lane = lax.broadcasted_iota(jnp.int32, (8, 128), 1)
    weight = jnp.where(lane == 0, 64.0, jnp.where(lane == 1, 1.0, 0.0)).astype(jnp.bfloat16)
    places_ref[...] = lax.dot_general(
        weight, arrived_ref[:, width:], (((1,), (1,)), ((), ())), preferred_element_type=jnp.float32
    )
    rows_ref[...] = arrived_ref[:, :width]


def dense_kernel(count_ref, column_ref, weight_ref, dense_ref, scale_ref):
    blocks, _, size, _ = weight_ref.shape
    for b in range(blocks):
        span = pl.ds(b * size, size)
        dense_ref[span, :] = jnp.zeros((size, dense_ref.shape[1]), dense_ref.dtype)

        def put(k, total):
            block = weight_ref[b, k]
            start = pl.multiple_of(column_ref[b, k] * size, size)
            dense_ref[span, pl.ds(start, size)] = block
            return total + block.astype(jnp.float32)

        total = lax.fori_loop(0, count_ref[b], put, jnp.zeros((size, size), jnp.float32))
        degree = jnp.sum(total, axis=1, keepdims=True)
        scale_ref[span, :] = jnp.broadcast_to((1.0 - MIX) * lax.rsqrt(degree), (size, 128))


def scatter_kernel(fz_ref, own_at, row_at, both_at, last_at, own_ref, row_ref, both_ref, part_ref, last_pick_ref):
    nodes = part_ref.shape[0]
    rx, fx = fz_ref[0], fz_ref[1]
    z = fz_ref[2]
    size = own_ref.shape[0]

    def local(at):
        p = at[0:1, :].astype(jnp.int32)
        step = (p // size) ^ z
        where = jnp.where(step == 0, 0, jnp.where(step == rx, 1, jnp.where(step == fx, 2, 3)))
        return where * size + p % size

    spots = [local(a) for a in (own_at, row_at, both_at, last_at)]
    tile = 256

    def one(t, _):
        base = pl.multiple_of(t * tile, tile)
        node = lax.broadcasted_iota(jnp.int32, (tile, size), 0) + base
        picks = [(node == s).astype(jnp.bfloat16) for s in spots]
        total = jnp.dot(picks[0], own_ref[...], preferred_element_type=jnp.float32)
        total += jnp.dot(picks[1], row_ref[...], preferred_element_type=jnp.float32)
        total += jnp.dot(picks[2], both_ref[...], preferred_element_type=jnp.float32)
        part_ref[pl.ds(base, tile), :] = total.astype(jnp.bfloat16)
        last_pick_ref[pl.ds(base, tile), :] = picks[3]
        return 0

    lax.fori_loop(0, nodes // tile, one, 0)


def first_kernel(col, dense_a, dense_b, scale_a, scale_b, part_ref, last_pick_ref, last_ref, base_ref, hidden_ref, panel):
    width = hidden_ref.shape[1]
    cols = pl.ds(col * width, width)
    nodes = part_ref.shape[0]
    tile = 256
    last = last_ref[:, cols]

    def one(t, _):
        at = pl.ds(pl.multiple_of(t * tile, tile), tile)
        fresh = jnp.dot(last_pick_ref[at, :], last, preferred_element_type=jnp.float32)
        panel[at, :] = (part_ref[at, cols].astype(jnp.float32) + fresh).astype(jnp.bfloat16)
        return 0

    lax.fori_loop(0, nodes // tile, one, 0)
    size = dense_a.shape[0]
    for n, (dense, scale) in enumerate(((dense_a, scale_a), (dense_b, scale_b))):

        def two(t, _):
            at = pl.ds(pl.multiple_of(t * tile, tile), tile)
            to = pl.ds(pl.multiple_of(t * tile + n * size, tile), tile)
            total = jnp.dot(dense[at, :], panel[...], preferred_element_type=jnp.float32)
            base = panel[to, :]
            base_ref[to, :] = base
            hidden_ref[to, :] = (MIX * base.astype(jnp.float32) + total * scale[at, 0:1]).astype(jnp.bfloat16)
            return 0

        lax.fori_loop(0, size // tile, two, 0)


def half_kernel(dense_a, dense_b, hidden_ref, total_ref):
    size = dense_a.shape[0]
    depth = hidden_ref.shape[0]
    tile = 256
    for n, dense in enumerate((dense_a, dense_b)):

        def one(t, _):
            at = pl.ds(pl.multiple_of(t * tile, tile), tile)
            to = pl.ds(pl.multiple_of(t * tile + n * size, tile), tile)
            total_ref[to, :] = jnp.dot(dense[at, :depth], hidden_ref[...], preferred_element_type=jnp.float32)
            return 0

        lax.fori_loop(0, size // tile, one, 0)


def last_kernel(dense_a, dense_b, scale_a, scale_b, total_ref, hidden_ref, base_ref, keep_ref, send_ref):
    size = dense_a.shape[0]
    depth = hidden_ref.shape[0]
    tile = 256
    for n, (dense, scale, out) in enumerate(((dense_a, scale_a, keep_ref), (dense_b, scale_b, send_ref))):

        def one(t, _):
            at = pl.ds(pl.multiple_of(t * tile, tile), tile)
            to = pl.ds(pl.multiple_of(t * tile + n * size, tile), tile)
            total = total_ref[to, :] + jnp.dot(
                dense[at, depth:], hidden_ref[...], preferred_element_type=jnp.float32
            )
            out[at, :] = (MIX * base_ref[to, :].astype(jnp.float32) + total * scale[at, 0:1]).astype(jnp.bfloat16)
            return 0

        lax.fori_loop(0, size // tile, one, 0)


def row_step(core):
    return 1 if core == 0 else 3


def upper_half(core, z):
    return int(z in (1, 2)) if core == 0 else z // 2


def shards(doms, depth, encoded, owner_of, nbr_blocks, nbr_count, edge_weights):
    f32, bf16, i32 = jnp.float32, jnp.bfloat16, jnp.int32
    rows, width = encoded.shape
    half = width // 2
    blocks, slots, size, _ = edge_weights.shape
    nodes = rows * depth
    part = half // CHUNKS
    z = lax.axis_index("grp").astype(i32)
    core = (lax.axis_index("dom") % 2).astype(i32)
    rx = jnp.where(core == 0, 1, 3).astype(i32)
    fx = jnp.where(core == 0, 3, 1).astype(i32)
    halves = jnp.array([[upper_half(c, q) for c in range(2)] for q in range(depth)], i32)
    flips = halves[z]
    upper = flips[core]
    row_pairs = [(d * depth + q, d * depth + (q ^ row_step(d % 2))) for d in range(doms) for q in range(depth)]
    col_pairs = [(d * depth + q, d * depth + (q ^ row_step(1 - d % 2))) for d in range(doms) for q in range(depth)]
    both_pairs = [(d * depth + q, d * depth + (q ^ 2)) for d in range(doms) for q in range(depth)]

    def to_row(a):
        return lax.ppermute(a, AXES, row_pairs)

    def to_col(a):
        return lax.ppermute(a, AXES, col_pairs)

    lists = jnp.concatenate([nbr_blocks, jnp.broadcast_to(nbr_count[:, None], (blocks, slots))], 0)
    far_weights = to_row(edge_weights)
    far_lists = to_row(lists)

    def columns(table):
        step = (table // blocks) ^ z
        where = jnp.where(step == 0, 0, jnp.where(step == rx, 1, jnp.where(step == fx, 2, 3)))
        return (where * blocks + table % blocks).astype(i32)

    def dense_of(lists, weights):
        return kernel_call(
            dense_kernel,
            (jax.ShapeDtypeStruct((blocks * size, nodes), bf16), jax.ShapeDtypeStruct((blocks * size, 128), f32)),
            [SMEM, SMEM, VMEM],
            0,
            8 << 20,
        )(lists[blocks:, 0], columns(lists[:blocks]), weights)

    other, mine = kernel_call(
        functools.partial(sort_kernel, doms),
        (jax.ShapeDtypeStruct((rows, half + 128), bf16), jax.ShapeDtypeStruct((rows, half), bf16)),
        [SMEM, VMEM, VMEM],
        2 * rows * rows * width,
        4 << 20,
    )(flips, owner_of.reshape(1, rows), encoded)

    got_other = lax.all_to_all(other, "dom", 0, 0, tiled=True)
    got_mine = lax.all_to_all(mine, "dom", 0, 0, tiled=True)
    own_at, got_other = kernel_call(
        place_kernel,
        (jax.ShapeDtypeStruct((8, rows), f32), jax.ShapeDtypeStruct((rows, half), bf16)),
        [VMEM],
        1 << 20,
        1 << 20,
    )(got_other)
    row_at, last_at, both_at = (
        to_row(own_at),
        to_col(own_at),
        lax.ppermute(own_at, AXES, both_pairs),
    )
    row_rows = to_row(got_other)
    both_rows = to_col(row_rows)
    last_rows = to_col(got_mine)

    dense_a, scale_a = dense_of(lists, edge_weights)
    dense_b, scale_b = dense_of(far_lists, far_weights)

    placed, last_pick = kernel_call(
        scatter_kernel,
        (jax.ShapeDtypeStruct((nodes, half), bf16), jax.ShapeDtypeStruct((nodes, rows), bf16)),
        [SMEM] + [VMEM] * 7,
        2 * nodes * 3 * rows * half,
        8 << 20,
    )(jnp.stack([rx, fx, z]), own_at, row_at, both_at, last_at, got_mine, row_rows, both_rows)

    mine_n = 2 * rows
    kept, sent = [], []
    for c in range(CHUNKS):
        base, hidden = kernel_call(
            functools.partial(first_kernel, c),
            (jax.ShapeDtypeStruct((mine_n, part), bf16), jax.ShapeDtypeStruct((mine_n, part), bf16)),
            [VMEM] * 7,
            2 * nodes * rows * part + 2 * mine_n * nodes * part,
            8 << 20,
            scratch=[pltpu.VMEM((nodes, part), bf16)],
        )(dense_a, dense_b, scale_a, scale_b, placed, last_pick, last_rows)
        far_hidden = to_col(hidden)
        total = kernel_call(
            half_kernel,
            jax.ShapeDtypeStruct((mine_n, part), f32),
            [VMEM] * 3,
            2 * mine_n * mine_n * part,
            4 << 20,
        )(dense_a, dense_b, hidden)
        keep, send = kernel_call(
            last_kernel,
            (jax.ShapeDtypeStruct((rows, part), bf16), jax.ShapeDtypeStruct((rows, part), bf16)),
            [VMEM] * 7,
            2 * mine_n * mine_n * part,
            4 << 20,
        )(dense_a, dense_b, scale_a, scale_b, total, far_hidden, base)
        kept.append(keep)
        sent.append(to_row(send))
    kept = jnp.concatenate(kept, 1)
    sent = jnp.concatenate(sent, 1)
    low = jnp.where(upper == 0, kept, sent)
    high = jnp.where(upper == 0, sent, kept)
    return jnp.concatenate([low, high], 1)


def solution(mesh):
    return jax.shard_map(
        functools.partial(shards, mesh.shape["dom"], mesh.shape["grp"]),
        mesh=mesh,
        in_specs=(P(AXES, None), P(AXES), P(AXES, None), P(AXES), P(AXES, None, None, None)),
        out_specs=P(AXES, None),
        check_vma=False,
    )
```

```python
import functools

import jax
import jax.numpy as jnp
from jax import lax
from jax.experimental import pallas as pl
from jax.experimental.pallas import tpu as pltpu
from jax.sharding import PartitionSpec as P

AXES = ("dom", "grp")
MIX = 0.3
CHUNKS = 2
VMEM = pl.BlockSpec(memory_space=pltpu.VMEM)
SMEM = pl.BlockSpec(memory_space=pltpu.SMEM)
ANY = pl.BlockSpec(memory_space=pl.ANY)


def kernel_call(body, out_shape, in_specs, flops, moved, scratch=(), limit=10):
    outs = out_shape if isinstance(out_shape, (tuple, list)) else (out_shape,)
    specs = tuple(VMEM for _ in outs)
    return pl.pallas_call(
        body,
        out_shape=out_shape,
        in_specs=in_specs,
        out_specs=specs if isinstance(out_shape, (tuple, list)) else specs[0],
        scratch_shapes=scratch,
        compiler_params=pltpu.CompilerParams(vmem_limit_bytes=limit * 1024 * 1024),
        cost_estimate=pl.CostEstimate(flops=flops, bytes_accessed=moved, transcendentals=0),
    )


def half_of(core_is_odd, z):
    return jnp.where(core_is_odd, z // 2, ((z + 1) // 2) % 2)


def sort_kernel(doms, owner_hbm, enc_ref, other_0, other_1, pick_ref, place_ref, enc, owner_ref, sems):
    rows, width = enc_ref.shape
    half = width // 2
    z = lax.axis_index("grp")
    first = pltpu.make_async_copy(owner_hbm, owner_ref, sems.at[2])
    first.start()
    loads = []
    for core in range(2):
        start = pl.multiple_of((1 - half_of(core == 1, z)) * half, half)
        loads.append(pltpu.make_async_copy(enc_ref.at[:, pl.ds(start, half)], enc.at[core], sems.at[core]))
    for load in loads:
        load.start()
    per = rows // doms
    before = (
        lax.broadcasted_iota(jnp.int32, (rows, rows), 0)
        < lax.broadcasted_iota(jnp.int32, (rows, rows), 1)
    ).astype(jnp.bfloat16)
    first.wait()
    owner = owner_ref[...]
    group_nodes = rows * 4
    tdom = owner // group_nodes
    place = owner - tdom * group_nodes
    hot = (lax.broadcasted_iota(jnp.int32, (doms, rows), 0) == tdom).astype(jnp.float32)
    seen = jnp.dot(hot.astype(jnp.bfloat16), before, preferred_element_type=jnp.float32)
    rank = jnp.sum(hot * seen, axis=0, keepdims=True)
    block = (tdom % 2) * (doms // 2) + tdom // 2
    slot = block * per + rank.astype(jnp.int32)
    pick_ref[...] = (lax.broadcasted_iota(jnp.int32, (rows, rows), 0) == slot).astype(jnp.bfloat16)
    line = lax.broadcasted_iota(jnp.int32, (16, rows), 0)
    coded = jnp.where(line == 0, place // 64, jnp.where(line == 1, place % 64, 0))
    places = lax.dot_general(
        coded.astype(jnp.float32).astype(jnp.bfloat16),
        pick_ref[...],
        (((1,), (1,)), ((), ())),
        preferred_element_type=jnp.float32,
    ).astype(jnp.bfloat16)
    place_ref[...] = places
    part = rows // 2
    for core, out in enumerate((other_0, other_1)):
        out[part:, :part] = places[:, core * part : (core + 1) * part]
        out[part:, part:] = jnp.zeros((16, half - part), jnp.bfloat16)
        loads[core].wait()
        out[:part, :] = jnp.dot(
            pick_ref[pl.ds(core * part, part), :],
            enc[core].astype(jnp.bfloat16),
            preferred_element_type=jnp.float32,
        ).astype(jnp.bfloat16)


def mine_kernel(enc_ref, pick_ref, mine_ref, enc, sems):
    rows, width = enc_ref.shape
    half = width // 2
    z = lax.axis_index("grp")
    loads = []
    for core in range(2):
        start = pl.multiple_of(half_of(core == 1, z) * half, half)
        loads.append(pltpu.make_async_copy(enc_ref.at[:, pl.ds(start, half)], enc.at[core], sems.at[core]))
    for load in loads:
        load.start()
    for core in range(2):
        span = pl.ds(core * rows // 2, rows // 2)
        loads[core].wait()
        mine_ref[span, :] = jnp.dot(
            pick_ref[span, :], enc[core].astype(jnp.bfloat16), preferred_element_type=jnp.float32
        ).astype(jnp.bfloat16)


def pack_kernel(mine_ref, place_ref, row_0, row_1, out_ref):
    rows, half = mine_ref.shape
    part = half // CHUNKS
    line = lax.broadcasted_iota(jnp.int32, (16, 128), 0)
    lane = lax.broadcasted_iota(jnp.int32, (16, 128), 1)
    for core, row in enumerate((row_0, row_1)):
        span = pl.ds(core * rows // 2, rows // 2)
        for c in range(CHUNKS):
            cols = pl.ds(c * part, part)
            out_ref[span, 2 * c * part : (2 * c + 1) * part] = mine_ref[span, cols]
            out_ref[span, (2 * c + 1) * part : (2 * c + 2) * part] = row[: rows // 2, cols]
        total = jnp.zeros((rows // 2, 128), jnp.float32)
        for n, lines in enumerate((place_ref[:, span], row[rows // 2 :, : rows // 2])):
            spread = ((lane == line + 2 * n) & (line < 2)).astype(jnp.bfloat16)
            total += lax.dot_general(
                lines, spread, (((0,), (0,)), ((), ())), preferred_element_type=jnp.float32
            )
        out_ref[span, 2 * half :] = total.astype(jnp.bfloat16)


def place_kernel(arrived_ref, *outs):
    rows = arrived_ref.shape[0]
    part = outs[0].shape[1]
    line = lax.broadcasted_iota(jnp.int32, (16, 128), 0)
    lane = lax.broadcasted_iota(jnp.int32, (16, 128), 1)
    spread = ((lane == line) & (line < 4)).astype(jnp.bfloat16)
    outs[0][rows:, :] = lax.dot_general(
        spread, arrived_ref[:, len(outs) * part :], (((1,), (1,)), ((), ())), preferred_element_type=jnp.float32
    ).astype(jnp.bfloat16)
    for c, out in enumerate(outs):
        out[:rows, :] = arrived_ref[:, c * part : (c + 1) * part]


def dense_kernel(list_ref, count_ref, weight_ref, dense_ref, scale_ref, held, sems):
    blocks, _, size, _ = weight_ref.shape
    dom, z = lax.axis_index("dom"), lax.axis_index("grp")
    loads = [pltpu.make_async_copy(weight_ref.at[b], held.at[b], sems.at[b]) for b in range(blocks)]
    for load in loads:
        load.start()
    for b in range(blocks):
        dense_ref[pl.ds(b * size, size), :] = jnp.zeros((size, dense_ref.shape[1]), dense_ref.dtype)
    for b in range(blocks):
        span = pl.ds(b * size, size)
        loads[b].wait()

        def put(k, total):
            block = held[b, k]
            target = list_ref[b, k]
            column = steps_of(dom, z, target // blocks) * blocks + target % blocks
            start = pl.multiple_of(column * size, size)
            dense_ref[span, pl.ds(start, size)] = block
            return total + block.astype(jnp.float32)

        total = lax.fori_loop(0, count_ref[b], put, jnp.zeros((size, size), jnp.float32))
        degree = jnp.sum(total, axis=1, keepdims=True)
        scale_ref[span, :] = jnp.broadcast_to((1.0 - MIX) * lax.rsqrt(degree), (size, 128))


def steps_of(dom, z, q):
    odd = dom % 2 == 1
    rx, fx = jnp.where(odd, 3, 1), jnp.where(odd, 1, 3)
    step = q ^ z
    return jnp.where(step == 0, 0, jnp.where(step == rx, 1, jnp.where(step == fx, 2, 3)))


def pick_kernel(order, rows_ref, pick_ref):
    nodes, size = pick_ref.shape[1:]
    dom, z = lax.axis_index("dom"), lax.axis_index("grp")
    coded = rows_ref[pl.ds(size, 16), :].astype(jnp.float32).astype(jnp.int32)
    for k, n in enumerate(order):
        p = coded[2 * n : 2 * n + 1, :] * 64 + coded[2 * n + 1 : 2 * n + 2, :]
        spot = steps_of(dom, z, p // size) * size + p % size
        for n in range(nodes // size):
            node = lax.broadcasted_iota(jnp.int32, (size, size), 0) + n * size
            pick_ref[k, pl.ds(n * size, size), :] = (node == spot).astype(jnp.bfloat16)


def part_kernel(pick_ref, near_ref, part_ref):
    size, width = pick_ref.shape[2], part_ref.shape[1]
    for n in range(part_ref.shape[0] // size):
        at = pl.ds(n * size, size)
        total = jnp.dot(pick_ref[0, at, :], near_ref[:size, :width], preferred_element_type=jnp.float32)
        total += jnp.dot(pick_ref[1, at, :], near_ref[:size, width:], preferred_element_type=jnp.float32)
        part_ref[at, :] = total.astype(jnp.bfloat16)


def first_kernel(dense_a, dense_b, scale_a, scale_b, pick_ref, part_ref, far_ref, base_ref, hidden_ref, panel):
    size = dense_a.shape[0]
    width = part_ref.shape[1]
    for n in range(panel.shape[0] // size):
        at = pl.ds(n * size, size)
        total = jnp.dot(pick_ref[0, at, :], far_ref[:size, :width], preferred_element_type=jnp.float32)
        total += jnp.dot(pick_ref[1, at, :], far_ref[:size, width:], preferred_element_type=jnp.float32)
        panel[at, :] = part_ref[at, :] + total.astype(jnp.bfloat16)
    for n, (dense, scale) in enumerate(((dense_a, scale_a), (dense_b, scale_b))):
        at = pl.ds(n * size, size)
        total = jnp.dot(dense[...], panel[...], preferred_element_type=jnp.float32)
        base = panel[at, :]
        base_ref[at, :] = base
        hidden_ref[at, :] = (MIX * base.astype(jnp.float32) + total * scale[:, 0:1]).astype(jnp.bfloat16)


def half_kernel(dense_a, dense_b, hidden_ref, total_ref):
    size = dense_a.shape[0]
    depth = hidden_ref.shape[0]
    for n, dense in enumerate((dense_a, dense_b)):
        total_ref[pl.ds(n * size, size), :] = jnp.dot(
            dense[:, :depth], hidden_ref[...], preferred_element_type=jnp.float32
        )


def last_kernel(dense_a, dense_b, scale_a, scale_b, total_ref, hidden_ref, base_ref, keep_ref, send_ref):
    size = dense_a.shape[0]
    depth = hidden_ref.shape[0]
    for n, (dense, scale, out) in enumerate(((dense_a, scale_a, keep_ref), (dense_b, scale_b, send_ref))):
        at = pl.ds(n * size, size)
        total = total_ref[at, :] + jnp.dot(dense[:, depth:], hidden_ref[...], preferred_element_type=jnp.float32)
        out[...] = (MIX * base_ref[at, :].astype(jnp.float32) + total * scale[:, 0:1]).astype(jnp.bfloat16)


def join_kernel(keep_0, keep_1, got_0, got_1, out_ref, sems):
    part = keep_0.shape[1]
    dom, z = lax.axis_index("dom"), lax.axis_index("grp")
    upper = half_of(dom % 2 == 1, z)
    copies = []
    for n, piece in enumerate((keep_0, keep_1, got_0, got_1)):
        start = (upper if n < 2 else 1 - upper) * 2 * part + (n % 2) * part
        copies.append(
            pltpu.make_async_copy(piece, out_ref.at[:, pl.ds(pl.multiple_of(start, part), part)], sems.at[n])
        )
    for copy in copies:
        copy.start()
    for copy in copies:
        copy.wait()


def row_step(core):
    return 1 if core == 0 else 3


def shards(doms, depth, encoded, owner_of, nbr_blocks, nbr_count, edge_weights):
    f32, bf16, i32 = jnp.float32, jnp.bfloat16, jnp.int32
    rows, width = encoded.shape
    half = width // 2
    blocks, slots, size, _ = edge_weights.shape
    nodes = rows * depth
    part = half // CHUNKS
    devices = [(d, q) for d in range(doms) for q in range(depth)]
    row_pairs = [(d * depth + q, d * depth + (q ^ row_step(d % 2))) for d, q in devices]
    col_pairs = [(d * depth + q, d * depth + (q ^ row_step(1 - d % 2))) for d, q in devices]
    core_major = [[d for core in range(2) for d in range(core, doms, 2)]]

    def to_row(a):
        return lax.ppermute(a, AXES, row_pairs)

    def to_col(a):
        return lax.ppermute(a, AXES, col_pairs)

    def to_row_of(core, a):
        return lax.ppermute(a, AXES, [(d * depth + q, d * depth + (q ^ row_step(core))) for d, q in devices])

    far_blocks, far_count = to_row(nbr_blocks), to_row(nbr_count)

    def dense_of(lists, count, weights, limit):
        return kernel_call(
            dense_kernel,
            (jax.ShapeDtypeStruct((blocks * size, nodes), bf16), jax.ShapeDtypeStruct((blocks * size, 128), f32)),
            [SMEM, SMEM, ANY],
            0,
            8 << 20,
            scratch=[pltpu.VMEM(weights.shape, bf16), pltpu.SemaphoreType.DMA((blocks,))],
            limit=limit,
        )(lists, count, weights)

    held = pltpu.VMEM((2, rows, half), f32)
    other = jax.ShapeDtypeStruct((rows // 2 + 16, half), bf16)
    other_0, other_1, pick, place = kernel_call(
        functools.partial(sort_kernel, doms),
        (other, other, jax.ShapeDtypeStruct((rows, rows), bf16), jax.ShapeDtypeStruct((16, rows), bf16)),
        [ANY, ANY],
        2 * rows * rows * half,
        4 << 20,
        scratch=[held, pltpu.VMEM((1, rows), i32), pltpu.SemaphoreType.DMA((3,))],
        limit=58,
    )(owner_of.reshape(1, rows), encoded)
    row_0, row_1 = to_row_of(0, other_0), to_row_of(1, other_1)
    mine = kernel_call(
        mine_kernel,
        jax.ShapeDtypeStruct((rows, half), bf16),
        [ANY, VMEM],
        2 * rows * rows * half,
        4 << 20,
        scratch=[held, pltpu.SemaphoreType.DMA((2,))],
        limit=50,
    )(encoded, pick)
    sent_weights, row_0, row_1, far_blocks, far_count = lax.optimization_barrier(
        (edge_weights, row_0, row_1, far_blocks, far_count)
    )
    far_weights = to_row(sent_weights)
    packed = kernel_call(
        pack_kernel,
        jax.ShapeDtypeStruct((rows, width + 128), bf16),
        [VMEM] * 4,
        1 << 20,
        2 << 20,
    )(mine, place, row_0, row_1)

    packed = lax.all_to_all(packed, "dom", 0, 0, axis_index_groups=core_major, tiled=True)
    near_rows = kernel_call(
        place_kernel,
        tuple(jax.ShapeDtypeStruct((rows + (16 if c == 0 else 0), 2 * part), bf16) for c in range(CHUNKS)),
        [VMEM],
        1 << 20,
        1 << 20,
    )(packed)
    far_rows = [to_col(a) for a in near_rows]

    dense_a, scale_a = dense_of(nbr_blocks, nbr_count, edge_weights, 50)
    dense_b, scale_b = dense_of(far_blocks, far_count, far_weights, 10)

    def picks_of(order, first_rows):
        return kernel_call(
            functools.partial(pick_kernel, order),
            jax.ShapeDtypeStruct((2, nodes, rows), bf16),
            [VMEM],
            1 << 20,
            4 << 20,
        )(first_rows)

    near_picks, far_picks = picks_of((0, 1), near_rows[0]), picks_of((0, 1), far_rows[0])

    mine_n = 2 * rows
    kept, sent = [], []
    for c in range(CHUNKS):
        placed = kernel_call(
            part_kernel,
            jax.ShapeDtypeStruct((nodes, part), bf16),
            [VMEM] * 2,
            4 * nodes * rows * part,
            4 << 20,
        )(near_picks, near_rows[c])
        base, hidden = kernel_call(
            first_kernel,
            (jax.ShapeDtypeStruct((mine_n, part), bf16), jax.ShapeDtypeStruct((mine_n, part), bf16)),
            [VMEM] * 7,
            4 * nodes * rows * part + 2 * mine_n * nodes * part,
            4 << 20,
            scratch=[pltpu.VMEM((nodes, part), bf16)],
        )(dense_a, dense_b, scale_a, scale_b, far_picks, placed, far_rows[c])
        far_hidden = to_col(hidden)
        running = kernel_call(
            half_kernel,
            jax.ShapeDtypeStruct((mine_n, part), f32),
            [VMEM] * 3,
            2 * mine_n * mine_n * part,
            4 << 20,
        )(dense_a, dense_b, hidden)
        keep, send = kernel_call(
            last_kernel,
            (jax.ShapeDtypeStruct((rows, part), bf16), jax.ShapeDtypeStruct((rows, part), bf16)),
            [VMEM] * 7,
            2 * mine_n * mine_n * part,
            4 << 20,
        )(dense_a, dense_b, scale_a, scale_b, running, far_hidden, base)
        kept.append(keep)
        sent.append(to_row(send))
    return pl.pallas_call(
        join_kernel,
        out_shape=jax.ShapeDtypeStruct((rows, width), bf16),
        in_specs=[VMEM] * 4,
        out_specs=ANY,
        scratch_shapes=[pltpu.SemaphoreType.DMA((4,))],
        compiler_params=pltpu.CompilerParams(vmem_limit_bytes=8 << 20),
    )(*kept, *sent)


def solution(mesh):
    return jax.shard_map(
        functools.partial(shards, mesh.shape["dom"], mesh.shape["grp"]),
        mesh=mesh,
        in_specs=(P(AXES, None), P(AXES), P(AXES, None), P(AXES), P(AXES, None, None, None)),
        out_specs=P(AXES, None),
        check_vma=False,
    )
```

```python
import functools

import jax
import jax.numpy as jnp
from jax import lax
from jax.experimental import pallas as pl
from jax.experimental.pallas import tpu as pltpu
from jax.sharding import PartitionSpec as P

AXES = ("dom", "grp")
MIX = 0.3
WIDTHS = (256, 256)
VMEM = pl.BlockSpec(memory_space=pltpu.VMEM)
SMEM = pl.BlockSpec(memory_space=pltpu.SMEM)
ANY = pl.BlockSpec(memory_space=pl.ANY)


def kernel_call(body, out_shape, in_specs, flops, moved, scratch=(), limit=10):
    outs = out_shape if isinstance(out_shape, (tuple, list)) else (out_shape,)
    specs = tuple(VMEM for _ in outs)
    return pl.pallas_call(
        body,
        out_shape=out_shape,
        in_specs=in_specs,
        out_specs=specs if isinstance(out_shape, (tuple, list)) else specs[0],
        scratch_shapes=scratch,
        compiler_params=pltpu.CompilerParams(vmem_limit_bytes=limit * 1024 * 1024),
        cost_estimate=pl.CostEstimate(flops=flops, bytes_accessed=moved, transcendentals=0),
    )


def half_of(core_is_odd, z):
    return jnp.where(core_is_odd, z // 2, ((z + 1) // 2) % 2)


def sort_kernel(doms, owner_hbm, enc_ref, other_0, other_1, pick_ref, place_ref, enc, owner_ref, sems):
    rows, width = enc_ref.shape
    half = width // 2
    z = lax.axis_index("grp")
    first = pltpu.make_async_copy(owner_hbm, owner_ref, sems.at[2])
    first.start()
    loads = []
    for core in range(2):
        start = pl.multiple_of((1 - half_of(core == 1, z)) * half, half)
        loads.append(pltpu.make_async_copy(enc_ref.at[:, pl.ds(start, half)], enc.at[core], sems.at[core]))
    for load in loads:
        load.start()
    per = rows // doms
    before = (
        lax.broadcasted_iota(jnp.int32, (rows, rows), 0)
        < lax.broadcasted_iota(jnp.int32, (rows, rows), 1)
    ).astype(jnp.bfloat16)
    first.wait()
    owner = owner_ref[...]
    group_nodes = rows * 4
    tdom = owner // group_nodes
    place = owner - tdom * group_nodes
    hot = (lax.broadcasted_iota(jnp.int32, (doms, rows), 0) == tdom).astype(jnp.float32)
    seen = jnp.dot(hot.astype(jnp.bfloat16), before, preferred_element_type=jnp.float32)
    rank = jnp.sum(hot * seen, axis=0, keepdims=True)
    block = (tdom % 2) * (doms // 2) + tdom // 2
    slot = block * per + rank.astype(jnp.int32)
    pick_ref[...] = (lax.broadcasted_iota(jnp.int32, (rows, rows), 0) == slot).astype(jnp.bfloat16)
    line = lax.broadcasted_iota(jnp.int32, (16, rows), 0)
    coded = jnp.where(line == 0, place // 64, jnp.where(line == 1, place % 64, 0))
    places = lax.dot_general(
        coded.astype(jnp.float32).astype(jnp.bfloat16),
        pick_ref[...],
        (((1,), (1,)), ((), ())),
        preferred_element_type=jnp.float32,
    ).astype(jnp.bfloat16)
    place_ref[...] = places
    part = rows // 2
    for core, out in enumerate((other_0, other_1)):
        out[part:, :part] = places[:, core * part : (core + 1) * part]
        out[part:, part:] = jnp.zeros((16, half - part), jnp.bfloat16)
        loads[core].wait()
        out[:part, :] = jnp.dot(
            pick_ref[pl.ds(core * part, part), :],
            enc[core].astype(jnp.bfloat16),
            preferred_element_type=jnp.float32,
        ).astype(jnp.bfloat16)


def by_dom(core, block, per):
    return pl.ds((2 * block + core) * per, per)


def pieces(own):
    at, start = [], 0
    for width in WIDTHS:
        at.append((2 * start + (0 if own else width), start, width))
        start += width
    return at


def mine_kernel(per, enc_ref, pick_ref, mine_ref, enc, sems):
    rows, width = enc_ref.shape
    half = width // 2
    z = lax.axis_index("grp")
    loads = []
    for core in range(2):
        start = pl.multiple_of(half_of(core == 1, z) * half, half)
        loads.append(pltpu.make_async_copy(enc_ref.at[:, pl.ds(start, half)], enc.at[core], sems.at[core]))
    for load in loads:
        load.start()
    for core in range(2):
        loads[core].wait()
        part = jnp.dot(
            pick_ref[pl.ds(core * rows // 2, rows // 2), :],
            enc[core].astype(jnp.bfloat16),
            preferred_element_type=jnp.float32,
        ).astype(jnp.bfloat16)
        for block in range(rows // 2 // per):
            mine_ref[by_dom(core, block, per), :] = part[block * per : (block + 1) * per, :]


def pack_kernel(per, place_ref, row_0, row_1, mine_ref, packed_ref):
    half = row_0.shape[1]
    size = row_0.shape[0] - 16
    line = lax.broadcasted_iota(jnp.int32, (16, 128), 0)
    lane = lax.broadcasted_iota(jnp.int32, (16, 128), 1)
    for to, start, wide in pieces(True):
        packed_ref[:, to : to + wide] = mine_ref[:, start : start + wide]
    for core, row in enumerate((row_0, row_1)):
        total = jnp.zeros((size, 128), jnp.float32)
        for n, lines in enumerate((place_ref[:, core * size : (core + 1) * size], row[size:, :size])):
            spread = ((lane == line + 2 * n) & (line < 2)).astype(jnp.bfloat16)
            total += lax.dot_general(
                lines, spread, (((0,), (0,)), ((), ())), preferred_element_type=jnp.float32
            )
        total = total.astype(jnp.bfloat16)
        for block in range(size // per):
            at = by_dom(core, block, per)
            span = slice(block * per, (block + 1) * per)
            for to, start, wide in pieces(False):
                packed_ref[at, to : to + wide] = row[span, start : start + wide]
            packed_ref[at, 2 * half :] = total[span, :]


def place_kernel(arrived_ref, token, *outs):
    rows = arrived_ref.shape[0]
    total = sum(out.shape[1] for out in outs)
    line = lax.broadcasted_iota(jnp.int32, (16, 128), 0)
    lane = lax.broadcasted_iota(jnp.int32, (16, 128), 1)
    spread = ((lane == line) & (line < 4)).astype(jnp.bfloat16)
    outs[0][rows:, :rows] = lax.dot_general(
        spread, arrived_ref[:, total:], (((1,), (1,)), ((), ())), preferred_element_type=jnp.float32
    ).astype(jnp.bfloat16)
    if outs[0].shape[1] > rows:
        outs[0][rows:, rows:] = jnp.zeros((16, outs[0].shape[1] - rows), jnp.bfloat16)
    start = 0
    for out in outs:
        out[:rows, :] = arrived_ref[:, start : start + out.shape[1]]
        start += out.shape[1]


def dense_kernel(list_ref, count_ref, weight_ref, dense_ref, scale_ref, token_ref, held, sems):
    blocks, _, size, _ = weight_ref.shape
    dom, z = lax.axis_index("dom"), lax.axis_index("grp")
    loads = [pltpu.make_async_copy(weight_ref.at[b], held.at[b], sems.at[b]) for b in range(blocks)]
    for load in loads:
        load.start()
    for b in range(blocks):
        dense_ref[pl.ds(b * size, size), :] = jnp.zeros((size, dense_ref.shape[1]), dense_ref.dtype)
    for b in range(blocks):
        span = pl.ds(b * size, size)
        loads[b].wait()

        def put(k, total):
            block = held[b, k]
            target = list_ref[b, k]
            column = steps_of(dom, z, target // blocks) * blocks + target % blocks
            start = pl.multiple_of(column * size, size)
            dense_ref[span, pl.ds(start, size)] = block
            return total + block.astype(jnp.float32)

        total = lax.fori_loop(0, count_ref[b], put, jnp.zeros((size, size), jnp.float32))
        degree = jnp.sum(total, axis=1, keepdims=True)
        scale_ref[span, :] = jnp.broadcast_to((1.0 - MIX) * lax.rsqrt(degree), (size, 128))
    token_ref[...] = jnp.zeros(token_ref.shape, token_ref.dtype)


def steps_of(dom, z, q):
    odd = dom % 2 == 1
    rx, fx = jnp.where(odd, 3, 1), jnp.where(odd, 1, 3)
    step = q ^ z
    return jnp.where(step == 0, 0, jnp.where(step == rx, 1, jnp.where(step == fx, 2, 3)))


def pick_kernel(rows_ref, token, pick_ref):
    nodes, size = pick_ref.shape[1:]
    dom, z = lax.axis_index("dom"), lax.axis_index("grp")
    coded = rows_ref[pl.ds(size, 16), :size].astype(jnp.float32).astype(jnp.int32)
    for k in range(2):
        p = coded[2 * k : 2 * k + 1, :] * 64 + coded[2 * k + 1 : 2 * k + 2, :]
        spot = steps_of(dom, z, p // size) * size + p % size
        for n in range(nodes // size):
            node = lax.broadcasted_iota(jnp.int32, (size, size), 0) + n * size
            pick_ref[k, pl.ds(n * size, size), :] = (node == spot).astype(jnp.bfloat16)


def part_kernel(pick_ref, near_ref, part_ref):
    size, width = pick_ref.shape[2], part_ref.shape[1]
    for n in range(part_ref.shape[0] // size):
        at = pl.ds(n * size, size)
        total = jnp.dot(pick_ref[0, at, :], near_ref[:size, :width], preferred_element_type=jnp.float32)
        total += jnp.dot(pick_ref[1, at, :], near_ref[:size, width:], preferred_element_type=jnp.float32)
        part_ref[at, :] = total.astype(jnp.bfloat16)


def first_kernel(dense_a, dense_b, scale_a, scale_b, pick_ref, part_ref, far_ref, base_ref, hidden_ref, panel):
    size = dense_a.shape[0]
    width = part_ref.shape[1]
    for n in range(panel.shape[0] // size):
        at = pl.ds(n * size, size)
        total = jnp.dot(pick_ref[0, at, :], far_ref[:size, :width], preferred_element_type=jnp.float32)
        total += jnp.dot(pick_ref[1, at, :], far_ref[:size, width:], preferred_element_type=jnp.float32)
        panel[at, :] = part_ref[at, :] + total.astype(jnp.bfloat16)
    for n, (dense, scale) in enumerate(((dense_a, scale_a), (dense_b, scale_b))):
        at = pl.ds(n * size, size)
        total = jnp.dot(dense[...], panel[...], preferred_element_type=jnp.float32)
        base = panel[at, :]
        base_ref[at, :] = base
        hidden_ref[at, :] = (MIX * base.astype(jnp.float32) + total * scale[:, 0:1]).astype(jnp.bfloat16)


def half_kernel(dense_a, dense_b, hidden_ref, total_ref):
    size = dense_a.shape[0]
    depth = hidden_ref.shape[0]
    for n, dense in enumerate((dense_a, dense_b)):
        total_ref[pl.ds(n * size, size), :] = jnp.dot(
            dense[:, :depth], hidden_ref[...], preferred_element_type=jnp.float32
        )


def last_kernel(start, dense_a, dense_b, scale_a, scale_b, total_ref, hidden_ref, base_ref, *refs):
    keep_ref, send_ref = refs[-2:]
    for done, out in zip(refs[:-2], (keep_ref, send_ref)):
        out[:, :start] = done[...]
    size = dense_a.shape[0]
    depth, width = hidden_ref.shape
    for n, (dense, scale, out) in enumerate(((dense_a, scale_a, keep_ref), (dense_b, scale_b, send_ref))):
        at = pl.ds(n * size, size)
        total = total_ref[at, :] + jnp.dot(dense[:, depth:], hidden_ref[...], preferred_element_type=jnp.float32)
        out[:, start : start + width] = (
            MIX * base_ref[at, :].astype(jnp.float32) + total * scale[:, 0:1]
        ).astype(jnp.bfloat16)


def join_kernel(keep_ref, got_ref, out_ref, sems):
    half = keep_ref.shape[1]
    dom, z = lax.axis_index("dom"), lax.axis_index("grp")
    upper = half_of(dom % 2 == 1, z)
    copies = []
    for n, (piece, side) in enumerate(((keep_ref, upper), (got_ref, 1 - upper))):
        to = out_ref.at[:, pl.ds(pl.multiple_of(side * half, half), half)]
        copies.append(pltpu.make_async_copy(piece, to, sems.at[n]))
    for copy in copies:
        copy.start()
    for copy in copies:
        copy.wait()


def row_step(core):
    return 1 if core == 0 else 3


def shards(doms, depth, encoded, owner_of, nbr_blocks, nbr_count, edge_weights):
    f32, bf16, i32 = jnp.float32, jnp.bfloat16, jnp.int32
    rows, width = encoded.shape
    half = width // 2
    blocks, slots, size, _ = edge_weights.shape
    nodes = rows * depth
    devices = [(d, q) for d in range(doms) for q in range(depth)]
    row_pairs = [(d * depth + q, d * depth + (q ^ row_step(d % 2))) for d, q in devices]
    col_pairs = [(d * depth + q, d * depth + (q ^ row_step(1 - d % 2))) for d, q in devices]

    def to_row(a):
        return lax.ppermute(a, AXES, row_pairs)

    def to_col(a):
        return lax.ppermute(a, AXES, col_pairs)

    def to_row_of(core, a):
        return lax.ppermute(a, AXES, [(d * depth + q, d * depth + (q ^ row_step(core))) for d, q in devices])

    far_blocks, far_count = to_row(nbr_blocks), to_row(nbr_count)

    def dense_of(lists, count, weights, limit):
        return kernel_call(
            dense_kernel,
            (
                jax.ShapeDtypeStruct((blocks * size, nodes), bf16),
                jax.ShapeDtypeStruct((blocks * size, 128), f32),
                jax.ShapeDtypeStruct((8, 128), f32),
            ),
            [SMEM, SMEM, ANY],
            0,
            8 << 20,
            scratch=[pltpu.VMEM(weights.shape, bf16), pltpu.SemaphoreType.DMA((blocks,))],
            limit=limit,
        )(lists, count, weights)

    held = pltpu.VMEM((2, rows, half), f32)
    other = jax.ShapeDtypeStruct((rows // 2 + 16, half), bf16)
    other_0, other_1, pick, place = kernel_call(
        functools.partial(sort_kernel, doms),
        (other, other, jax.ShapeDtypeStruct((rows, rows), bf16), jax.ShapeDtypeStruct((16, rows), bf16)),
        [ANY, ANY],
        2 * rows * rows * half,
        4 << 20,
        scratch=[held, pltpu.VMEM((1, rows), i32), pltpu.SemaphoreType.DMA((3,))],
        limit=58,
    )(owner_of.reshape(1, rows), encoded)
    row_0, row_1 = to_row_of(0, other_0), to_row_of(1, other_1)
    per = rows // doms
    mine = kernel_call(
        functools.partial(mine_kernel, per),
        jax.ShapeDtypeStruct((rows, half), bf16),
        [ANY, VMEM],
        2 * rows * rows * half,
        4 << 20,
        scratch=[held, pltpu.SemaphoreType.DMA((2,))],
        limit=50,
    )(encoded, pick)
    sent_weights, mine, row_0, row_1, far_blocks, far_count = lax.optimization_barrier(
        (edge_weights, mine, row_0, row_1, far_blocks, far_count)
    )
    far_weights = to_row(sent_weights)
    packed = kernel_call(
        functools.partial(pack_kernel, per),
        jax.ShapeDtypeStruct((rows, width + 128), bf16),
        [VMEM] * 4,
        1 << 20,
        2 << 20,
    )(place, row_0, row_1, mine)

    packed = lax.all_to_all(packed, "dom", 0, 0, tiled=True)
    dense_a, scale_a, token_a = dense_of(nbr_blocks, nbr_count, edge_weights, 50)
    near_rows = kernel_call(
        place_kernel,
        tuple(jax.ShapeDtypeStruct((rows + (16 if c == 0 else 0), 2 * w), bf16) for c, w in enumerate(WIDTHS)),
        [VMEM, ANY],
        1 << 20,
        1 << 20,
    )(packed, token_a)
    far_rows = [to_col(a) for a in near_rows]

    dense_b, scale_b, token_b = dense_of(far_blocks, far_count, far_weights, 10)

    def picks_of(first_rows, token):
        return kernel_call(
            pick_kernel,
            jax.ShapeDtypeStruct((2, nodes, rows), bf16),
            [VMEM, ANY],
            1 << 20,
            4 << 20,
        )(first_rows, token)

    near_picks, far_picks = picks_of(near_rows[0], token_a), picks_of(far_rows[0], token_b)

    mine_n = 2 * rows
    result = ()
    for c, part in enumerate(WIDTHS):
        placed = kernel_call(
            part_kernel,
            jax.ShapeDtypeStruct((nodes, part), bf16),
            [VMEM] * 2,
            4 * nodes * rows * part,
            4 << 20,
        )(near_picks, near_rows[c])
        base, hidden = kernel_call(
            first_kernel,
            (jax.ShapeDtypeStruct((mine_n, part), bf16), jax.ShapeDtypeStruct((mine_n, part), bf16)),
            [VMEM] * 7,
            4 * nodes * rows * part + 2 * mine_n * nodes * part,
            4 << 20,
            scratch=[pltpu.VMEM((nodes, part), bf16)],
        )(dense_a, dense_b, scale_a, scale_b, far_picks, placed, far_rows[c])
        far_hidden = to_col(hidden)
        running = kernel_call(
            half_kernel,
            jax.ShapeDtypeStruct((mine_n, part), f32),
            [VMEM] * 3,
            2 * mine_n * mine_n * part,
            4 << 20,
        )(dense_a, dense_b, hidden)
        result = kernel_call(
            functools.partial(last_kernel, sum(WIDTHS[:c])),
            (jax.ShapeDtypeStruct((rows, sum(WIDTHS[: c + 1])), bf16),) * 2,
            [VMEM] * (7 + len(result)),
            2 * mine_n * mine_n * part,
            4 << 20,
        )(dense_a, dense_b, scale_a, scale_b, running, far_hidden, base, *result)
    keep, send = result
    return pl.pallas_call(
        join_kernel,
        out_shape=jax.ShapeDtypeStruct((rows, width), bf16),
        in_specs=[VMEM] * 2,
        out_specs=ANY,
        scratch_shapes=[pltpu.SemaphoreType.DMA((2,))],
        compiler_params=pltpu.CompilerParams(vmem_limit_bytes=8 << 20),
    )(keep, to_row(send))


def solution(mesh):
    return jax.shard_map(
        functools.partial(shards, mesh.shape["dom"], mesh.shape["grp"]),
        mesh=mesh,
        in_specs=(P(AXES, None), P(AXES), P(AXES, None), P(AXES), P(AXES, None, None, None)),
        out_specs=P(AXES, None),
        check_vma=False,
    )
```

```python
import functools

import jax
import jax.numpy as jnp
from jax import lax
from jax.experimental import pallas as pl
from jax.experimental.pallas import tpu as pltpu
from jax.sharding import PartitionSpec as P

AXES = ("dom", "grp")
MIX = 0.3
WIDTHS = (256, 256)
VMEM = pl.BlockSpec(memory_space=pltpu.VMEM)
SMEM = pl.BlockSpec(memory_space=pltpu.SMEM)
ANY = pl.BlockSpec(memory_space=pl.ANY)


def kernel_call(body, out_shape, in_specs, flops, moved, scratch=(), limit=10):
    outs = out_shape if isinstance(out_shape, (tuple, list)) else (out_shape,)
    specs = tuple(VMEM for _ in outs)
    return pl.pallas_call(
        body,
        out_shape=out_shape,
        in_specs=in_specs,
        out_specs=specs if isinstance(out_shape, (tuple, list)) else specs[0],
        scratch_shapes=scratch,
        compiler_params=pltpu.CompilerParams(vmem_limit_bytes=limit * 1024 * 1024),
        cost_estimate=pl.CostEstimate(flops=flops, bytes_accessed=moved, transcendentals=0),
    )


def half_of(core_is_odd, z):
    return jnp.where(core_is_odd, z // 2, ((z + 1) // 2) % 2)


def sort_kernel(doms, owner_hbm, enc_ref, other_0, other_1, pick_ref, place_ref, enc, owner_ref, sems):
    rows, width = enc_ref.shape
    half = width // 2
    z = lax.axis_index("grp")
    first = pltpu.make_async_copy(owner_hbm, owner_ref, sems.at[2])
    first.start()
    loads = []
    for core in range(2):
        start = pl.multiple_of((1 - half_of(core == 1, z)) * half, half)
        loads.append(pltpu.make_async_copy(enc_ref.at[:, pl.ds(start, half)], enc.at[core], sems.at[core]))
    for load in loads:
        load.start()
    per = rows // doms
    before = (
        lax.broadcasted_iota(jnp.int32, (rows, rows), 0)
        < lax.broadcasted_iota(jnp.int32, (rows, rows), 1)
    ).astype(jnp.bfloat16)
    first.wait()
    owner = owner_ref[...]
    group_nodes = rows * 4
    tdom = owner // group_nodes
    place = owner - tdom * group_nodes
    hot = (lax.broadcasted_iota(jnp.int32, (doms, rows), 0) == tdom).astype(jnp.float32)
    seen = jnp.dot(hot.astype(jnp.bfloat16), before, preferred_element_type=jnp.float32)
    rank = jnp.sum(hot * seen, axis=0, keepdims=True)
    block = (tdom % 2) * (doms // 2) + tdom // 2
    slot = block * per + rank.astype(jnp.int32)
    pick_ref[...] = (lax.broadcasted_iota(jnp.int32, (rows, rows), 0) == slot).astype(jnp.bfloat16)
    line = lax.broadcasted_iota(jnp.int32, (16, rows), 0)
    coded = jnp.where(line == 0, place // 64, jnp.where(line == 1, place % 64, 0))
    places = lax.dot_general(
        coded.astype(jnp.float32).astype(jnp.bfloat16),
        pick_ref[...],
        (((1,), (1,)), ((), ())),
        preferred_element_type=jnp.float32,
    ).astype(jnp.bfloat16)
    place_ref[...] = places
    part = rows // 2
    for core, out in enumerate((other_0, other_1)):
        out[part:, :part] = places[:, core * part : (core + 1) * part]
        out[part:, part:] = jnp.zeros((16, half - part), jnp.bfloat16)
        loads[core].wait()
        out[:part, :] = jnp.dot(
            pick_ref[pl.ds(core * part, part), :],
            enc[core].astype(jnp.bfloat16),
            preferred_element_type=jnp.float32,
        ).astype(jnp.bfloat16)


def by_dom(core, block, per):
    return pl.ds((2 * block + core) * per, per)


def pieces(own):
    at, start = [], 0
    for width in WIDTHS:
        at.append((2 * start + (0 if own else width), start, width))
        start += width
    return at


def mine_kernel(per, enc_ref, pick_ref, mine_ref, enc, sems):
    rows, width = enc_ref.shape
    half = width // 2
    z = lax.axis_index("grp")
    loads = []
    for core in range(2):
        start = pl.multiple_of(half_of(core == 1, z) * half, half)
        loads.append(pltpu.make_async_copy(enc_ref.at[:, pl.ds(start, half)], enc.at[core], sems.at[core]))
    for load in loads:
        load.start()
    for core in range(2):
        loads[core].wait()
        part = jnp.dot(
            pick_ref[pl.ds(core * rows // 2, rows // 2), :],
            enc[core].astype(jnp.bfloat16),
            preferred_element_type=jnp.float32,
        ).astype(jnp.bfloat16)
        for block in range(rows // 2 // per):
            mine_ref[by_dom(core, block, per), :] = part[block * per : (block + 1) * per, :]


def pack_kernel(per, place_ref, row_0, row_1, mine_ref, packed_ref):
    half = row_0.shape[1]
    size = row_0.shape[0] - 16
    line = lax.broadcasted_iota(jnp.int32, (16, 128), 0)
    lane = lax.broadcasted_iota(jnp.int32, (16, 128), 1)
    for to, start, wide in pieces(True):
        packed_ref[:, to : to + wide] = mine_ref[:, start : start + wide]
    for core, row in enumerate((row_0, row_1)):
        total = jnp.zeros((size, 128), jnp.float32)
        for n, lines in enumerate((place_ref[:, core * size : (core + 1) * size], row[size:, :size])):
            spread = ((lane == line + 2 * n) & (line < 2)).astype(jnp.bfloat16)
            total += lax.dot_general(
                lines, spread, (((0,), (0,)), ((), ())), preferred_element_type=jnp.float32
            )
        total = total.astype(jnp.bfloat16)
        for block in range(size // per):
            at = by_dom(core, block, per)
            span = slice(block * per, (block + 1) * per)
            for to, start, wide in pieces(False):
                packed_ref[at, to : to + wide] = row[span, start : start + wide]
            packed_ref[at, 2 * half :] = total[span, :]


def place_kernel(arrived_ref, token, *outs):
    rows = arrived_ref.shape[0]
    total = sum(out.shape[1] for out in outs)
    line = lax.broadcasted_iota(jnp.int32, (16, 128), 0)
    lane = lax.broadcasted_iota(jnp.int32, (16, 128), 1)
    spread = ((lane == line) & (line < 4)).astype(jnp.bfloat16)
    outs[0][rows:, :rows] = lax.dot_general(
        spread, arrived_ref[:, total:], (((1,), (1,)), ((), ())), preferred_element_type=jnp.float32
    ).astype(jnp.bfloat16)
    if outs[0].shape[1] > rows:
        outs[0][rows:, rows:] = jnp.zeros((16, outs[0].shape[1] - rows), jnp.bfloat16)
    start = 0
    for out in outs:
        out[:rows, :] = arrived_ref[:, start : start + out.shape[1]]
        start += out.shape[1]


def dense_kernel(list_ref, count_ref, weight_ref, dense_ref, scale_ref, token_ref, held, sems):
    blocks, _, size, _ = weight_ref.shape
    dom, z = lax.axis_index("dom"), lax.axis_index("grp")
    loads = [pltpu.make_async_copy(weight_ref.at[b], held.at[b], sems.at[b]) for b in range(blocks)]
    for load in loads:
        load.start()
    for b in range(blocks):
        dense_ref[pl.ds(b * size, size), :] = jnp.zeros((size, dense_ref.shape[1]), dense_ref.dtype)
    for b in range(blocks):
        span = pl.ds(b * size, size)
        loads[b].wait()

        def put(k, total):
            block = held[b, k]
            target = list_ref[b, k]
            column = steps_of(dom, z, target // blocks) * blocks + target % blocks
            start = pl.multiple_of(column * size, size)
            dense_ref[span, pl.ds(start, size)] = block
            return total + block.astype(jnp.float32)

        total = lax.fori_loop(0, count_ref[b], put, jnp.zeros((size, size), jnp.float32))
        degree = jnp.sum(total, axis=1, keepdims=True)
        scale_ref[span, :] = jnp.broadcast_to((1.0 - MIX) * lax.rsqrt(degree), (size, 128))
    token_ref[...] = jnp.zeros(token_ref.shape, token_ref.dtype)


def steps_of(dom, z, q):
    odd = dom % 2 == 1
    rx, fx = jnp.where(odd, 3, 1), jnp.where(odd, 1, 3)
    step = q ^ z
    return jnp.where(step == 0, 0, jnp.where(step == rx, 1, jnp.where(step == fx, 2, 3)))


def pick_kernel(rows_ref, token, pick_ref):
    nodes, size = pick_ref.shape[1:]
    dom, z = lax.axis_index("dom"), lax.axis_index("grp")
    coded = rows_ref[pl.ds(size, 16), :size].astype(jnp.float32).astype(jnp.int32)
    for k in range(2):
        p = coded[2 * k : 2 * k + 1, :] * 64 + coded[2 * k + 1 : 2 * k + 2, :]
        spot = steps_of(dom, z, p // size) * size + p % size
        for n in range(nodes // size):
            node = lax.broadcasted_iota(jnp.int32, (size, size), 0) + n * size
            pick_ref[k, pl.ds(n * size, size), :] = (node == spot).astype(jnp.bfloat16)


def part_kernel(pick_ref, near_ref, part_ref):
    size, width = pick_ref.shape[2], part_ref.shape[1]
    for n in range(part_ref.shape[0] // size):
        at = pl.ds(n * size, size)
        total = jnp.dot(pick_ref[0, at, :], near_ref[:size, :width], preferred_element_type=jnp.float32)
        total += jnp.dot(pick_ref[1, at, :], near_ref[:size, width:], preferred_element_type=jnp.float32)
        part_ref[at, :] = total.astype(jnp.bfloat16)


def first_kernel(dense_a, dense_b, scale_a, scale_b, pick_ref, part_ref, far_ref, base_ref, hidden_ref, panel):
    size = dense_a.shape[0]
    width = part_ref.shape[1]
    for n in range(panel.shape[0] // size):
        at = pl.ds(n * size, size)
        total = jnp.dot(pick_ref[0, at, :], far_ref[:size, :width], preferred_element_type=jnp.float32)
        total += jnp.dot(pick_ref[1, at, :], far_ref[:size, width:], preferred_element_type=jnp.float32)
        panel[at, :] = part_ref[at, :] + total.astype(jnp.bfloat16)
    for n, (dense, scale) in enumerate(((dense_a, scale_a), (dense_b, scale_b))):
        at = pl.ds(n * size, size)
        total = jnp.dot(dense[...], panel[...], preferred_element_type=jnp.float32)
        base = panel[at, :]
        base_ref[at, :] = base
        hidden_ref[at, :] = (MIX * base.astype(jnp.float32) + total * scale[:, 0:1]).astype(jnp.bfloat16)


def half_kernel(dense_a, dense_b, hidden_ref, total_ref):
    size = dense_a.shape[0]
    depth = hidden_ref.shape[0]
    for n, dense in enumerate((dense_a, dense_b)):
        total_ref[pl.ds(n * size, size), :] = jnp.dot(
            dense[:, :depth], hidden_ref[...], preferred_element_type=jnp.float32
        )


def last_kernel(dense_a, dense_b, scale_a, scale_b, total_ref, hidden_ref, base_ref, keep_ref, send_ref):
    size = dense_a.shape[0]
    depth = hidden_ref.shape[0]
    for n, (dense, scale, out) in enumerate(((dense_a, scale_a, keep_ref), (dense_b, scale_b, send_ref))):
        at = pl.ds(n * size, size)
        total = total_ref[at, :] + jnp.dot(dense[:, depth:], hidden_ref[...], preferred_element_type=jnp.float32)
        out[...] = (MIX * base_ref[at, :].astype(jnp.float32) + total * scale[:, 0:1]).astype(jnp.bfloat16)


def move_halves(pieces, side, out_ref, sems):
    part = pieces[0].shape[1]
    copies = []
    for n, piece in enumerate(pieces):
        start = pl.multiple_of((side * len(pieces) + n) * part, part)
        copies.append(pltpu.make_async_copy(piece, out_ref.at[:, pl.ds(start, part)], sems.at[n]))
    for copy in copies:
        copy.start()
    for copy in copies:
        copy.wait()


def keep_kernel(keep_0, keep_1, out_ref, sems):
    dom, z = lax.axis_index("dom"), lax.axis_index("grp")
    move_halves((keep_0, keep_1), half_of(dom % 2 == 1, z), out_ref, sems)


def join_kernel(early_0, late_0, got_1, _, out_ref, sems):
    dom, z = lax.axis_index("dom"), lax.axis_index("grp")
    side = 1 - half_of(dom % 2 == 1, z)

    @pl.when(dom % 2 == 0)
    def _():
        move_halves((early_0, got_1), side, out_ref, sems)

    @pl.when(dom % 2 == 1)
    def _():
        move_halves((late_0, got_1), side, out_ref, sems)


def row_step(core):
    return 1 if core == 0 else 3


def shards(doms, depth, encoded, owner_of, nbr_blocks, nbr_count, edge_weights):
    f32, bf16, i32 = jnp.float32, jnp.bfloat16, jnp.int32
    rows, width = encoded.shape
    half = width // 2
    blocks, slots, size, _ = edge_weights.shape
    nodes = rows * depth
    devices = [(d, q) for d in range(doms) for q in range(depth)]
    row_pairs = [(d * depth + q, d * depth + (q ^ row_step(d % 2))) for d, q in devices]
    col_pairs = [(d * depth + q, d * depth + (q ^ row_step(1 - d % 2))) for d, q in devices]

    def to_row(a):
        return lax.ppermute(a, AXES, row_pairs)

    def to_col(a):
        return lax.ppermute(a, AXES, col_pairs)

    def to_row_of(core, a):
        return lax.ppermute(a, AXES, [(d * depth + q, d * depth + (q ^ row_step(core))) for d, q in devices])

    far_blocks, far_count = to_row(nbr_blocks), to_row(nbr_count)

    def dense_of(lists, count, weights, limit):
        return kernel_call(
            dense_kernel,
            (
                jax.ShapeDtypeStruct((blocks * size, nodes), bf16),
                jax.ShapeDtypeStruct((blocks * size, 128), f32),
                jax.ShapeDtypeStruct((8, 128), f32),
            ),
            [SMEM, SMEM, ANY],
            0,
            8 << 20,
            scratch=[pltpu.VMEM(weights.shape, bf16), pltpu.SemaphoreType.DMA((blocks,))],
            limit=limit,
        )(lists, count, weights)

    held = pltpu.VMEM((2, rows, half), f32)
    other = jax.ShapeDtypeStruct((rows // 2 + 16, half), bf16)
    other_0, other_1, pick, place = kernel_call(
        functools.partial(sort_kernel, doms),
        (other, other, jax.ShapeDtypeStruct((rows, rows), bf16), jax.ShapeDtypeStruct((16, rows), bf16)),
        [ANY, ANY],
        2 * rows * rows * half,
        4 << 20,
        scratch=[held, pltpu.VMEM((1, rows), i32), pltpu.SemaphoreType.DMA((3,))],
        limit=58,
    )(owner_of.reshape(1, rows), encoded)
    row_0, row_1 = to_row_of(0, other_0), to_row_of(1, other_1)
    per = rows // doms
    mine = kernel_call(
        functools.partial(mine_kernel, per),
        jax.ShapeDtypeStruct((rows, half), bf16),
        [ANY, VMEM],
        2 * rows * rows * half,
        4 << 20,
        scratch=[held, pltpu.SemaphoreType.DMA((2,))],
        limit=50,
    )(encoded, pick)
    sent_weights, mine, row_0, row_1, far_blocks, far_count = lax.optimization_barrier(
        (edge_weights, mine, row_0, row_1, far_blocks, far_count)
    )
    far_weights = to_row(sent_weights)
    packed = kernel_call(
        functools.partial(pack_kernel, per),
        jax.ShapeDtypeStruct((rows, width + 128), bf16),
        [VMEM] * 4,
        1 << 20,
        2 << 20,
    )(place, row_0, row_1, mine)

    packed = lax.all_to_all(packed, "dom", 0, 0, tiled=True)
    dense_a, scale_a, token_a = dense_of(nbr_blocks, nbr_count, edge_weights, 50)
    near_rows = kernel_call(
        place_kernel,
        tuple(jax.ShapeDtypeStruct((rows + (16 if c == 0 else 0), 2 * w), bf16) for c, w in enumerate(WIDTHS)),
        [VMEM, ANY],
        1 << 20,
        1 << 20,
    )(packed, token_a)
    far_rows = [to_col(a) for a in near_rows]

    dense_b, scale_b, token_b = dense_of(far_blocks, far_count, far_weights, 10)

    def picks_of(first_rows, token):
        return kernel_call(
            pick_kernel,
            jax.ShapeDtypeStruct((2, nodes, rows), bf16),
            [VMEM, ANY],
            1 << 20,
            4 << 20,
        )(first_rows, token)

    near_picks, far_picks = picks_of(near_rows[0], token_a), picks_of(far_rows[0], token_b)

    mine_n = 2 * rows
    kept, sent = [], []
    for c, part in enumerate(WIDTHS):
        placed = kernel_call(
            part_kernel,
            jax.ShapeDtypeStruct((nodes, part), bf16),
            [VMEM] * 2,
            4 * nodes * rows * part,
            4 << 20,
        )(near_picks, near_rows[c])
        base, hidden = kernel_call(
            first_kernel,
            (jax.ShapeDtypeStruct((mine_n, part), bf16), jax.ShapeDtypeStruct((mine_n, part), bf16)),
            [VMEM] * 7,
            4 * nodes * rows * part + 2 * mine_n * nodes * part,
            4 << 20,
            scratch=[pltpu.VMEM((nodes, part), bf16)],
        )(dense_a, dense_b, scale_a, scale_b, far_picks, placed, far_rows[c])
        far_hidden = to_col(hidden)
        running = kernel_call(
            half_kernel,
            jax.ShapeDtypeStruct((mine_n, part), f32),
            [VMEM] * 3,
            2 * mine_n * mine_n * part,
            4 << 20,
        )(dense_a, dense_b, hidden)
        keep, send = kernel_call(
            last_kernel,
            (jax.ShapeDtypeStruct((rows, part), bf16),) * 2,
            [VMEM] * 7,
            2 * mine_n * mine_n * part,
            4 << 20,
        )(dense_a, dense_b, scale_a, scale_b, running, far_hidden, base)
        kept.append(keep)
        sent.append(send)

    def to_row_on(core, a):
        return lax.ppermute(a, AXES, [(p, q) for p, q in row_pairs if p // depth % 2 == core])

    early_0 = to_row_on(0, sent[0])
    got_1 = to_row(sent[1])
    held_back, _ = lax.optimization_barrier((sent[0], sent[1]))
    late_0 = to_row_on(1, held_back)
    whole = jax.ShapeDtypeStruct((rows, width), bf16)
    half_done = pl.pallas_call(
        keep_kernel,
        out_shape=whole,
        in_specs=[VMEM] * 2,
        out_specs=ANY,
        scratch_shapes=[pltpu.SemaphoreType.DMA((2,))],
        compiler_params=pltpu.CompilerParams(vmem_limit_bytes=8 << 20),
    )(*kept)
    return pl.pallas_call(
        join_kernel,
        out_shape=whole,
        in_specs=[VMEM] * 3 + [ANY],
        out_specs=ANY,
        input_output_aliases={3: 0},
        scratch_shapes=[pltpu.SemaphoreType.DMA((2,))],
        compiler_params=pltpu.CompilerParams(vmem_limit_bytes=8 << 20),
    )(early_0, late_0, got_1, half_done)


def solution(mesh):
    return jax.shard_map(
        functools.partial(shards, mesh.shape["dom"], mesh.shape["grp"]),
        mesh=mesh,
        in_specs=(P(AXES, None), P(AXES), P(AXES, None), P(AXES), P(AXES, None, None, None)),
        out_specs=P(AXES, None),
        check_vma=False,
    )
```

```python
import functools

import jax
import jax.numpy as jnp
from jax import lax
from jax.experimental import pallas as pl
from jax.experimental.pallas import tpu as pltpu
from jax.sharding import PartitionSpec as P

AXES = ("dom", "grp")
MIX = 0.3
WIDTHS = (256, 256)
VMEM = pl.BlockSpec(memory_space=pltpu.VMEM)
SMEM = pl.BlockSpec(memory_space=pltpu.SMEM)
ANY = pl.BlockSpec(memory_space=pl.ANY)


def kernel_call(body, out_shape, in_specs, flops, moved, scratch=(), limit=10):
    outs = out_shape if isinstance(out_shape, (tuple, list)) else (out_shape,)
    specs = tuple(VMEM for _ in outs)
    return pl.pallas_call(
        body,
        out_shape=out_shape,
        in_specs=in_specs,
        out_specs=specs if isinstance(out_shape, (tuple, list)) else specs[0],
        scratch_shapes=scratch,
        compiler_params=pltpu.CompilerParams(vmem_limit_bytes=limit * 1024 * 1024),
        cost_estimate=pl.CostEstimate(flops=flops, bytes_accessed=moved, transcendentals=0),
    )


def half_of(core_is_odd, z):
    return jnp.where(core_is_odd, z // 2, ((z + 1) // 2) % 2)


def sort_kernel(doms, owner_hbm, enc_ref, other_0, other_1, pick_ref, place_ref, enc, owner_ref, sems):
    rows, width = enc_ref.shape
    half = width // 2
    z = lax.axis_index("grp")
    first = pltpu.make_async_copy(owner_hbm, owner_ref, sems.at[2])
    first.start()
    loads = []
    for core in range(2):
        start = pl.multiple_of((1 - half_of(core == 1, z)) * half, half)
        loads.append(pltpu.make_async_copy(enc_ref.at[:, pl.ds(start, half)], enc.at[core], sems.at[core]))
    for load in loads:
        load.start()
    per = rows // doms
    before = (
        lax.broadcasted_iota(jnp.int32, (rows, rows), 0)
        < lax.broadcasted_iota(jnp.int32, (rows, rows), 1)
    ).astype(jnp.bfloat16)
    first.wait()
    owner = owner_ref[...]
    group_nodes = rows * 4
    tdom = owner // group_nodes
    place = owner - tdom * group_nodes
    hot = (lax.broadcasted_iota(jnp.int32, (doms, rows), 0) == tdom).astype(jnp.float32)
    seen = jnp.dot(hot.astype(jnp.bfloat16), before, preferred_element_type=jnp.float32)
    rank = jnp.sum(hot * seen, axis=0, keepdims=True)
    block = (tdom % 2) * (doms // 2) + tdom // 2
    slot = block * per + rank.astype(jnp.int32)
    pick_ref[...] = (lax.broadcasted_iota(jnp.int32, (rows, rows), 0) == slot).astype(jnp.bfloat16)
    line = lax.broadcasted_iota(jnp.int32, (16, rows), 0)
    coded = jnp.where(line == 0, place // 64, jnp.where(line == 1, place % 64, 0))
    places = lax.dot_general(
        coded.astype(jnp.float32).astype(jnp.bfloat16),
        pick_ref[...],
        (((1,), (1,)), ((), ())),
        preferred_element_type=jnp.float32,
    ).astype(jnp.bfloat16)
    place_ref[...] = places
    part = rows // 2
    for core, out in enumerate((other_0, other_1)):
        out[part:, :part] = places[:, core * part : (core + 1) * part]
        out[part:, part:] = jnp.zeros((16, half - part), jnp.bfloat16)
        loads[core].wait()
        out[:part, :] = jnp.dot(
            pick_ref[pl.ds(core * part, part), :],
            enc[core].astype(jnp.bfloat16),
            preferred_element_type=jnp.float32,
        ).astype(jnp.bfloat16)


def by_dom(core, block, per):
    return pl.ds((2 * block + core) * per, per)


def pieces(own):
    at, start = [], 0
    for width in WIDTHS:
        at.append((2 * start + (0 if own else width), start, width))
        start += width
    return at


def mine_kernel(per, enc_ref, pick_ref, mine_ref, enc, sems):
    rows, width = enc_ref.shape
    half = width // 2
    z = lax.axis_index("grp")
    loads = []
    for core in range(2):
        start = pl.multiple_of(half_of(core == 1, z) * half, half)
        loads.append(pltpu.make_async_copy(enc_ref.at[:, pl.ds(start, half)], enc.at[core], sems.at[core]))
    for load in loads:
        load.start()
    for core in range(2):
        loads[core].wait()
        part = jnp.dot(
            pick_ref[pl.ds(core * rows // 2, rows // 2), :],
            enc[core].astype(jnp.bfloat16),
            preferred_element_type=jnp.float32,
        ).astype(jnp.bfloat16)
        for block in range(rows // 2 // per):
            mine_ref[by_dom(core, block, per), :] = part[block * per : (block + 1) * per, :]


def pack_kernel(per, place_ref, row_0, row_1, mine_ref, packed_ref):
    half = row_0.shape[1]
    size = row_0.shape[0] - 16
    line = lax.broadcasted_iota(jnp.int32, (16, 128), 0)
    lane = lax.broadcasted_iota(jnp.int32, (16, 128), 1)
    for to, start, wide in pieces(True):
        packed_ref[:, to : to + wide] = mine_ref[:, start : start + wide]
    for core, row in enumerate((row_0, row_1)):
        total = jnp.zeros((size, 128), jnp.float32)
        for n, lines in enumerate((place_ref[:, core * size : (core + 1) * size], row[size:, :size])):
            spread = ((lane == line + 2 * n) & (line < 2)).astype(jnp.bfloat16)
            total += lax.dot_general(
                lines, spread, (((0,), (0,)), ((), ())), preferred_element_type=jnp.float32
            )
        total = total.astype(jnp.bfloat16)
        for block in range(size // per):
            at = by_dom(core, block, per)
            span = slice(block * per, (block + 1) * per)
            for to, start, wide in pieces(False):
                packed_ref[at, to : to + wide] = row[span, start : start + wide]
            packed_ref[at, 2 * half :] = total[span, :]


def place_kernel(arrived_ref, token, *outs):
    rows = arrived_ref.shape[0]
    total = sum(out.shape[1] for out in outs)
    line = lax.broadcasted_iota(jnp.int32, (16, 128), 0)
    lane = lax.broadcasted_iota(jnp.int32, (16, 128), 1)
    spread = ((lane == line) & (line < 4)).astype(jnp.bfloat16)
    outs[0][rows:, :rows] = lax.dot_general(
        spread, arrived_ref[:, total:], (((1,), (1,)), ((), ())), preferred_element_type=jnp.float32
    ).astype(jnp.bfloat16)
    if outs[0].shape[1] > rows:
        outs[0][rows:, rows:] = jnp.zeros((16, outs[0].shape[1] - rows), jnp.bfloat16)
    start = 0
    for out in outs:
        out[:rows, :] = arrived_ref[:, start : start + out.shape[1]]
        start += out.shape[1]


def dense_kernel(list_ref, count_ref, weight_ref, dense_ref, scale_ref, token_ref, held, sems):
    blocks, _, size, _ = weight_ref.shape
    dom, z = lax.axis_index("dom"), lax.axis_index("grp")
    loads = [pltpu.make_async_copy(weight_ref.at[b], held.at[b], sems.at[b]) for b in range(blocks)]
    for load in loads:
        load.start()
    for b in range(blocks):
        dense_ref[pl.ds(b * size, size), :] = jnp.zeros((size, dense_ref.shape[1]), dense_ref.dtype)
    for b in range(blocks):
        span = pl.ds(b * size, size)
        loads[b].wait()

        def put(k, total):
            block = held[b, k]
            target = list_ref[b, k]
            column = steps_of(dom, z, target // blocks) * blocks + target % blocks
            start = pl.multiple_of(column * size, size)
            dense_ref[span, pl.ds(start, size)] = block
            return total + block.astype(jnp.float32)

        total = lax.fori_loop(0, count_ref[b], put, jnp.zeros((size, size), jnp.float32))
        degree = jnp.sum(total, axis=1, keepdims=True)
        scale_ref[span, :] = jnp.broadcast_to((1.0 - MIX) * lax.rsqrt(degree), (size, 128))
    token_ref[...] = jnp.zeros(token_ref.shape, token_ref.dtype)


def steps_of(dom, z, q):
    odd = dom % 2 == 1
    rx, fx = jnp.where(odd, 3, 1), jnp.where(odd, 1, 3)
    step = q ^ z
    return jnp.where(step == 0, 0, jnp.where(step == rx, 1, jnp.where(step == fx, 2, 3)))


def pick_kernel(rows_ref, token, pick_ref):
    nodes, size = pick_ref.shape[1:]
    dom, z = lax.axis_index("dom"), lax.axis_index("grp")
    coded = rows_ref[pl.ds(size, 16), :size].astype(jnp.float32).astype(jnp.int32)
    for k in range(2):
        p = coded[2 * k : 2 * k + 1, :] * 64 + coded[2 * k + 1 : 2 * k + 2, :]
        spot = steps_of(dom, z, p // size) * size + p % size
        for n in range(nodes // size):
            node = lax.broadcasted_iota(jnp.int32, (size, size), 0) + n * size
            pick_ref[k, pl.ds(n * size, size), :] = (node == spot).astype(jnp.bfloat16)


def part_kernel(pick_ref, near_ref, part_ref):
    size, width = pick_ref.shape[2], part_ref.shape[1]
    for n in range(part_ref.shape[0] // size):
        at = pl.ds(n * size, size)
        total = jnp.dot(pick_ref[0, at, :], near_ref[:size, :width], preferred_element_type=jnp.float32)
        total += jnp.dot(pick_ref[1, at, :], near_ref[:size, width:], preferred_element_type=jnp.float32)
        part_ref[at, :] = total.astype(jnp.bfloat16)


def first_kernel(dense_a, dense_b, scale_a, scale_b, pick_ref, part_ref, far_ref, base_ref, hidden_ref, panel):
    size = dense_a.shape[0]
    width = part_ref.shape[1]
    for n in range(panel.shape[0] // size):
        at = pl.ds(n * size, size)
        total = jnp.dot(pick_ref[0, at, :], far_ref[:size, :width], preferred_element_type=jnp.float32)
        total += jnp.dot(pick_ref[1, at, :], far_ref[:size, width:], preferred_element_type=jnp.float32)
        panel[at, :] = part_ref[at, :] + total.astype(jnp.bfloat16)
    for n, (dense, scale) in enumerate(((dense_a, scale_a), (dense_b, scale_b))):
        at = pl.ds(n * size, size)
        total = jnp.dot(dense[...], panel[...], preferred_element_type=jnp.float32)
        base = panel[at, :]
        base_ref[at, :] = base
        hidden_ref[at, :] = (MIX * base.astype(jnp.float32) + total * scale[:, 0:1]).astype(jnp.bfloat16)


def half_kernel(dense_a, dense_b, hidden_ref, total_ref):
    size = dense_a.shape[0]
    depth = hidden_ref.shape[0]
    for n, dense in enumerate((dense_a, dense_b)):
        total_ref[pl.ds(n * size, size), :] = jnp.dot(
            dense[:, :depth], hidden_ref[...], preferred_element_type=jnp.float32
        )


def finish(dense, scale, total_ref, hidden_ref, base_ref, at, out):
    depth = hidden_ref.shape[0]
    total = total_ref[at, :] + jnp.dot(dense[:, depth:], hidden_ref[...], preferred_element_type=jnp.float32)
    out[...] = (MIX * base_ref[at, :].astype(jnp.float32) + total * scale[:, 0:1]).astype(jnp.bfloat16)


def last_kernel(dense_a, dense_b, scale_a, scale_b, total_ref, hidden_ref, base_ref, after, keep_ref, send_ref):
    size = dense_a.shape[0]
    finish(dense_b, scale_b, total_ref, hidden_ref, base_ref, pl.ds(size, size), send_ref)
    finish(dense_a, scale_a, total_ref, hidden_ref, base_ref, pl.ds(0, size), keep_ref)


def side_kernel(row, dense, scale, total_ref, hidden_ref, base_ref, after, out_ref):
    size = dense.shape[0]
    finish(dense, scale, total_ref, hidden_ref, base_ref, pl.ds(row * size, size), out_ref)


def move_halves(pieces, side, out_ref, sems):
    part = pieces[0].shape[1]
    copies = []
    for n, piece in enumerate(pieces):
        start = pl.multiple_of((side * len(pieces) + n) * part, part)
        copies.append(pltpu.make_async_copy(piece, out_ref.at[:, pl.ds(start, part)], sems.at[n]))
    for copy in copies:
        copy.start()
    for copy in copies:
        copy.wait()


def hold_kernel(sent_ref, after_0, after_1, back_ref):
    back_ref[...] = sent_ref[...]


def keep_kernel(keep_0, keep_1, out_ref, sems):
    dom, z = lax.axis_index("dom"), lax.axis_index("grp")
    move_halves((keep_0, keep_1), half_of(dom % 2 == 1, z), out_ref, sems)


def join_kernel(early_0, late_0, got_1, _, out_ref, sems):
    dom, z = lax.axis_index("dom"), lax.axis_index("grp")
    side = 1 - half_of(dom % 2 == 1, z)

    @pl.when(dom % 2 == 0)
    def _():
        move_halves((early_0, got_1), side, out_ref, sems)

    @pl.when(dom % 2 == 1)
    def _():
        move_halves((late_0, got_1), side, out_ref, sems)


def row_step(core):
    return 1 if core == 0 else 3


def shards(doms, depth, encoded, owner_of, nbr_blocks, nbr_count, edge_weights):
    f32, bf16, i32 = jnp.float32, jnp.bfloat16, jnp.int32
    rows, width = encoded.shape
    half = width // 2
    blocks, slots, size, _ = edge_weights.shape
    nodes = rows * depth
    devices = [(d, q) for d in range(doms) for q in range(depth)]
    row_pairs = [(d * depth + q, d * depth + (q ^ row_step(d % 2))) for d, q in devices]
    col_pairs = [(d * depth + q, d * depth + (q ^ row_step(1 - d % 2))) for d, q in devices]

    def to_row(a):
        return lax.ppermute(a, AXES, row_pairs)

    def to_col(a):
        return lax.ppermute(a, AXES, col_pairs)

    def to_row_of(core, a):
        return lax.ppermute(a, AXES, [(d * depth + q, d * depth + (q ^ row_step(core))) for d, q in devices])

    far_blocks, far_count = to_row(nbr_blocks), to_row(nbr_count)

    def dense_of(lists, count, weights, limit):
        return kernel_call(
            dense_kernel,
            (
                jax.ShapeDtypeStruct((blocks * size, nodes), bf16),
                jax.ShapeDtypeStruct((blocks * size, 128), f32),
                jax.ShapeDtypeStruct((8, 128), f32),
            ),
            [SMEM, SMEM, ANY],
            0,
            8 << 20,
            scratch=[pltpu.VMEM(weights.shape, bf16), pltpu.SemaphoreType.DMA((blocks,))],
            limit=limit,
        )(lists, count, weights)

    held = pltpu.VMEM((2, rows, half), f32)
    other = jax.ShapeDtypeStruct((rows // 2 + 16, half), bf16)
    other_0, other_1, pick, place = kernel_call(
        functools.partial(sort_kernel, doms),
        (other, other, jax.ShapeDtypeStruct((rows, rows), bf16), jax.ShapeDtypeStruct((16, rows), bf16)),
        [ANY, ANY],
        2 * rows * rows * half,
        4 << 20,
        scratch=[held, pltpu.VMEM((1, rows), i32), pltpu.SemaphoreType.DMA((3,))],
        limit=58,
    )(owner_of.reshape(1, rows), encoded)
    row_0, row_1 = to_row_of(0, other_0), to_row_of(1, other_1)
    per = rows // doms
    mine = kernel_call(
        functools.partial(mine_kernel, per),
        jax.ShapeDtypeStruct((rows, half), bf16),
        [ANY, VMEM],
        2 * rows * rows * half,
        4 << 20,
        scratch=[held, pltpu.SemaphoreType.DMA((2,))],
        limit=50,
    )(encoded, pick)
    sent_weights, mine, row_0, row_1, far_blocks, far_count = lax.optimization_barrier(
        (edge_weights, mine, row_0, row_1, far_blocks, far_count)
    )
    far_weights = to_row(sent_weights)
    packed = kernel_call(
        functools.partial(pack_kernel, per),
        jax.ShapeDtypeStruct((rows, width + 128), bf16),
        [VMEM] * 4,
        1 << 20,
        2 << 20,
    )(place, row_0, row_1, mine)

    packed = lax.all_to_all(packed, "dom", 0, 0, tiled=True)
    dense_a, scale_a, token_a = dense_of(nbr_blocks, nbr_count, edge_weights, 50)
    near_rows = kernel_call(
        place_kernel,
        tuple(jax.ShapeDtypeStruct((rows + (16 if c == 0 else 0), 2 * w), bf16) for c, w in enumerate(WIDTHS)),
        [VMEM, ANY],
        1 << 20,
        1 << 20,
    )(packed, token_a)
    far_rows = [to_col(a) for a in near_rows]

    dense_b, scale_b, token_b = dense_of(far_blocks, far_count, far_weights, 10)

    def picks_of(first_rows, token):
        return kernel_call(
            pick_kernel,
            jax.ShapeDtypeStruct((2, nodes, rows), bf16),
            [VMEM, ANY],
            1 << 20,
            4 << 20,
        )(first_rows, token)

    near_picks, far_picks = picks_of(near_rows[0], token_a), picks_of(far_rows[0], token_b)

    mine_n = 2 * rows
    steps = []
    for c, part in enumerate(WIDTHS):
        placed = kernel_call(
            part_kernel,
            jax.ShapeDtypeStruct((nodes, part), bf16),
            [VMEM] * 2,
            4 * nodes * rows * part,
            4 << 20,
        )(near_picks, near_rows[c])
        base, hidden = kernel_call(
            first_kernel,
            (jax.ShapeDtypeStruct((mine_n, part), bf16), jax.ShapeDtypeStruct((mine_n, part), bf16)),
            [VMEM] * 7,
            4 * nodes * rows * part + 2 * mine_n * nodes * part,
            4 << 20,
            scratch=[pltpu.VMEM((nodes, part), bf16)],
        )(dense_a, dense_b, scale_a, scale_b, far_picks, placed, far_rows[c])
        far_hidden = to_col(hidden)
        running = kernel_call(
            half_kernel,
            jax.ShapeDtypeStruct((mine_n, part), f32),
            [VMEM] * 3,
            2 * mine_n * mine_n * part,
            4 << 20,
        )(dense_a, dense_b, hidden)
        steps.append((running, far_hidden, base))

    part = WIDTHS[0]
    out_shape = jax.ShapeDtypeStruct((rows, part), bf16)
    work = 2 * rows * mine_n * part
    keep_0, send_0 = kernel_call(last_kernel, (out_shape,) * 2, [VMEM] * 7 + [ANY], 2 * work, 4 << 20)(
        dense_a, dense_b, scale_a, scale_b, *steps[0], steps[1][0]
    )
    sides = []
    for row, dense, scale, after in ((1, dense_b, scale_b, send_0), (0, dense_a, scale_a, None)):
        sides.append(
            kernel_call(
                functools.partial(side_kernel, row), out_shape, [VMEM] * 5 + [ANY], work, 2 << 20
            )(dense, scale, *steps[1], sides[0] if after is None else after)
        )
    kept, sent = [keep_0, sides[1]], [send_0, sides[0]]

    def to_row_on(core, a):
        return lax.ppermute(a, AXES, [(p, q) for p, q in row_pairs if p // depth % 2 == core])

    early_0 = to_row_on(0, sent[0])
    got_1 = to_row(sent[1])
    whole = jax.ShapeDtypeStruct((rows, width), bf16)
    held_back = kernel_call(hold_kernel, out_shape, [VMEM, ANY, ANY], 0, 1 << 19)(sent[0], early_0, sent[1])
    late_0 = to_row_on(1, held_back)
    half_done = pl.pallas_call(
        keep_kernel,
        out_shape=whole,
        in_specs=[VMEM] * 2,
        out_specs=ANY,
        scratch_shapes=[pltpu.SemaphoreType.DMA((2,))],
        compiler_params=pltpu.CompilerParams(vmem_limit_bytes=8 << 20),
    )(*kept)
    return pl.pallas_call(
        join_kernel,
        out_shape=whole,
        in_specs=[VMEM] * 3 + [ANY],
        out_specs=ANY,
        input_output_aliases={3: 0},
        scratch_shapes=[pltpu.SemaphoreType.DMA((2,))],
        compiler_params=pltpu.CompilerParams(vmem_limit_bytes=8 << 20),
    )(early_0, late_0, got_1, half_done)


def solution(mesh):
    return jax.shard_map(
        functools.partial(shards, mesh.shape["dom"], mesh.shape["grp"]),
        mesh=mesh,
        in_specs=(P(AXES, None), P(AXES), P(AXES, None), P(AXES), P(AXES, None, None, None)),
        out_specs=P(AXES, None),
        check_vma=False,
    )
```

```python
import functools

import jax
import jax.numpy as jnp
from jax import lax
from jax.experimental import pallas as pl
from jax.experimental.pallas import tpu as pltpu
from jax.sharding import PartitionSpec as P

AXES = ("dom", "grp")
MIX = 0.3
WIDTHS = (256, 256)
VMEM = pl.BlockSpec(memory_space=pltpu.VMEM)
SMEM = pl.BlockSpec(memory_space=pltpu.SMEM)
ANY = pl.BlockSpec(memory_space=pl.ANY)


def kernel_call(body, out_shape, in_specs, flops, moved, scratch=(), limit=10):
    outs = out_shape if isinstance(out_shape, (tuple, list)) else (out_shape,)
    specs = tuple(VMEM for _ in outs)
    return pl.pallas_call(
        body,
        out_shape=out_shape,
        in_specs=in_specs,
        out_specs=specs if isinstance(out_shape, (tuple, list)) else specs[0],
        scratch_shapes=scratch,
        compiler_params=pltpu.CompilerParams(vmem_limit_bytes=limit * 1024 * 1024),
        cost_estimate=pl.CostEstimate(flops=flops, bytes_accessed=moved, transcendentals=0),
    )


def half_of(core_is_odd, z):
    return jnp.where(core_is_odd, z // 2, ((z + 1) // 2) % 2)


def sort_kernel(doms, owner_hbm, enc_ref, other_0, other_1, pick_ref, place_ref, enc, owner_ref, sems):
    rows, width = enc_ref.shape
    half = width // 2
    z = lax.axis_index("grp")
    first = pltpu.make_async_copy(owner_hbm, owner_ref, sems.at[2])
    first.start()
    loads = []
    for core in range(2):
        start = pl.multiple_of((1 - half_of(core == 1, z)) * half, half)
        loads.append(pltpu.make_async_copy(enc_ref.at[:, pl.ds(start, half)], enc.at[core], sems.at[core]))
    for load in loads:
        load.start()
    per = rows // doms
    before = (
        lax.broadcasted_iota(jnp.int32, (rows, rows), 0)
        < lax.broadcasted_iota(jnp.int32, (rows, rows), 1)
    ).astype(jnp.bfloat16)
    first.wait()
    owner = owner_ref[...]
    group_nodes = rows * 4
    tdom = owner // group_nodes
    place = owner - tdom * group_nodes
    hot = (lax.broadcasted_iota(jnp.int32, (doms, rows), 0) == tdom).astype(jnp.float32)
    seen = jnp.dot(hot.astype(jnp.bfloat16), before, preferred_element_type=jnp.float32)
    rank = jnp.sum(hot * seen, axis=0, keepdims=True)
    block = (tdom % 2) * (doms // 2) + tdom // 2
    slot = block * per + rank.astype(jnp.int32)
    pick_ref[...] = (lax.broadcasted_iota(jnp.int32, (rows, rows), 0) == slot).astype(jnp.bfloat16)
    line = lax.broadcasted_iota(jnp.int32, (16, rows), 0)
    coded = jnp.where(line == 0, place // 64, jnp.where(line == 1, place % 64, 0))
    places = lax.dot_general(
        coded.astype(jnp.float32).astype(jnp.bfloat16),
        pick_ref[...],
        (((1,), (1,)), ((), ())),
        preferred_element_type=jnp.float32,
    ).astype(jnp.bfloat16)
    place_ref[...] = places
    part = rows // 2
    for core, out in enumerate((other_0, other_1)):
        out[part:, :part] = places[:, core * part : (core + 1) * part]
        out[part:, part:] = jnp.zeros((16, half - part), jnp.bfloat16)
        loads[core].wait()
        out[:part, :] = jnp.dot(
            pick_ref[pl.ds(core * part, part), :],
            enc[core].astype(jnp.bfloat16),
            preferred_element_type=jnp.float32,
        ).astype(jnp.bfloat16)


def by_dom(core, block, per):
    return pl.ds((2 * block + core) * per, per)


def pieces(own):
    at, start = [], 0
    for width in WIDTHS:
        at.append((2 * start + (0 if own else width), start, width))
        start += width
    return at


def mine_kernel(per, enc_ref, pick_ref, mine_ref, enc, sems):
    rows, width = enc_ref.shape
    half = width // 2
    z = lax.axis_index("grp")
    loads = []
    for core in range(2):
        start = pl.multiple_of(half_of(core == 1, z) * half, half)
        loads.append(pltpu.make_async_copy(enc_ref.at[:, pl.ds(start, half)], enc.at[core], sems.at[core]))
    for load in loads:
        load.start()
    for core in range(2):
        loads[core].wait()
        part = jnp.dot(
            pick_ref[pl.ds(core * rows // 2, rows // 2), :],
            enc[core].astype(jnp.bfloat16),
            preferred_element_type=jnp.float32,
        ).astype(jnp.bfloat16)
        for block in range(rows // 2 // per):
            mine_ref[by_dom(core, block, per), :] = part[block * per : (block + 1) * per, :]


def pack_kernel(per, place_ref, row_0, row_1, mine_ref, packed_ref):
    half = row_0.shape[1]
    size = row_0.shape[0] - 16
    line = lax.broadcasted_iota(jnp.int32, (16, 128), 0)
    lane = lax.broadcasted_iota(jnp.int32, (16, 128), 1)
    for to, start, wide in pieces(True):
        packed_ref[:, to : to + wide] = mine_ref[:, start : start + wide]
    for core, row in enumerate((row_0, row_1)):
        total = jnp.zeros((size, 128), jnp.float32)
        for n, lines in enumerate((place_ref[:, core * size : (core + 1) * size], row[size:, :size])):
            spread = ((lane == line + 2 * n) & (line < 2)).astype(jnp.bfloat16)
            total += lax.dot_general(
                lines, spread, (((0,), (0,)), ((), ())), preferred_element_type=jnp.float32
            )
        total = total.astype(jnp.bfloat16)
        for block in range(size // per):
            at = by_dom(core, block, per)
            span = slice(block * per, (block + 1) * per)
            for to, start, wide in pieces(False):
                packed_ref[at, to : to + wide] = row[span, start : start + wide]
            packed_ref[at, 2 * half :] = total[span, :]


def place_kernel(arrived_ref, token, *outs):
    rows = arrived_ref.shape[0]
    total = sum(out.shape[1] for out in outs)
    line = lax.broadcasted_iota(jnp.int32, (16, 128), 0)
    lane = lax.broadcasted_iota(jnp.int32, (16, 128), 1)
    spread = ((lane == line) & (line < 4)).astype(jnp.bfloat16)
    outs[0][rows:, :rows] = lax.dot_general(
        spread, arrived_ref[:, total:], (((1,), (1,)), ((), ())), preferred_element_type=jnp.float32
    ).astype(jnp.bfloat16)
    if outs[0].shape[1] > rows:
        outs[0][rows:, rows:] = jnp.zeros((16, outs[0].shape[1] - rows), jnp.bfloat16)
    start = 0
    for out in outs:
        out[:rows, :] = arrived_ref[:, start : start + out.shape[1]]
        start += out.shape[1]


def dense_kernel(list_ref, count_ref, weight_ref, dense_ref, scale_ref, token_ref, held, sems):
    blocks, _, size, _ = weight_ref.shape
    dom, z = lax.axis_index("dom"), lax.axis_index("grp")
    loads = [pltpu.make_async_copy(weight_ref.at[b], held.at[b], sems.at[b]) for b in range(blocks)]
    for load in loads:
        load.start()
    for b in range(blocks):
        dense_ref[pl.ds(b * size, size), :] = jnp.zeros((size, dense_ref.shape[1]), dense_ref.dtype)
    for b in range(blocks):
        span = pl.ds(b * size, size)
        loads[b].wait()

        def put(k, total):
            block = held[b, k]
            target = list_ref[b, k]
            column = steps_of(dom, z, target // blocks) * blocks + target % blocks
            start = pl.multiple_of(column * size, size)
            dense_ref[span, pl.ds(start, size)] = block
            return total + block.astype(jnp.float32)

        total = lax.fori_loop(0, count_ref[b], put, jnp.zeros((size, size), jnp.float32))
        degree = jnp.sum(total, axis=1, keepdims=True)
        scale_ref[span, :] = jnp.broadcast_to((1.0 - MIX) * lax.rsqrt(degree), (size, 128))
    token_ref[...] = jnp.zeros(token_ref.shape, token_ref.dtype)


def steps_of(dom, z, q):
    odd = dom % 2 == 1
    rx, fx = jnp.where(odd, 3, 1), jnp.where(odd, 1, 3)
    step = q ^ z
    return jnp.where(step == 0, 0, jnp.where(step == rx, 1, jnp.where(step == fx, 2, 3)))


def pick_kernel(rows_ref, *refs):
    pick_ref = refs[-1]
    nodes, size = pick_ref.shape[1:]
    dom, z = lax.axis_index("dom"), lax.axis_index("grp")
    coded = rows_ref[pl.ds(size, 16), :size].astype(jnp.float32).astype(jnp.int32)
    for k in range(2):
        p = coded[2 * k : 2 * k + 1, :] * 64 + coded[2 * k + 1 : 2 * k + 2, :]
        spot = steps_of(dom, z, p // size) * size + p % size
        for n in range(nodes // size):
            node = lax.broadcasted_iota(jnp.int32, (size, size), 0) + n * size
            pick_ref[k, pl.ds(n * size, size), :] = (node == spot).astype(jnp.bfloat16)


def part_kernel(pick_ref, near_ref, part_ref):
    size, width = pick_ref.shape[2], part_ref.shape[1]
    for n in range(part_ref.shape[0] // size):
        at = pl.ds(n * size, size)
        total = jnp.dot(pick_ref[0, at, :], near_ref[:size, :width], preferred_element_type=jnp.float32)
        total += jnp.dot(pick_ref[1, at, :], near_ref[:size, width:], preferred_element_type=jnp.float32)
        part_ref[at, :] = total.astype(jnp.bfloat16)


def first_kernel(dense_a, dense_b, scale_a, scale_b, pick_ref, part_ref, far_ref, base_ref, hidden_ref, panel):
    size = dense_a.shape[0]
    width = part_ref.shape[1]
    for n in range(panel.shape[0] // size):
        at = pl.ds(n * size, size)
        total = jnp.dot(pick_ref[0, at, :], far_ref[:size, :width], preferred_element_type=jnp.float32)
        total += jnp.dot(pick_ref[1, at, :], far_ref[:size, width:], preferred_element_type=jnp.float32)
        panel[at, :] = part_ref[at, :] + total.astype(jnp.bfloat16)
    for n, (dense, scale) in enumerate(((dense_a, scale_a), (dense_b, scale_b))):
        at = pl.ds(n * size, size)
        total = jnp.dot(dense[...], panel[...], preferred_element_type=jnp.float32)
        base = panel[at, :]
        base_ref[at, :] = base
        hidden_ref[at, :] = (MIX * base.astype(jnp.float32) + total * scale[:, 0:1]).astype(jnp.bfloat16)


def half_kernel(dense_a, dense_b, hidden_ref, total_ref):
    size = dense_a.shape[0]
    depth = hidden_ref.shape[0]
    for n, dense in enumerate((dense_a, dense_b)):
        total_ref[pl.ds(n * size, size), :] = jnp.dot(
            dense[:, :depth], hidden_ref[...], preferred_element_type=jnp.float32
        )


def finish(dense, scale, total_ref, hidden_ref, base_ref, at, out):
    depth = hidden_ref.shape[0]
    total = total_ref[at, :] + jnp.dot(dense[:, depth:], hidden_ref[...], preferred_element_type=jnp.float32)
    out[...] = (MIX * base_ref[at, :].astype(jnp.float32) + total * scale[:, 0:1]).astype(jnp.bfloat16)


def last_kernel(dense_a, dense_b, scale_a, scale_b, total_ref, hidden_ref, base_ref, after, keep_ref, send_ref):
    size = dense_a.shape[0]
    finish(dense_b, scale_b, total_ref, hidden_ref, base_ref, pl.ds(size, size), send_ref)
    finish(dense_a, scale_a, total_ref, hidden_ref, base_ref, pl.ds(0, size), keep_ref)


def side_kernel(row, dense, scale, total_ref, hidden_ref, base_ref, after, out_ref):
    size = dense.shape[0]
    finish(dense, scale, total_ref, hidden_ref, base_ref, pl.ds(row * size, size), out_ref)


def move_halves(pieces, side, out_ref, sems):
    part = pieces[0].shape[1]
    copies = []
    for n, piece in enumerate(pieces):
        start = pl.multiple_of((side * len(pieces) + n) * part, part)
        copies.append(pltpu.make_async_copy(piece, out_ref.at[:, pl.ds(start, part)], sems.at[n]))
    for copy in copies:
        copy.start()
    for copy in copies:
        copy.wait()


def hold_kernel(sent_ref, after_0, after_1, back_ref):
    back_ref[...] = sent_ref[...]


def keep_kernel(keep_0, keep_1, out_ref, sems):
    dom, z = lax.axis_index("dom"), lax.axis_index("grp")
    move_halves((keep_0, keep_1), half_of(dom % 2 == 1, z), out_ref, sems)


def join_kernel(early_0, late_0, got_1, _, out_ref, sems):
    dom, z = lax.axis_index("dom"), lax.axis_index("grp")
    side = 1 - half_of(dom % 2 == 1, z)

    @pl.when(dom % 2 == 0)
    def _():
        move_halves((early_0, got_1), side, out_ref, sems)

    @pl.when(dom % 2 == 1)
    def _():
        move_halves((late_0, got_1), side, out_ref, sems)


def row_step(core):
    return 1 if core == 0 else 3


def shards(doms, depth, encoded, owner_of, nbr_blocks, nbr_count, edge_weights):
    f32, bf16, i32 = jnp.float32, jnp.bfloat16, jnp.int32
    rows, width = encoded.shape
    half = width // 2
    blocks, slots, size, _ = edge_weights.shape
    nodes = rows * depth
    devices = [(d, q) for d in range(doms) for q in range(depth)]
    row_pairs = [(d * depth + q, d * depth + (q ^ row_step(d % 2))) for d, q in devices]
    col_pairs = [(d * depth + q, d * depth + (q ^ row_step(1 - d % 2))) for d, q in devices]

    def to_row(a):
        return lax.ppermute(a, AXES, row_pairs)

    def to_col(a):
        return lax.ppermute(a, AXES, col_pairs)

    def to_row_of(core, a):
        return lax.ppermute(a, AXES, [(d * depth + q, d * depth + (q ^ row_step(core))) for d, q in devices])

    far_blocks, far_count = to_row(nbr_blocks), to_row(nbr_count)

    def dense_of(lists, count, weights, limit):
        return kernel_call(
            dense_kernel,
            (
                jax.ShapeDtypeStruct((blocks * size, nodes), bf16),
                jax.ShapeDtypeStruct((blocks * size, 128), f32),
                jax.ShapeDtypeStruct((8, 128), f32),
            ),
            [SMEM, SMEM, ANY],
            0,
            8 << 20,
            scratch=[pltpu.VMEM(weights.shape, bf16), pltpu.SemaphoreType.DMA((blocks,))],
            limit=limit,
        )(lists, count, weights)

    held = pltpu.VMEM((2, rows, half), f32)
    other = jax.ShapeDtypeStruct((rows // 2 + 16, half), bf16)
    other_0, other_1, pick, place = kernel_call(
        functools.partial(sort_kernel, doms),
        (other, other, jax.ShapeDtypeStruct((rows, rows), bf16), jax.ShapeDtypeStruct((16, rows), bf16)),
        [ANY, ANY],
        2 * rows * rows * half,
        4 << 20,
        scratch=[held, pltpu.VMEM((1, rows), i32), pltpu.SemaphoreType.DMA((3,))],
        limit=58,
    )(owner_of.reshape(1, rows), encoded)
    row_0, row_1 = to_row_of(0, other_0), to_row_of(1, other_1)
    per = rows // doms
    mine = kernel_call(
        functools.partial(mine_kernel, per),
        jax.ShapeDtypeStruct((rows, half), bf16),
        [ANY, VMEM],
        2 * rows * rows * half,
        4 << 20,
        scratch=[held, pltpu.SemaphoreType.DMA((2,))],
        limit=50,
    )(encoded, pick)
    sent_weights, mine, row_0, row_1, far_blocks, far_count = lax.optimization_barrier(
        (edge_weights, mine, row_0, row_1, far_blocks, far_count)
    )
    far_weights = to_row(sent_weights)
    packed = kernel_call(
        functools.partial(pack_kernel, per),
        jax.ShapeDtypeStruct((rows, width + 128), bf16),
        [VMEM] * 4,
        1 << 20,
        2 << 20,
    )(place, row_0, row_1, mine)

    packed = lax.all_to_all(packed, "dom", 0, 0, tiled=True)
    dense_a, scale_a, token_a = dense_of(nbr_blocks, nbr_count, edge_weights, 50)
    near_rows = kernel_call(
        place_kernel,
        tuple(jax.ShapeDtypeStruct((rows + (16 if c == 0 else 0), 2 * w), bf16) for c, w in enumerate(WIDTHS)),
        [VMEM, ANY],
        1 << 20,
        1 << 20,
    )(packed, token_a)
    far_rows = [to_col(a) for a in near_rows]

    dense_b, scale_b, token_b = dense_of(far_blocks, far_count, far_weights, 10)

    def picks_of(first_rows, *after):
        return kernel_call(
            pick_kernel,
            jax.ShapeDtypeStruct((2, nodes, rows), bf16),
            [VMEM] + [ANY] * len(after),
            1 << 20,
            4 << 20,
        )(first_rows, *after)

    near_picks = picks_of(near_rows[0], token_a)
    placed = [
        kernel_call(
            part_kernel,
            jax.ShapeDtypeStruct((nodes, part), bf16),
            [VMEM] * 2,
            4 * nodes * rows * part,
            4 << 20,
        )(near_picks, near_rows[c])
        for c, part in enumerate(WIDTHS)
    ]
    far_picks = picks_of(far_rows[0], token_b, *placed)

    mine_n = 2 * rows
    steps = []
    for c, part in enumerate(WIDTHS):
        base, hidden = kernel_call(
            first_kernel,
            (jax.ShapeDtypeStruct((mine_n, part), bf16), jax.ShapeDtypeStruct((mine_n, part), bf16)),
            [VMEM] * 7,
            4 * nodes * rows * part + 2 * mine_n * nodes * part,
            4 << 20,
            scratch=[pltpu.VMEM((nodes, part), bf16)],
        )(dense_a, dense_b, scale_a, scale_b, far_picks, placed[c], far_rows[c])
        far_hidden = to_col(hidden)
        running = kernel_call(
            half_kernel,
            jax.ShapeDtypeStruct((mine_n, part), f32),
            [VMEM] * 3,
            2 * mine_n * mine_n * part,
            4 << 20,
        )(dense_a, dense_b, hidden)
        steps.append((running, far_hidden, base))

    part = WIDTHS[0]
    out_shape = jax.ShapeDtypeStruct((rows, part), bf16)
    work = 2 * rows * mine_n * part
    keep_0, send_0 = kernel_call(last_kernel, (out_shape,) * 2, [VMEM] * 7 + [ANY], 2 * work, 4 << 20)(
        dense_a, dense_b, scale_a, scale_b, *steps[0], steps[1][0]
    )
    sides = []
    for row, dense, scale, after in ((1, dense_b, scale_b, send_0), (0, dense_a, scale_a, None)):
        sides.append(
            kernel_call(
                functools.partial(side_kernel, row), out_shape, [VMEM] * 5 + [ANY], work, 2 << 20
            )(dense, scale, *steps[1], sides[0] if after is None else after)
        )
    kept, sent = [keep_0, sides[1]], [send_0, sides[0]]

    def to_row_on(core, a):
        return lax.ppermute(a, AXES, [(p, q) for p, q in row_pairs if p // depth % 2 == core])

    early_0 = to_row_on(0, sent[0])
    got_1 = to_row(sent[1])
    whole = jax.ShapeDtypeStruct((rows, width), bf16)
    held_back = kernel_call(hold_kernel, out_shape, [VMEM, ANY, ANY], 0, 1 << 19)(sent[0], early_0, sent[1])
    late_0 = to_row_on(1, held_back)
    half_done = pl.pallas_call(
        keep_kernel,
        out_shape=whole,
        in_specs=[VMEM] * 2,
        out_specs=ANY,
        scratch_shapes=[pltpu.SemaphoreType.DMA((2,))],
        compiler_params=pltpu.CompilerParams(vmem_limit_bytes=8 << 20),
    )(*kept)
    return pl.pallas_call(
        join_kernel,
        out_shape=whole,
        in_specs=[VMEM] * 3 + [ANY],
        out_specs=ANY,
        input_output_aliases={3: 0},
        scratch_shapes=[pltpu.SemaphoreType.DMA((2,))],
        compiler_params=pltpu.CompilerParams(vmem_limit_bytes=8 << 20),
    )(early_0, late_0, got_1, half_done)


def solution(mesh):
    return jax.shard_map(
        functools.partial(shards, mesh.shape["dom"], mesh.shape["grp"]),
        mesh=mesh,
        in_specs=(P(AXES, None), P(AXES), P(AXES, None), P(AXES), P(AXES, None, None, None)),
        out_specs=P(AXES, None),
        check_vma=False,
    )
```

```python
import functools

import jax
import jax.numpy as jnp
from jax import lax
from jax.experimental import pallas as pl
from jax.experimental.pallas import tpu as pltpu
from jax.sharding import PartitionSpec as P

AXES = ("dom", "grp")
MIX = 0.3
WIDTHS = (256, 256)
VMEM = pl.BlockSpec(memory_space=pltpu.VMEM)
SMEM = pl.BlockSpec(memory_space=pltpu.SMEM)
ANY = pl.BlockSpec(memory_space=pl.ANY)


def kernel_call(body, out_shape, in_specs, flops, moved, scratch=(), limit=10):
    outs = out_shape if isinstance(out_shape, (tuple, list)) else (out_shape,)
    specs = tuple(VMEM for _ in outs)
    return pl.pallas_call(
        body,
        out_shape=out_shape,
        in_specs=in_specs,
        out_specs=specs if isinstance(out_shape, (tuple, list)) else specs[0],
        scratch_shapes=scratch,
        compiler_params=pltpu.CompilerParams(vmem_limit_bytes=limit * 1024 * 1024),
        cost_estimate=pl.CostEstimate(flops=flops, bytes_accessed=moved, transcendentals=0),
    )


def half_of(core_is_odd, z):
    return jnp.where(core_is_odd, z // 2, ((z + 1) // 2) % 2)


def sort_kernel(doms, owner_hbm, enc_ref, other_0, other_1, pick_ref, place_ref, enc, owner_ref, sems):
    rows, width = enc_ref.shape
    half = width // 2
    z = lax.axis_index("grp")
    first = pltpu.make_async_copy(owner_hbm, owner_ref, sems.at[2])
    first.start()
    loads = []
    for core in range(2):
        start = pl.multiple_of((1 - half_of(core == 1, z)) * half, half)
        loads.append(pltpu.make_async_copy(enc_ref.at[:, pl.ds(start, half)], enc.at[core], sems.at[core]))
    for load in loads:
        load.start()
    per = rows // doms
    before = (
        lax.broadcasted_iota(jnp.int32, (rows, rows), 0)
        < lax.broadcasted_iota(jnp.int32, (rows, rows), 1)
    ).astype(jnp.bfloat16)
    first.wait()
    owner = owner_ref[...]
    group_nodes = rows * 4
    tdom = owner // group_nodes
    place = owner - tdom * group_nodes
    hot = (lax.broadcasted_iota(jnp.int32, (doms, rows), 0) == tdom).astype(jnp.float32)
    seen = jnp.dot(hot.astype(jnp.bfloat16), before, preferred_element_type=jnp.float32)
    rank = jnp.sum(hot * seen, axis=0, keepdims=True)
    block = (tdom % 2) * (doms // 2) + tdom // 2
    slot = block * per + rank.astype(jnp.int32)
    pick_ref[...] = (lax.broadcasted_iota(jnp.int32, (rows, rows), 0) == slot).astype(jnp.bfloat16)
    line = lax.broadcasted_iota(jnp.int32, (16, rows), 0)
    coded = jnp.where(line == 0, place // 64, jnp.where(line == 1, place % 64, 0))
    places = lax.dot_general(
        coded.astype(jnp.float32).astype(jnp.bfloat16),
        pick_ref[...],
        (((1,), (1,)), ((), ())),
        preferred_element_type=jnp.float32,
    ).astype(jnp.bfloat16)
    place_ref[...] = places
    part = rows // 2
    for core, out in enumerate((other_0, other_1)):
        out[part:, :part] = places[:, core * part : (core + 1) * part]
        out[part:, part:] = jnp.zeros((16, half - part), jnp.bfloat16)
        loads[core].wait()
        out[:part, :] = jnp.dot(
            pick_ref[pl.ds(core * part, part), :],
            enc[core].astype(jnp.bfloat16),
            preferred_element_type=jnp.float32,
        ).astype(jnp.bfloat16)


def by_dom(core, block, per):
    return pl.ds((2 * block + core) * per, per)


def pieces(own):
    at, start = [], 0
    for width in WIDTHS:
        at.append((2 * start + (0 if own else width), start, width))
        start += width
    return at


def mine_kernel(per, enc_ref, pick_ref, mine_ref, enc, sems):
    rows, width = enc_ref.shape
    half = width // 2
    z = lax.axis_index("grp")
    loads = []
    for core in range(2):
        start = pl.multiple_of(half_of(core == 1, z) * half, half)
        loads.append(pltpu.make_async_copy(enc_ref.at[:, pl.ds(start, half)], enc.at[core], sems.at[core]))
    for load in loads:
        load.start()
    for core in range(2):
        loads[core].wait()
        part = jnp.dot(
            pick_ref[pl.ds(core * rows // 2, rows // 2), :],
            enc[core].astype(jnp.bfloat16),
            preferred_element_type=jnp.float32,
        ).astype(jnp.bfloat16)
        for block in range(rows // 2 // per):
            mine_ref[by_dom(core, block, per), :] = part[block * per : (block + 1) * per, :]


def pack_kernel(per, place_ref, row_0, row_1, mine_ref, packed_ref):
    half = row_0.shape[1]
    size = row_0.shape[0] - 16
    line = lax.broadcasted_iota(jnp.int32, (16, 128), 0)
    lane = lax.broadcasted_iota(jnp.int32, (16, 128), 1)
    for to, start, wide in pieces(True):
        packed_ref[:, to : to + wide] = mine_ref[:, start : start + wide]
    for core, row in enumerate((row_0, row_1)):
        total = jnp.zeros((size, 128), jnp.float32)
        for n, lines in enumerate((place_ref[:, core * size : (core + 1) * size], row[size:, :size])):
            spread = ((lane == line + 2 * n) & (line < 2)).astype(jnp.bfloat16)
            total += lax.dot_general(
                lines, spread, (((0,), (0,)), ((), ())), preferred_element_type=jnp.float32
            )
        total = total.astype(jnp.bfloat16)
        for block in range(size // per):
            at = by_dom(core, block, per)
            span = slice(block * per, (block + 1) * per)
            for to, start, wide in pieces(False):
                packed_ref[at, to : to + wide] = row[span, start : start + wide]
            packed_ref[at, 2 * half :] = total[span, :]


def place_kernel(arrived_ref, token, *outs):
    rows = arrived_ref.shape[0]
    total = sum(out.shape[1] for out in outs)
    line = lax.broadcasted_iota(jnp.int32, (16, 128), 0)
    lane = lax.broadcasted_iota(jnp.int32, (16, 128), 1)
    spread = ((lane == line) & (line < 4)).astype(jnp.bfloat16)
    outs[0][rows:, :rows] = lax.dot_general(
        spread, arrived_ref[:, total:], (((1,), (1,)), ((), ())), preferred_element_type=jnp.float32
    ).astype(jnp.bfloat16)
    if outs[0].shape[1] > rows:
        outs[0][rows:, rows:] = jnp.zeros((16, outs[0].shape[1] - rows), jnp.bfloat16)
    start = 0
    for out in outs:
        out[:rows, :] = arrived_ref[:, start : start + out.shape[1]]
        start += out.shape[1]


def dense_kernel(list_ref, count_ref, weight_ref, dense_ref, scale_ref, token_ref, held, sems):
    blocks, _, size, _ = weight_ref.shape
    dom, z = lax.axis_index("dom"), lax.axis_index("grp")
    loads = [pltpu.make_async_copy(weight_ref.at[b], held.at[b], sems.at[b]) for b in range(blocks)]
    for load in loads:
        load.start()
    for b in range(blocks):
        dense_ref[pl.ds(b * size, size), :] = jnp.zeros((size, dense_ref.shape[1]), dense_ref.dtype)
    for b in range(blocks):
        span = pl.ds(b * size, size)
        loads[b].wait()

        def put(k, total):
            block = held[b, k]
            target = list_ref[b, k]
            column = steps_of(dom, z, target // blocks) * blocks + target % blocks
            start = pl.multiple_of(column * size, size)
            dense_ref[span, pl.ds(start, size)] = block
            return total + block.astype(jnp.float32)

        total = lax.fori_loop(0, count_ref[b], put, jnp.zeros((size, size), jnp.float32))
        degree = jnp.sum(total, axis=1, keepdims=True)
        scale_ref[span, :] = jnp.broadcast_to((1.0 - MIX) * lax.rsqrt(degree), (size, 128))
    token_ref[...] = jnp.zeros(token_ref.shape, token_ref.dtype)


def steps_of(dom, z, q):
    odd = dom % 2 == 1
    rx, fx = jnp.where(odd, 3, 1), jnp.where(odd, 1, 3)
    step = q ^ z
    return jnp.where(step == 0, 0, jnp.where(step == rx, 1, jnp.where(step == fx, 2, 3)))


def pick_kernel(rows_ref, *refs):
    pick_ref = refs[-1]
    nodes, size = pick_ref.shape[1:]
    dom, z = lax.axis_index("dom"), lax.axis_index("grp")
    coded = rows_ref[pl.ds(size, 16), :size].astype(jnp.float32).astype(jnp.int32)
    for k in range(2):
        p = coded[2 * k : 2 * k + 1, :] * 64 + coded[2 * k + 1 : 2 * k + 2, :]
        spot = steps_of(dom, z, p // size) * size + p % size
        for n in range(nodes // size):
            node = lax.broadcasted_iota(jnp.int32, (size, size), 0) + n * size
            pick_ref[k, pl.ds(n * size, size), :] = (node == spot).astype(jnp.bfloat16)


def part_kernel(pick_ref, near_ref, part_ref):
    size, width = pick_ref.shape[2], part_ref.shape[1]
    for n in range(part_ref.shape[0] // size):
        at = pl.ds(n * size, size)
        total = jnp.dot(pick_ref[0, at, :], near_ref[:size, :width], preferred_element_type=jnp.float32)
        total += jnp.dot(pick_ref[1, at, :], near_ref[:size, width:], preferred_element_type=jnp.float32)
        part_ref[at, :] = total.astype(jnp.bfloat16)


def first_kernel(dense_a, dense_b, scale_a, scale_b, pick_ref, part_ref, far_ref, base_ref, hidden_ref, panel):
    size = dense_a.shape[0]
    width = part_ref.shape[1]
    for n in range(panel.shape[0] // size):
        at = pl.ds(n * size, size)
        total = jnp.dot(pick_ref[0, at, :], far_ref[:size, :width], preferred_element_type=jnp.float32)
        total += jnp.dot(pick_ref[1, at, :], far_ref[:size, width:], preferred_element_type=jnp.float32)
        panel[at, :] = part_ref[at, :] + total.astype(jnp.bfloat16)
    for n, (dense, scale) in enumerate(((dense_a, scale_a), (dense_b, scale_b))):
        at = pl.ds(n * size, size)
        total = jnp.dot(dense[...], panel[...], preferred_element_type=jnp.float32)
        base = panel[at, :]
        base_ref[at, :] = base
        hidden_ref[at, :] = (MIX * base.astype(jnp.float32) + total * scale[:, 0:1]).astype(jnp.bfloat16)


def half_kernel(dense_a, dense_b, hidden_ref, total_ref):
    size = dense_a.shape[0]
    depth = hidden_ref.shape[0]
    for n, dense in enumerate((dense_a, dense_b)):
        total_ref[pl.ds(n * size, size), :] = jnp.dot(
            dense[:, :depth], hidden_ref[...], preferred_element_type=jnp.float32
        )


def finish(dense, scale, total_ref, hidden_ref, base_ref, at, out):
    depth = hidden_ref.shape[0]
    total = total_ref[at, :] + jnp.dot(dense[:, depth:], hidden_ref[...], preferred_element_type=jnp.float32)
    out[...] = (MIX * base_ref[at, :].astype(jnp.float32) + total * scale[:, 0:1]).astype(jnp.bfloat16)


def last_kernel(dense_a, dense_b, scale_a, scale_b, total_ref, hidden_ref, base_ref, after, keep_ref, send_ref):
    size = dense_a.shape[0]
    finish(dense_b, scale_b, total_ref, hidden_ref, base_ref, pl.ds(size, size), send_ref)
    finish(dense_a, scale_a, total_ref, hidden_ref, base_ref, pl.ds(0, size), keep_ref)


def side_kernel(row, dense, scale, total_ref, hidden_ref, base_ref, after, out_ref):
    size = dense.shape[0]
    finish(dense, scale, total_ref, hidden_ref, base_ref, pl.ds(row * size, size), out_ref)


def move_halves(pieces, side, out_ref, sems):
    part = pieces[0].shape[1]
    copies = []
    for n, piece in enumerate(pieces):
        start = pl.multiple_of((side * len(pieces) + n) * part, part)
        copies.append(pltpu.make_async_copy(piece, out_ref.at[:, pl.ds(start, part)], sems.at[n]))
    for copy in copies:
        copy.start()
    for copy in copies:
        copy.wait()


def hold_kernel(sent_ref, after_0, after_1, back_ref):
    back_ref[...] = sent_ref[...]


def keep_kernel(keep_0, keep_1, out_ref, sems):
    dom, z = lax.axis_index("dom"), lax.axis_index("grp")
    move_halves((keep_0, keep_1), half_of(dom % 2 == 1, z), out_ref, sems)


def join_kernel(early_0, late_0, got_1, _, out_ref, sems):
    dom, z = lax.axis_index("dom"), lax.axis_index("grp")
    side = 1 - half_of(dom % 2 == 1, z)

    @pl.when(dom % 2 == 0)
    def _():
        move_halves((early_0, got_1), side, out_ref, sems)

    @pl.when(dom % 2 == 1)
    def _():
        move_halves((late_0, got_1), side, out_ref, sems)


def row_step(core):
    return 1 if core == 0 else 3


def shards(doms, depth, encoded, owner_of, nbr_blocks, nbr_count, edge_weights):
    f32, bf16, i32 = jnp.float32, jnp.bfloat16, jnp.int32
    rows, width = encoded.shape
    half = width // 2
    blocks, slots, size, _ = edge_weights.shape
    nodes = rows * depth
    devices = [(d, q) for d in range(doms) for q in range(depth)]
    row_pairs = [(d * depth + q, d * depth + (q ^ row_step(d % 2))) for d, q in devices]
    col_pairs = [(d * depth + q, d * depth + (q ^ row_step(1 - d % 2))) for d, q in devices]

    def to_row(a):
        return lax.ppermute(a, AXES, row_pairs)

    def to_col(a):
        return lax.ppermute(a, AXES, col_pairs)

    def to_row_of(core, a):
        return lax.ppermute(a, AXES, [(d * depth + q, d * depth + (q ^ row_step(core))) for d, q in devices])

    far_blocks, far_count = to_row(nbr_blocks), to_row(nbr_count)

    def dense_of(lists, count, weights, limit, work=0):
        return kernel_call(
            dense_kernel,
            (
                jax.ShapeDtypeStruct((blocks * size, nodes), bf16),
                jax.ShapeDtypeStruct((blocks * size, 128), f32),
                jax.ShapeDtypeStruct((8, 128), f32),
            ),
            [SMEM, SMEM, ANY],
            work,
            8 << 20,
            scratch=[pltpu.VMEM(weights.shape, bf16), pltpu.SemaphoreType.DMA((blocks,))],
            limit=limit,
        )(lists, count, weights)

    held = pltpu.VMEM((2, rows, half), f32)
    other = jax.ShapeDtypeStruct((rows // 2 + 16, half), bf16)
    other_0, other_1, pick, place = kernel_call(
        functools.partial(sort_kernel, doms),
        (other, other, jax.ShapeDtypeStruct((rows, rows), bf16), jax.ShapeDtypeStruct((16, rows), bf16)),
        [ANY, ANY],
        2 * rows * rows * half,
        4 << 20,
        scratch=[held, pltpu.VMEM((1, rows), i32), pltpu.SemaphoreType.DMA((3,))],
        limit=58,
    )(owner_of.reshape(1, rows), encoded)
    row_0, row_1 = to_row_of(0, other_0), to_row_of(1, other_1)
    per = rows // doms
    mine = kernel_call(
        functools.partial(mine_kernel, per),
        jax.ShapeDtypeStruct((rows, half), bf16),
        [ANY, VMEM],
        2 * rows * rows * half,
        4 << 20,
        scratch=[held, pltpu.SemaphoreType.DMA((2,))],
        limit=50,
    )(encoded, pick)
    sent_weights, mine, far_blocks, far_count = lax.optimization_barrier(
        (edge_weights, mine, far_blocks, far_count)
    )
    far_weights = to_row(sent_weights)
    packed = kernel_call(
        functools.partial(pack_kernel, per),
        jax.ShapeDtypeStruct((rows, width + 128), bf16),
        [VMEM] * 4,
        1 << 20,
        2 << 20,
    )(place, row_0, row_1, mine)

    packed = lax.all_to_all(packed, "dom", 0, 0, tiled=True)
    dense_a, scale_a, token_a = dense_of(nbr_blocks, nbr_count, edge_weights, 50, 40_000_000_000)
    near_rows = kernel_call(
        place_kernel,
        tuple(jax.ShapeDtypeStruct((rows + (16 if c == 0 else 0), 2 * w), bf16) for c, w in enumerate(WIDTHS)),
        [VMEM, ANY],
        1 << 20,
        1 << 20,
    )(packed, token_a)
    far_rows = [to_col(a) for a in near_rows]

    dense_b, scale_b, token_b = dense_of(far_blocks, far_count, far_weights, 10)

    def picks_of(first_rows, *after):
        return kernel_call(
            pick_kernel,
            jax.ShapeDtypeStruct((2, nodes, rows), bf16),
            [VMEM] + [ANY] * len(after),
            1 << 20,
            4 << 20,
        )(first_rows, *after)

    near_picks = picks_of(near_rows[0], token_a)
    placed = [
        kernel_call(
            part_kernel,
            jax.ShapeDtypeStruct((nodes, part), bf16),
            [VMEM] * 2,
            4 * nodes * rows * part,
            4 << 20,
        )(near_picks, near_rows[c])
        for c, part in enumerate(WIDTHS)
    ]
    far_picks = picks_of(far_rows[0], token_b, *placed)

    mine_n = 2 * rows
    steps = []
    for c, part in enumerate(WIDTHS):
        base, hidden = kernel_call(
            first_kernel,
            (jax.ShapeDtypeStruct((mine_n, part), bf16), jax.ShapeDtypeStruct((mine_n, part), bf16)),
            [VMEM] * 7,
            4 * nodes * rows * part + 2 * mine_n * nodes * part,
            4 << 20,
            scratch=[pltpu.VMEM((nodes, part), bf16)],
        )(dense_a, dense_b, scale_a, scale_b, far_picks, placed[c], far_rows[c])
        far_hidden = to_col(hidden)
        running = kernel_call(
            half_kernel,
            jax.ShapeDtypeStruct((mine_n, part), f32),
            [VMEM] * 3,
            2 * mine_n * mine_n * part,
            4 << 20,
        )(dense_a, dense_b, hidden)
        steps.append((running, far_hidden, base))

    part = WIDTHS[0]
    out_shape = jax.ShapeDtypeStruct((rows, part), bf16)
    work = 2 * rows * mine_n * part
    keep_0, send_0 = kernel_call(last_kernel, (out_shape,) * 2, [VMEM] * 7 + [ANY], 2 * work, 4 << 20)(
        dense_a, dense_b, scale_a, scale_b, *steps[0], steps[1][0]
    )
    sides = []
    for row, dense, scale, after in ((1, dense_b, scale_b, send_0), (0, dense_a, scale_a, None)):
        sides.append(
            kernel_call(
                functools.partial(side_kernel, row), out_shape, [VMEM] * 5 + [ANY], work, 2 << 20
            )(dense, scale, *steps[1], sides[0] if after is None else after)
        )
    kept, sent = [keep_0, sides[1]], [send_0, sides[0]]

    def to_row_on(core, a):
        return lax.ppermute(a, AXES, [(p, q) for p, q in row_pairs if p // depth % 2 == core])

    early_0 = to_row_on(0, sent[0])
    got_1 = to_row(sent[1])
    whole = jax.ShapeDtypeStruct((rows, width), bf16)
    held_back = kernel_call(hold_kernel, out_shape, [VMEM, ANY, ANY], 0, 1 << 19)(sent[0], early_0, sent[1])
    late_0 = to_row_on(1, held_back)
    half_done = pl.pallas_call(
        keep_kernel,
        out_shape=whole,
        in_specs=[VMEM] * 2,
        out_specs=ANY,
        scratch_shapes=[pltpu.SemaphoreType.DMA((2,))],
        compiler_params=pltpu.CompilerParams(vmem_limit_bytes=8 << 20),
    )(*kept)
    return pl.pallas_call(
        join_kernel,
        out_shape=whole,
        in_specs=[VMEM] * 3 + [ANY],
        out_specs=ANY,
        input_output_aliases={3: 0},
        scratch_shapes=[pltpu.SemaphoreType.DMA((2,))],
        compiler_params=pltpu.CompilerParams(vmem_limit_bytes=8 << 20),
    )(early_0, late_0, got_1, half_done)


def solution(mesh):
    return jax.shard_map(
        functools.partial(shards, mesh.shape["dom"], mesh.shape["grp"]),
        mesh=mesh,
        in_specs=(P(AXES, None), P(AXES), P(AXES, None), P(AXES), P(AXES, None, None, None)),
        out_specs=P(AXES, None),
        check_vma=False,
    )
```

```python
import functools

import jax
import jax.numpy as jnp
from jax import lax
from jax.experimental import pallas as pl
from jax.experimental.pallas import tpu as pltpu
from jax.sharding import PartitionSpec as P

AXES = ("dom", "grp")
MIX = 0.3
WIDTHS = (256, 256)
VMEM = pl.BlockSpec(memory_space=pltpu.VMEM)
SMEM = pl.BlockSpec(memory_space=pltpu.SMEM)
ANY = pl.BlockSpec(memory_space=pl.ANY)


def kernel_call(body, out_shape, in_specs, flops, moved, scratch=(), limit=10):
    outs = out_shape if isinstance(out_shape, (tuple, list)) else (out_shape,)
    specs = tuple(VMEM for _ in outs)
    return pl.pallas_call(
        body,
        out_shape=out_shape,
        in_specs=in_specs,
        out_specs=specs if isinstance(out_shape, (tuple, list)) else specs[0],
        scratch_shapes=scratch,
        compiler_params=pltpu.CompilerParams(vmem_limit_bytes=limit * 1024 * 1024),
        cost_estimate=pl.CostEstimate(flops=flops, bytes_accessed=moved, transcendentals=0),
    )


def half_of(core_is_odd, z):
    return jnp.where(core_is_odd, z // 2, ((z + 1) // 2) % 2)


def sort_kernel(doms, owner_hbm, enc_ref, other_0, other_1, pick_ref, place_ref, enc, owner_ref, sems):
    rows, width = enc_ref.shape
    half = width // 2
    z = lax.axis_index("grp")
    first = pltpu.make_async_copy(owner_hbm, owner_ref, sems.at[2])
    first.start()
    loads = []
    for core in range(2):
        start = pl.multiple_of((1 - half_of(core == 1, z)) * half, half)
        loads.append(pltpu.make_async_copy(enc_ref.at[:, pl.ds(start, half)], enc.at[core], sems.at[core]))
    for load in loads:
        load.start()
    per = rows // doms
    before = (
        lax.broadcasted_iota(jnp.int32, (rows, rows), 0)
        < lax.broadcasted_iota(jnp.int32, (rows, rows), 1)
    ).astype(jnp.bfloat16)
    first.wait()
    owner = owner_ref[...]
    group_nodes = rows * 4
    tdom = owner // group_nodes
    place = owner - tdom * group_nodes
    hot = (lax.broadcasted_iota(jnp.int32, (doms, rows), 0) == tdom).astype(jnp.float32)
    seen = jnp.dot(hot.astype(jnp.bfloat16), before, preferred_element_type=jnp.float32)
    rank = jnp.sum(hot * seen, axis=0, keepdims=True)
    block = (tdom % 2) * (doms // 2) + tdom // 2
    slot = block * per + rank.astype(jnp.int32)
    pick_ref[...] = (lax.broadcasted_iota(jnp.int32, (rows, rows), 0) == slot).astype(jnp.bfloat16)
    line = lax.broadcasted_iota(jnp.int32, (16, rows), 0)
    coded = jnp.where(line == 0, place // 64, jnp.where(line == 1, place % 64, 0))
    places = lax.dot_general(
        coded.astype(jnp.float32).astype(jnp.bfloat16),
        pick_ref[...],
        (((1,), (1,)), ((), ())),
        preferred_element_type=jnp.float32,
    ).astype(jnp.bfloat16)
    place_ref[...] = places
    part = rows // 2
    for core, out in enumerate((other_0, other_1)):
        out[part:, :part] = places[:, core * part : (core + 1) * part]
        out[part:, part:] = jnp.zeros((16, half - part), jnp.bfloat16)
        loads[core].wait()
        out[:part, :] = jnp.dot(
            pick_ref[pl.ds(core * part, part), :],
            enc[core].astype(jnp.bfloat16),
            preferred_element_type=jnp.float32,
        ).astype(jnp.bfloat16)


def by_dom(core, block, per):
    return pl.ds((2 * block + core) * per, per)


def pieces(own):
    at, start = [], 0
    for width in WIDTHS:
        at.append((2 * start + (0 if own else width), start, width))
        start += width
    return at


def mine_kernel(per, enc_ref, pick_ref, mine_ref, enc, sems):
    rows, width = enc_ref.shape
    half = width // 2
    z = lax.axis_index("grp")
    loads = []
    for core in range(2):
        start = pl.multiple_of(half_of(core == 1, z) * half, half)
        loads.append(pltpu.make_async_copy(enc_ref.at[:, pl.ds(start, half)], enc.at[core], sems.at[core]))
    for load in loads:
        load.start()
    for core in range(2):
        loads[core].wait()
        part = jnp.dot(
            pick_ref[pl.ds(core * rows // 2, rows // 2), :],
            enc[core].astype(jnp.bfloat16),
            preferred_element_type=jnp.float32,
        ).astype(jnp.bfloat16)
        for block in range(rows // 2 // per):
            mine_ref[by_dom(core, block, per), :] = part[block * per : (block + 1) * per, :]


def pack_kernel(per, place_ref, row_0, row_1, mine_ref, packed_ref, stage, sems):
    rows, half = stage.shape[0], row_0.shape[1]
    size = rows // 2
    copies = []

    def send(source, target):
        copies.append(pltpu.make_async_copy(source, target, sems.at[len(copies)]))
        copies[-1].start()

    for to, start, wide in pieces(True):
        send(mine_ref.at[:, pl.ds(start, wide)], packed_ref.at[:, pl.ds(to, wide)])
    line = lax.broadcasted_iota(jnp.int32, (16, 128), 0)
    lane = lax.broadcasted_iota(jnp.int32, (16, 128), 1)
    ids = []
    for core, row in enumerate((row_0, row_1)):
        total = jnp.zeros((size, 128), jnp.float32)
        for n, lines in enumerate((place_ref[:, core * size : (core + 1) * size], row[size:, :size])):
            spread = ((lane == line + 2 * n) & (line < 2)).astype(jnp.bfloat16)
            total += lax.dot_general(
                lines, spread, (((0,), (0,)), ((), ())), preferred_element_type=jnp.float32
            )
        ids.append(total.astype(jnp.bfloat16))
    chips = size // per
    for part in range(2):
        for block in range(part * chips // 2, (part + 1) * chips // 2):
            span = slice(block * per, (block + 1) * per)
            for core, row in enumerate((row_0, row_1)):
                at = by_dom(core, block, per)
                stage[at, :half] = row[span, :]
                stage[at, half:] = ids[core][span, :]
        some = pl.ds(part * size, size)
        for n, (to, start, wide) in enumerate(pieces(False)):
            wide += 128 if n == len(WIDTHS) - 1 else 0
            send(stage.at[some, pl.ds(start, wide)], packed_ref.at[some, pl.ds(to, wide)])
    for copy in copies:
        copy.wait()


def place_kernel(arrived_ref, token, *outs):
    rows = arrived_ref.shape[0]
    total = sum(out.shape[1] for out in outs)
    line = lax.broadcasted_iota(jnp.int32, (16, 128), 0)
    lane = lax.broadcasted_iota(jnp.int32, (16, 128), 1)
    spread = ((lane == line) & (line < 4)).astype(jnp.bfloat16)
    outs[0][rows:, :rows] = lax.dot_general(
        spread, arrived_ref[:, total:], (((1,), (1,)), ((), ())), preferred_element_type=jnp.float32
    ).astype(jnp.bfloat16)
    if outs[0].shape[1] > rows:
        outs[0][rows:, rows:] = jnp.zeros((16, outs[0].shape[1] - rows), jnp.bfloat16)
    start = 0
    for out in outs:
        out[:rows, :] = arrived_ref[:, start : start + out.shape[1]]
        start += out.shape[1]


def dense_kernel(list_ref, count_ref, weight_ref, dense_ref, scale_ref, token_ref, held, sems):
    blocks, _, size, _ = weight_ref.shape
    dom, z = lax.axis_index("dom"), lax.axis_index("grp")
    loads = [pltpu.make_async_copy(weight_ref.at[b], held.at[b], sems.at[b]) for b in range(blocks)]
    for load in loads:
        load.start()
    for b in range(blocks):
        dense_ref[pl.ds(b * size, size), :] = jnp.zeros((size, dense_ref.shape[1]), dense_ref.dtype)
    for b in range(blocks):
        span = pl.ds(b * size, size)
        loads[b].wait()

        def put(k, total):
            block = held[b, k]
            target = list_ref[b, k]
            column = steps_of(dom, z, target // blocks) * blocks + target % blocks
            start = pl.multiple_of(column * size, size)
            dense_ref[span, pl.ds(start, size)] = block
            return total + block.astype(jnp.float32)

        total = lax.fori_loop(0, count_ref[b], put, jnp.zeros((size, size), jnp.float32))
        degree = jnp.sum(total, axis=1, keepdims=True)
        scale_ref[span, :] = jnp.broadcast_to((1.0 - MIX) * lax.rsqrt(degree), (size, 128))
    token_ref[...] = jnp.zeros(token_ref.shape, token_ref.dtype)


def steps_of(dom, z, q):
    odd = dom % 2 == 1
    rx, fx = jnp.where(odd, 3, 1), jnp.where(odd, 1, 3)
    step = q ^ z
    return jnp.where(step == 0, 0, jnp.where(step == rx, 1, jnp.where(step == fx, 2, 3)))


def pick_kernel(rows_ref, *refs):
    pick_ref = refs[-1]
    nodes, size = pick_ref.shape[1:]
    dom, z = lax.axis_index("dom"), lax.axis_index("grp")
    coded = rows_ref[pl.ds(size, 16), :size].astype(jnp.float32).astype(jnp.int32)
    for k in range(2):
        p = coded[2 * k : 2 * k + 1, :] * 64 + coded[2 * k + 1 : 2 * k + 2, :]
        spot = steps_of(dom, z, p // size) * size + p % size
        for n in range(nodes // size):
            node = lax.broadcasted_iota(jnp.int32, (size, size), 0) + n * size
            pick_ref[k, pl.ds(n * size, size), :] = (node == spot).astype(jnp.bfloat16)


def part_kernel(pick_ref, near_ref, part_ref):
    size, width = pick_ref.shape[2], part_ref.shape[1]
    for n in range(part_ref.shape[0] // size):
        at = pl.ds(n * size, size)
        total = jnp.dot(pick_ref[0, at, :], near_ref[:size, :width], preferred_element_type=jnp.float32)
        total += jnp.dot(pick_ref[1, at, :], near_ref[:size, width:], preferred_element_type=jnp.float32)
        part_ref[at, :] = total.astype(jnp.bfloat16)


def first_kernel(dense_a, dense_b, scale_a, scale_b, pick_ref, part_ref, far_ref, base_ref, hidden_ref, panel):
    size = dense_a.shape[0]
    width = part_ref.shape[1]
    for n in range(panel.shape[0] // size):
        at = pl.ds(n * size, size)
        total = jnp.dot(pick_ref[0, at, :], far_ref[:size, :width], preferred_element_type=jnp.float32)
        total += jnp.dot(pick_ref[1, at, :], far_ref[:size, width:], preferred_element_type=jnp.float32)
        panel[at, :] = part_ref[at, :] + total.astype(jnp.bfloat16)
    for n, (dense, scale) in enumerate(((dense_a, scale_a), (dense_b, scale_b))):
        at = pl.ds(n * size, size)
        total = jnp.dot(dense[...], panel[...], preferred_element_type=jnp.float32)
        base = panel[at, :]
        base_ref[at, :] = base
        hidden_ref[at, :] = (MIX * base.astype(jnp.float32) + total * scale[:, 0:1]).astype(jnp.bfloat16)


def half_kernel(dense_a, dense_b, hidden_ref, total_ref):
    size = dense_a.shape[0]
    depth = hidden_ref.shape[0]
    for n, dense in enumerate((dense_a, dense_b)):
        total_ref[pl.ds(n * size, size), :] = jnp.dot(
            dense[:, :depth], hidden_ref[...], preferred_element_type=jnp.float32
        )


def finish(dense, scale, total_ref, hidden_ref, base_ref, at, out):
    depth = hidden_ref.shape[0]
    total = total_ref[at, :] + jnp.dot(dense[:, depth:], hidden_ref[...], preferred_element_type=jnp.float32)
    out[...] = (MIX * base_ref[at, :].astype(jnp.float32) + total * scale[:, 0:1]).astype(jnp.bfloat16)


def side_kernel(row, dense, scale, total_ref, hidden_ref, base_ref, after, out_ref):
    size = dense.shape[0]
    finish(dense, scale, total_ref, hidden_ref, base_ref, pl.ds(row * size, size), out_ref)


def move_halves(pieces, side, out_ref, sems):
    part = pieces[0].shape[1]
    copies = []
    for n, piece in enumerate(pieces):
        start = pl.multiple_of((side * len(pieces) + n) * part, part)
        copies.append(pltpu.make_async_copy(piece, out_ref.at[:, pl.ds(start, part)], sems.at[n]))
    for copy in copies:
        copy.start()
    for copy in copies:
        copy.wait()


def hold_kernel(sent_ref, after_0, after_1, back_ref):
    back_ref[...] = sent_ref[...]


def keep_kernel(keep_0, keep_1, out_ref, sems):
    dom, z = lax.axis_index("dom"), lax.axis_index("grp")
    move_halves((keep_0, keep_1), half_of(dom % 2 == 1, z), out_ref, sems)


def join_kernel(early_0, late_0, got_1, _, out_ref, sems):
    dom, z = lax.axis_index("dom"), lax.axis_index("grp")
    side = 1 - half_of(dom % 2 == 1, z)

    @pl.when(dom % 2 == 0)
    def _():
        move_halves((early_0, got_1), side, out_ref, sems)

    @pl.when(dom % 2 == 1)
    def _():
        move_halves((late_0, got_1), side, out_ref, sems)


def row_step(core):
    return 1 if core == 0 else 3


def shards(doms, depth, encoded, owner_of, nbr_blocks, nbr_count, edge_weights):
    f32, bf16, i32 = jnp.float32, jnp.bfloat16, jnp.int32
    rows, width = encoded.shape
    half = width // 2
    blocks, slots, size, _ = edge_weights.shape
    nodes = rows * depth
    devices = [(d, q) for d in range(doms) for q in range(depth)]
    row_pairs = [(d * depth + q, d * depth + (q ^ row_step(d % 2))) for d, q in devices]
    col_pairs = [(d * depth + q, d * depth + (q ^ row_step(1 - d % 2))) for d, q in devices]

    def to_row(a):
        return lax.ppermute(a, AXES, row_pairs)

    def to_col(a):
        return lax.ppermute(a, AXES, col_pairs)

    def to_row_of(core, a):
        return lax.ppermute(a, AXES, [(d * depth + q, d * depth + (q ^ row_step(core))) for d, q in devices])

    far_blocks, far_count = to_row(nbr_blocks), to_row(nbr_count)

    def dense_of(lists, count, weights, limit, work=0):
        return kernel_call(
            dense_kernel,
            (
                jax.ShapeDtypeStruct((blocks * size, nodes), bf16),
                jax.ShapeDtypeStruct((blocks * size, 128), f32),
                jax.ShapeDtypeStruct((8, 128), f32),
            ),
            [SMEM, SMEM, ANY],
            work,
            8 << 20,
            scratch=[pltpu.VMEM(weights.shape, bf16), pltpu.SemaphoreType.DMA((blocks,))],
            limit=limit,
        )(lists, count, weights)

    held = pltpu.VMEM((2, rows, half), f32)
    other = jax.ShapeDtypeStruct((rows // 2 + 16, half), bf16)
    other_0, other_1, pick, place = kernel_call(
        functools.partial(sort_kernel, doms),
        (other, other, jax.ShapeDtypeStruct((rows, rows), bf16), jax.ShapeDtypeStruct((16, rows), bf16)),
        [ANY, ANY],
        2 * rows * rows * half,
        4 << 20,
        scratch=[held, pltpu.VMEM((1, rows), i32), pltpu.SemaphoreType.DMA((3,))],
        limit=58,
    )(owner_of.reshape(1, rows), encoded)
    row_0, row_1 = to_row_of(0, other_0), to_row_of(1, other_1)
    per = rows // doms
    mine = kernel_call(
        functools.partial(mine_kernel, per),
        jax.ShapeDtypeStruct((rows, half), bf16),
        [ANY, VMEM],
        2 * rows * rows * half,
        4 << 20,
        scratch=[held, pltpu.SemaphoreType.DMA((2,))],
        limit=50,
    )(encoded, pick)
    sent_weights, mine, far_blocks, far_count = lax.optimization_barrier(
        (edge_weights, mine, far_blocks, far_count)
    )
    far_weights = to_row(sent_weights)
    packed = pl.pallas_call(
        functools.partial(pack_kernel, per),
        out_shape=jax.ShapeDtypeStruct((rows, width + 128), bf16),
        in_specs=[VMEM] * 3 + [ANY],
        out_specs=ANY,
        scratch_shapes=[pltpu.VMEM((rows, half + 128), bf16), pltpu.SemaphoreType.DMA((3 * len(WIDTHS),))],
        compiler_params=pltpu.CompilerParams(vmem_limit_bytes=10 << 20),
        cost_estimate=pl.CostEstimate(flops=1 << 20, bytes_accessed=2 << 20, transcendentals=0),
    )(place, row_0, row_1, mine)

    packed = lax.all_to_all(packed, "dom", 0, 0, tiled=True)
    dense_a, scale_a, token_a = dense_of(nbr_blocks, nbr_count, edge_weights, 50, 40_000_000_000)
    near_rows = kernel_call(
        place_kernel,
        tuple(jax.ShapeDtypeStruct((rows + (16 if c == 0 else 0), 2 * w), bf16) for c, w in enumerate(WIDTHS)),
        [VMEM, ANY],
        1 << 20,
        1 << 20,
    )(packed, token_a)
    far_rows = [to_col(a) for a in near_rows]

    dense_b, scale_b, token_b = dense_of(far_blocks, far_count, far_weights, 10)

    def picks_of(first_rows, *after):
        return kernel_call(
            pick_kernel,
            jax.ShapeDtypeStruct((2, nodes, rows), bf16),
            [VMEM] + [ANY] * len(after),
            1 << 20,
            4 << 20,
        )(first_rows, *after)

    near_picks = picks_of(near_rows[0], token_a)
    placed = [
        kernel_call(
            part_kernel,
            jax.ShapeDtypeStruct((nodes, part), bf16),
            [VMEM] * 2,
            4 * nodes * rows * part,
            4 << 20,
        )(near_picks, near_rows[c])
        for c, part in enumerate(WIDTHS)
    ]
    far_picks = picks_of(far_rows[0], token_b, *placed)

    mine_n = 2 * rows
    steps = []
    for c, part in enumerate(WIDTHS):
        base, hidden = kernel_call(
            first_kernel,
            (jax.ShapeDtypeStruct((mine_n, part), bf16), jax.ShapeDtypeStruct((mine_n, part), bf16)),
            [VMEM] * 7,
            4 * nodes * rows * part + 2 * mine_n * nodes * part,
            4 << 20,
            scratch=[pltpu.VMEM((nodes, part), bf16)],
        )(dense_a, dense_b, scale_a, scale_b, far_picks, placed[c], far_rows[c])
        far_hidden = to_col(hidden)
        running = kernel_call(
            half_kernel,
            jax.ShapeDtypeStruct((mine_n, part), f32),
            [VMEM] * 3,
            2 * mine_n * mine_n * part,
            4 << 20,
        )(dense_a, dense_b, hidden)
        steps.append((running, far_hidden, base))

    part = WIDTHS[0]
    out_shape = jax.ShapeDtypeStruct((rows, part), bf16)
    work = 2 * rows * mine_n * part
    def side(row, step, after):
        dense, scale = ((dense_a, scale_a), (dense_b, scale_b))[row]
        return kernel_call(functools.partial(side_kernel, row), out_shape, [VMEM] * 5 + [ANY], work, 2 << 20)(
            dense, scale, *steps[step], after
        )

    send_0 = side(1, 0, steps[1][0])
    keep_0 = side(0, 0, send_0)
    send_1 = side(1, 1, keep_0)
    keep_1 = side(0, 1, send_1)
    kept, sent = [keep_0, keep_1], [send_0, send_1]

    def to_row_on(core, a):
        return lax.ppermute(a, AXES, [(p, q) for p, q in row_pairs if p // depth % 2 == core])

    early_0 = to_row_on(0, sent[0])
    got_1 = to_row(sent[1])
    whole = jax.ShapeDtypeStruct((rows, width), bf16)
    held_back = kernel_call(hold_kernel, out_shape, [VMEM, ANY, ANY], 0, 1 << 19)(sent[0], early_0, sent[1])
    late_0 = to_row_on(1, held_back)
    half_done = pl.pallas_call(
        keep_kernel,
        out_shape=whole,
        in_specs=[VMEM] * 2,
        out_specs=ANY,
        scratch_shapes=[pltpu.SemaphoreType.DMA((2,))],
        compiler_params=pltpu.CompilerParams(vmem_limit_bytes=8 << 20),
    )(*kept)
    return pl.pallas_call(
        join_kernel,
        out_shape=whole,
        in_specs=[VMEM] * 3 + [ANY],
        out_specs=ANY,
        input_output_aliases={3: 0},
        scratch_shapes=[pltpu.SemaphoreType.DMA((2,))],
        compiler_params=pltpu.CompilerParams(vmem_limit_bytes=8 << 20),
    )(early_0, late_0, got_1, half_done)


def solution(mesh):
    return jax.shard_map(
        functools.partial(shards, mesh.shape["dom"], mesh.shape["grp"]),
        mesh=mesh,
        in_specs=(P(AXES, None), P(AXES), P(AXES, None), P(AXES), P(AXES, None, None, None)),
        out_specs=P(AXES, None),
        check_vma=False,
    )
```

```python
import functools

import jax
import jax.numpy as jnp
from jax import lax
from jax.experimental import pallas as pl
from jax.experimental.pallas import tpu as pltpu
from jax.sharding import PartitionSpec as P

AXES = ("dom", "grp")
MIX = 0.3
WIDTHS = (256, 256)
VMEM = pl.BlockSpec(memory_space=pltpu.VMEM)
SMEM = pl.BlockSpec(memory_space=pltpu.SMEM)
ANY = pl.BlockSpec(memory_space=pl.ANY)


def kernel_call(body, out_shape, in_specs, flops, moved, scratch=(), limit=10):
    outs = out_shape if isinstance(out_shape, (tuple, list)) else (out_shape,)
    specs = tuple(VMEM for _ in outs)
    return pl.pallas_call(
        body,
        out_shape=out_shape,
        in_specs=in_specs,
        out_specs=specs if isinstance(out_shape, (tuple, list)) else specs[0],
        scratch_shapes=scratch,
        compiler_params=pltpu.CompilerParams(vmem_limit_bytes=limit * 1024 * 1024),
        cost_estimate=pl.CostEstimate(flops=flops, bytes_accessed=moved, transcendentals=0),
    )


def half_of(core_is_odd, z):
    return jnp.where(core_is_odd, z // 2, ((z + 1) // 2) % 2)


def sort_kernel(
    doms, owner_hbm, enc_ref, out_0, out_1, pick_hbm, place_ref, enc, owner_ref, other_0, other_1, pick_ref, sems, out_sems
):
    rows, width = enc_ref.shape
    half = width // 2
    z = lax.axis_index("grp")
    first = pltpu.make_async_copy(owner_hbm, owner_ref, sems.at[2])
    first.start()
    loads = []
    for core in range(2):
        start = pl.multiple_of((1 - half_of(core == 1, z)) * half, half)
        loads.append(pltpu.make_async_copy(enc_ref.at[:, pl.ds(start, half)], enc.at[core], sems.at[core]))
    for load in loads:
        load.start()
    per = rows // doms
    before = (
        lax.broadcasted_iota(jnp.int32, (rows, rows), 0)
        < lax.broadcasted_iota(jnp.int32, (rows, rows), 1)
    ).astype(jnp.bfloat16)
    first.wait()
    owner = owner_ref[...]
    group_nodes = rows * 4
    tdom = owner // group_nodes
    place = owner - tdom * group_nodes
    hot = (lax.broadcasted_iota(jnp.int32, (doms, rows), 0) == tdom).astype(jnp.float32)
    seen = jnp.dot(hot.astype(jnp.bfloat16), before, preferred_element_type=jnp.float32)
    rank = jnp.sum(hot * seen, axis=0, keepdims=True)
    block = (tdom % 2) * (doms // 2) + tdom // 2
    slot = block * per + rank.astype(jnp.int32)
    pick_ref[...] = (lax.broadcasted_iota(jnp.int32, (rows, rows), 0) == slot).astype(jnp.bfloat16)
    copies = [pltpu.make_async_copy(pick_ref, pick_hbm, out_sems.at[2])]
    copies[0].start()
    line = lax.broadcasted_iota(jnp.int32, (16, rows), 0)
    coded = jnp.where(line == 0, place // 64, jnp.where(line == 1, place % 64, 0))
    places = lax.dot_general(
        coded.astype(jnp.float32).astype(jnp.bfloat16),
        pick_ref[...],
        (((1,), (1,)), ((), ())),
        preferred_element_type=jnp.float32,
    ).astype(jnp.bfloat16)
    place_ref[...] = places
    part = rows // 2
    for core, out in enumerate((other_0, other_1)):
        out[part:, :part] = places[:, core * part : (core + 1) * part]
        out[part:, part:] = jnp.zeros((16, half - part), jnp.bfloat16)
        loads[core].wait()
        out[:part, :] = jnp.dot(
            pick_ref[pl.ds(core * part, part), :],
            enc[core].astype(jnp.bfloat16),
            preferred_element_type=jnp.float32,
        ).astype(jnp.bfloat16)
        copies.append(pltpu.make_async_copy(out, (out_0, out_1)[core], out_sems.at[core]))
        copies[-1].start()
    for copy in copies:
        copy.wait()


def by_dom(core, block, per):
    return pl.ds((2 * block + core) * per, per)


def pieces(own):
    at, start = [], 0
    for width in WIDTHS:
        at.append((2 * start + (0 if own else width), start, width))
        start += width
    return at


def mine_kernel(per, enc_ref, pick_ref, mine_ref, enc, sems):
    rows, width = enc_ref.shape
    half = width // 2
    z = lax.axis_index("grp")
    loads = []
    for core in range(2):
        start = pl.multiple_of(half_of(core == 1, z) * half, half)
        loads.append(pltpu.make_async_copy(enc_ref.at[:, pl.ds(start, half)], enc.at[core], sems.at[core]))
    for load in loads:
        load.start()
    for core in range(2):
        loads[core].wait()
        part = jnp.dot(
            pick_ref[pl.ds(core * rows // 2, rows // 2), :],
            enc[core].astype(jnp.bfloat16),
            preferred_element_type=jnp.float32,
        ).astype(jnp.bfloat16)
        for block in range(rows // 2 // per):
            mine_ref[by_dom(core, block, per), :] = part[block * per : (block + 1) * per, :]


def pack_kernel(per, place_ref, row_0, row_1, mine_ref, packed_ref, stage, sems):
    rows, half = stage.shape[0], row_0.shape[1]
    size = rows // 2
    copies = []

    def send(source, target):
        copies.append(pltpu.make_async_copy(source, target, sems.at[len(copies)]))
        copies[-1].start()

    for to, start, wide in pieces(True):
        send(mine_ref.at[:, pl.ds(start, wide)], packed_ref.at[:, pl.ds(to, wide)])
    line = lax.broadcasted_iota(jnp.int32, (16, 128), 0)
    lane = lax.broadcasted_iota(jnp.int32, (16, 128), 1)
    ids = []
    for core, row in enumerate((row_0, row_1)):
        total = jnp.zeros((size, 128), jnp.float32)
        for n, lines in enumerate((place_ref[:, core * size : (core + 1) * size], row[size:, :size])):
            spread = ((lane == line + 2 * n) & (line < 2)).astype(jnp.bfloat16)
            total += lax.dot_general(
                lines, spread, (((0,), (0,)), ((), ())), preferred_element_type=jnp.float32
            )
        ids.append(total.astype(jnp.bfloat16))
    chips = size // per
    for part in range(2):
        for block in range(part * chips // 2, (part + 1) * chips // 2):
            span = slice(block * per, (block + 1) * per)
            for core, row in enumerate((row_0, row_1)):
                at = by_dom(core, block, per)
                stage[at, :half] = row[span, :]
                stage[at, half:] = ids[core][span, :]
        some = pl.ds(part * size, size)
        for n, (to, start, wide) in enumerate(pieces(False)):
            wide += 128 if n == len(WIDTHS) - 1 else 0
            send(stage.at[some, pl.ds(start, wide)], packed_ref.at[some, pl.ds(to, wide)])
    for copy in copies:
        copy.wait()


def place_kernel(arrived_ref, token, *outs):
    rows = arrived_ref.shape[0]
    total = sum(out.shape[1] for out in outs)
    line = lax.broadcasted_iota(jnp.int32, (16, 128), 0)
    lane = lax.broadcasted_iota(jnp.int32, (16, 128), 1)
    spread = ((lane == line) & (line < 4)).astype(jnp.bfloat16)
    outs[0][rows:, :rows] = lax.dot_general(
        spread, arrived_ref[:, total:], (((1,), (1,)), ((), ())), preferred_element_type=jnp.float32
    ).astype(jnp.bfloat16)
    if outs[0].shape[1] > rows:
        outs[0][rows:, rows:] = jnp.zeros((16, outs[0].shape[1] - rows), jnp.bfloat16)
    start = 0
    for out in outs:
        out[:rows, :] = arrived_ref[:, start : start + out.shape[1]]
        start += out.shape[1]


def dense_kernel(list_ref, count_ref, weight_ref, dense_ref, scale_ref, token_ref, held, sems):
    blocks, _, size, _ = weight_ref.shape
    dom, z = lax.axis_index("dom"), lax.axis_index("grp")
    loads = [pltpu.make_async_copy(weight_ref.at[b], held.at[b], sems.at[b]) for b in range(blocks)]
    for load in loads:
        load.start()
    for b in range(blocks):
        dense_ref[pl.ds(b * size, size), :] = jnp.zeros((size, dense_ref.shape[1]), dense_ref.dtype)
    for b in range(blocks):
        span = pl.ds(b * size, size)
        loads[b].wait()

        def put(k, total):
            block = held[b, k]
            target = list_ref[b, k]
            column = steps_of(dom, z, target // blocks) * blocks + target % blocks
            start = pl.multiple_of(column * size, size)
            dense_ref[span, pl.ds(start, size)] = block
            return total + block.astype(jnp.float32)

        total = lax.fori_loop(0, count_ref[b], put, jnp.zeros((size, size), jnp.float32))
        degree = jnp.sum(total, axis=1, keepdims=True)
        scale_ref[span, :] = jnp.broadcast_to((1.0 - MIX) * lax.rsqrt(degree), (size, 128))
    token_ref[...] = jnp.zeros(token_ref.shape, token_ref.dtype)


def steps_of(dom, z, q):
    odd = dom % 2 == 1
    rx, fx = jnp.where(odd, 3, 1), jnp.where(odd, 1, 3)
    step = q ^ z
    return jnp.where(step == 0, 0, jnp.where(step == rx, 1, jnp.where(step == fx, 2, 3)))


def pick_kernel(rows_ref, *refs):
    pick_ref = refs[-1]
    nodes, size = pick_ref.shape[1:]
    dom, z = lax.axis_index("dom"), lax.axis_index("grp")
    coded = rows_ref[pl.ds(size, 16), :size].astype(jnp.float32).astype(jnp.int32)
    for k in range(2):
        p = coded[2 * k : 2 * k + 1, :] * 64 + coded[2 * k + 1 : 2 * k + 2, :]
        spot = steps_of(dom, z, p // size) * size + p % size
        for n in range(nodes // size):
            node = lax.broadcasted_iota(jnp.int32, (size, size), 0) + n * size
            pick_ref[k, pl.ds(n * size, size), :] = (node == spot).astype(jnp.bfloat16)


def part_kernel(pick_ref, near_ref, part_ref):
    size, width = pick_ref.shape[2], part_ref.shape[1]
    for n in range(part_ref.shape[0] // size):
        at = pl.ds(n * size, size)
        total = jnp.dot(pick_ref[0, at, :], near_ref[:size, :width], preferred_element_type=jnp.float32)
        total += jnp.dot(pick_ref[1, at, :], near_ref[:size, width:], preferred_element_type=jnp.float32)
        part_ref[at, :] = total.astype(jnp.bfloat16)


def first_kernel(dense_a, dense_b, scale_a, scale_b, pick_ref, part_ref, far_ref, base_ref, hidden_ref, panel):
    size = dense_a.shape[0]
    width = part_ref.shape[1]
    for n in range(panel.shape[0] // size):
        at = pl.ds(n * size, size)
        total = jnp.dot(pick_ref[0, at, :], far_ref[:size, :width], preferred_element_type=jnp.float32)
        total += jnp.dot(pick_ref[1, at, :], far_ref[:size, width:], preferred_element_type=jnp.float32)
        panel[at, :] = part_ref[at, :] + total.astype(jnp.bfloat16)
    for n, (dense, scale) in enumerate(((dense_a, scale_a), (dense_b, scale_b))):
        at = pl.ds(n * size, size)
        total = jnp.dot(dense[...], panel[...], preferred_element_type=jnp.float32)
        base = panel[at, :]
        base_ref[at, :] = base
        hidden_ref[at, :] = (MIX * base.astype(jnp.float32) + total * scale[:, 0:1]).astype(jnp.bfloat16)


def half_kernel(dense_a, dense_b, hidden_ref, total_ref):
    size = dense_a.shape[0]
    depth = hidden_ref.shape[0]
    for n, dense in enumerate((dense_a, dense_b)):
        total_ref[pl.ds(n * size, size), :] = jnp.dot(
            dense[:, :depth], hidden_ref[...], preferred_element_type=jnp.float32
        )


def finish(dense, scale, total_ref, hidden_ref, base_ref, at, out):
    depth = hidden_ref.shape[0]
    total = total_ref[at, :] + jnp.dot(dense[:, depth:], hidden_ref[...], preferred_element_type=jnp.float32)
    out[...] = (MIX * base_ref[at, :].astype(jnp.float32) + total * scale[:, 0:1]).astype(jnp.bfloat16)


def side_kernel(row, dense, scale, total_ref, hidden_ref, base_ref, after, out_ref):
    size = dense.shape[0]
    finish(dense, scale, total_ref, hidden_ref, base_ref, pl.ds(row * size, size), out_ref)


def move_halves(pieces, side, out_ref, sems):
    part = pieces[0].shape[1]
    copies = []
    for n, piece in enumerate(pieces):
        start = pl.multiple_of((side * len(pieces) + n) * part, part)
        copies.append(pltpu.make_async_copy(piece, out_ref.at[:, pl.ds(start, part)], sems.at[n]))
    for copy in copies:
        copy.start()
    for copy in copies:
        copy.wait()


def hold_kernel(sent_ref, after_0, after_1, back_ref):
    back_ref[...] = sent_ref[...]


def keep_kernel(keep_0, keep_1, out_ref, sems):
    dom, z = lax.axis_index("dom"), lax.axis_index("grp")
    move_halves((keep_0, keep_1), half_of(dom % 2 == 1, z), out_ref, sems)


def join_kernel(early_0, late_0, got_1, _, out_ref, sems):
    dom, z = lax.axis_index("dom"), lax.axis_index("grp")
    side = 1 - half_of(dom % 2 == 1, z)

    @pl.when(dom % 2 == 0)
    def _():
        move_halves((early_0, got_1), side, out_ref, sems)

    @pl.when(dom % 2 == 1)
    def _():
        move_halves((late_0, got_1), side, out_ref, sems)


def row_step(core):
    return 1 if core == 0 else 3


def shards(doms, depth, encoded, owner_of, nbr_blocks, nbr_count, edge_weights):
    f32, bf16, i32 = jnp.float32, jnp.bfloat16, jnp.int32
    rows, width = encoded.shape
    half = width // 2
    blocks, slots, size, _ = edge_weights.shape
    nodes = rows * depth
    devices = [(d, q) for d in range(doms) for q in range(depth)]
    row_pairs = [(d * depth + q, d * depth + (q ^ row_step(d % 2))) for d, q in devices]
    col_pairs = [(d * depth + q, d * depth + (q ^ row_step(1 - d % 2))) for d, q in devices]

    def to_row(a):
        return lax.ppermute(a, AXES, row_pairs)

    def to_col(a):
        return lax.ppermute(a, AXES, col_pairs)

    def to_row_of(core, a):
        return lax.ppermute(a, AXES, [(d * depth + q, d * depth + (q ^ row_step(core))) for d, q in devices])

    far_blocks, far_count = to_row(nbr_blocks), to_row(nbr_count)

    def dense_of(lists, count, weights, limit, work=0):
        return kernel_call(
            dense_kernel,
            (
                jax.ShapeDtypeStruct((blocks * size, nodes), bf16),
                jax.ShapeDtypeStruct((blocks * size, 128), f32),
                jax.ShapeDtypeStruct((8, 128), f32),
            ),
            [SMEM, SMEM, ANY],
            work,
            8 << 20,
            scratch=[pltpu.VMEM(weights.shape, bf16), pltpu.SemaphoreType.DMA((blocks,))],
            limit=limit,
        )(lists, count, weights)

    held = pltpu.VMEM((2, rows, half), f32)
    other = jax.ShapeDtypeStruct((rows // 2 + 16, half), bf16)
    other_0, other_1, pick, place = pl.pallas_call(
        functools.partial(sort_kernel, doms),
        out_shape=(
            other,
            other,
            jax.ShapeDtypeStruct((rows, rows), bf16),
            jax.ShapeDtypeStruct((16, rows), bf16),
        ),
        in_specs=[ANY, ANY],
        out_specs=(ANY, ANY, ANY, VMEM),
        scratch_shapes=[
            held,
            pltpu.VMEM((1, rows), i32),
            pltpu.VMEM(other.shape, bf16),
            pltpu.VMEM(other.shape, bf16),
            pltpu.VMEM((rows, rows), bf16),
            pltpu.SemaphoreType.DMA((3,)),
            pltpu.SemaphoreType.DMA((3,)),
        ],
        compiler_params=pltpu.CompilerParams(vmem_limit_bytes=58 << 20),
        cost_estimate=pl.CostEstimate(flops=2 * rows * rows * half, bytes_accessed=4 << 20, transcendentals=0),
    )(owner_of.reshape(1, rows), encoded)
    row_0, row_1 = to_row_of(0, other_0), to_row_of(1, other_1)
    per = rows // doms
    mine = kernel_call(
        functools.partial(mine_kernel, per),
        jax.ShapeDtypeStruct((rows, half), bf16),
        [ANY, VMEM],
        2 * rows * rows * half,
        4 << 20,
        scratch=[held, pltpu.SemaphoreType.DMA((2,))],
        limit=50,
    )(encoded, pick)
    sent_weights, mine, far_blocks, far_count = lax.optimization_barrier(
        (edge_weights, mine, far_blocks, far_count)
    )
    far_weights = to_row(sent_weights)
    packed = pl.pallas_call(
        functools.partial(pack_kernel, per),
        out_shape=jax.ShapeDtypeStruct((rows, width + 128), bf16),
        in_specs=[VMEM] * 3 + [ANY],
        out_specs=ANY,
        scratch_shapes=[pltpu.VMEM((rows, half + 128), bf16), pltpu.SemaphoreType.DMA((3 * len(WIDTHS),))],
        compiler_params=pltpu.CompilerParams(vmem_limit_bytes=10 << 20),
        cost_estimate=pl.CostEstimate(flops=1 << 20, bytes_accessed=2 << 20, transcendentals=0),
    )(place, row_0, row_1, mine)

    packed = lax.all_to_all(packed, "dom", 0, 0, tiled=True)
    dense_a, scale_a, token_a = dense_of(nbr_blocks, nbr_count, edge_weights, 50, 40_000_000_000)
    near_rows = kernel_call(
        place_kernel,
        tuple(jax.ShapeDtypeStruct((rows + (16 if c == 0 else 0), 2 * w), bf16) for c, w in enumerate(WIDTHS)),
        [VMEM, ANY],
        1 << 20,
        1 << 20,
    )(packed, token_a)
    far_rows = [to_col(a) for a in near_rows]

    dense_b, scale_b, token_b = dense_of(far_blocks, far_count, far_weights, 10)

    def picks_of(first_rows, *after):
        return kernel_call(
            pick_kernel,
            jax.ShapeDtypeStruct((2, nodes, rows), bf16),
            [VMEM] + [ANY] * len(after),
            1 << 20,
            4 << 20,
        )(first_rows, *after)

    near_picks = picks_of(near_rows[0], token_a)
    placed = [
        kernel_call(
            part_kernel,
            jax.ShapeDtypeStruct((nodes, part), bf16),
            [VMEM] * 2,
            4 * nodes * rows * part,
            4 << 20,
        )(near_picks, near_rows[c])
        for c, part in enumerate(WIDTHS)
    ]
    far_picks = picks_of(far_rows[0], token_b, *placed)

    mine_n = 2 * rows
    steps = []
    for c, part in enumerate(WIDTHS):
        base, hidden = kernel_call(
            first_kernel,
            (jax.ShapeDtypeStruct((mine_n, part), bf16), jax.ShapeDtypeStruct((mine_n, part), bf16)),
            [VMEM] * 7,
            4 * nodes * rows * part + 2 * mine_n * nodes * part,
            4 << 20,
            scratch=[pltpu.VMEM((nodes, part), bf16)],
        )(dense_a, dense_b, scale_a, scale_b, far_picks, placed[c], far_rows[c])
        far_hidden = to_col(hidden)
        running = kernel_call(
            half_kernel,
            jax.ShapeDtypeStruct((mine_n, part), f32),
            [VMEM] * 3,
            2 * mine_n * mine_n * part,
            4 << 20,
        )(dense_a, dense_b, hidden)
        steps.append((running, far_hidden, base))

    part = WIDTHS[0]
    out_shape = jax.ShapeDtypeStruct((rows, part), bf16)
    work = 2 * rows * mine_n * part
    def side(row, step, after):
        dense, scale = ((dense_a, scale_a), (dense_b, scale_b))[row]
        return kernel_call(functools.partial(side_kernel, row), out_shape, [VMEM] * 5 + [ANY], work, 2 << 20)(
            dense, scale, *steps[step], after
        )

    send_0 = side(1, 0, steps[1][0])
    keep_0 = side(0, 0, send_0)
    send_1 = side(1, 1, keep_0)
    keep_1 = side(0, 1, send_1)
    kept, sent = [keep_0, keep_1], [send_0, send_1]

    def to_row_on(core, a):
        return lax.ppermute(a, AXES, [(p, q) for p, q in row_pairs if p // depth % 2 == core])

    early_0 = to_row_on(0, sent[0])
    got_1 = to_row(sent[1])
    whole = jax.ShapeDtypeStruct((rows, width), bf16)
    held_back = kernel_call(hold_kernel, out_shape, [VMEM, ANY, ANY], 0, 1 << 19)(sent[0], early_0, sent[1])
    late_0 = to_row_on(1, held_back)
    half_done = pl.pallas_call(
        keep_kernel,
        out_shape=whole,
        in_specs=[VMEM] * 2,
        out_specs=ANY,
        scratch_shapes=[pltpu.SemaphoreType.DMA((2,))],
        compiler_params=pltpu.CompilerParams(vmem_limit_bytes=8 << 20),
    )(*kept)
    return pl.pallas_call(
        join_kernel,
        out_shape=whole,
        in_specs=[VMEM] * 3 + [ANY],
        out_specs=ANY,
        input_output_aliases={3: 0},
        scratch_shapes=[pltpu.SemaphoreType.DMA((2,))],
        compiler_params=pltpu.CompilerParams(vmem_limit_bytes=8 << 20),
    )(early_0, late_0, got_1, half_done)


def solution(mesh):
    return jax.shard_map(
        functools.partial(shards, mesh.shape["dom"], mesh.shape["grp"]),
        mesh=mesh,
        in_specs=(P(AXES, None), P(AXES), P(AXES, None), P(AXES), P(AXES, None, None, None)),
        out_specs=P(AXES, None),
        check_vma=False,
    )
```

```python
import functools

import jax
import jax.numpy as jnp
from jax import lax
from jax.experimental import pallas as pl
from jax.experimental.pallas import tpu as pltpu
from jax.sharding import PartitionSpec as P

AXES = ("dom", "grp")
MIX = 0.3
WIDTHS = (256, 256)
VMEM = pl.BlockSpec(memory_space=pltpu.VMEM)
SMEM = pl.BlockSpec(memory_space=pltpu.SMEM)
ANY = pl.BlockSpec(memory_space=pl.ANY)


def kernel_call(body, out_shape, in_specs, flops, moved, scratch=(), limit=10):
    outs = out_shape if isinstance(out_shape, (tuple, list)) else (out_shape,)
    specs = tuple(VMEM for _ in outs)
    return pl.pallas_call(
        body,
        out_shape=out_shape,
        in_specs=in_specs,
        out_specs=specs if isinstance(out_shape, (tuple, list)) else specs[0],
        scratch_shapes=scratch,
        compiler_params=pltpu.CompilerParams(vmem_limit_bytes=limit * 1024 * 1024),
        cost_estimate=pl.CostEstimate(flops=flops, bytes_accessed=moved, transcendentals=0),
    )


def half_of(core_is_odd, z):
    return jnp.where(core_is_odd, z // 2, ((z + 1) // 2) % 2)


def sort_kernel(doms, owner_hbm, enc_ref, other_0, other_1, pick_ref, place_ref, enc, owner_ref, sems):
    rows, width = enc_ref.shape
    half = width // 2
    z = lax.axis_index("grp")
    first = pltpu.make_async_copy(owner_hbm, owner_ref, sems.at[2])
    first.start()
    loads = []
    for core in range(2):
        start = pl.multiple_of((1 - half_of(core == 1, z)) * half, half)
        loads.append(pltpu.make_async_copy(enc_ref.at[:, pl.ds(start, half)], enc.at[core], sems.at[core]))
    for load in loads:
        load.start()
    per = rows // doms
    before = (
        lax.broadcasted_iota(jnp.int32, (rows, rows), 0)
        < lax.broadcasted_iota(jnp.int32, (rows, rows), 1)
    ).astype(jnp.bfloat16)
    first.wait()
    owner = owner_ref[...]
    group_nodes = rows * 4
    tdom = owner // group_nodes
    place = owner - tdom * group_nodes
    hot = (lax.broadcasted_iota(jnp.int32, (doms, rows), 0) == tdom).astype(jnp.float32)
    seen = jnp.dot(hot.astype(jnp.bfloat16), before, preferred_element_type=jnp.float32)
    rank = jnp.sum(hot * seen, axis=0, keepdims=True)
    block = (tdom % 2) * (doms // 2) + tdom // 2
    slot = block * per + rank.astype(jnp.int32)
    pick_ref[...] = (lax.broadcasted_iota(jnp.int32, (rows, rows), 0) == slot).astype(jnp.bfloat16)
    line = lax.broadcasted_iota(jnp.int32, (16, rows), 0)
    coded = jnp.where(line == 0, place // 64, jnp.where(line == 1, place % 64, 0))
    places = lax.dot_general(
        coded.astype(jnp.float32).astype(jnp.bfloat16),
        pick_ref[...],
        (((1,), (1,)), ((), ())),
        preferred_element_type=jnp.float32,
    ).astype(jnp.bfloat16)
    place_ref[...] = places
    part = rows // 2
    for core, out in enumerate((other_0, other_1)):
        out[part:, :part] = places[:, core * part : (core + 1) * part]
        out[part:, part:] = jnp.zeros((16, half - part), jnp.bfloat16)
        loads[core].wait()
        out[:part, :] = jnp.dot(
            pick_ref[pl.ds(core * part, part), :],
            enc[core].astype(jnp.bfloat16),
            preferred_element_type=jnp.float32,
        ).astype(jnp.bfloat16)


def by_dom(core, block, per):
    return pl.ds((2 * block + core) * per, per)


def pieces(own):
    at, start = [], 0
    for width in WIDTHS:
        at.append((2 * start + (0 if own else width), start, width))
        start += width
    return at


def mine_kernel(per, enc_ref, pick_ref, mine_ref, enc, sems):
    rows, width = enc_ref.shape
    half = width // 2
    z = lax.axis_index("grp")
    loads = []
    for core in range(2):
        start = pl.multiple_of(half_of(core == 1, z) * half, half)
        loads.append(pltpu.make_async_copy(enc_ref.at[:, pl.ds(start, half)], enc.at[core], sems.at[core]))
    for load in loads:
        load.start()
    for core in range(2):
        loads[core].wait()
        part = jnp.dot(
            pick_ref[pl.ds(core * rows // 2, rows // 2), :],
            enc[core].astype(jnp.bfloat16),
            preferred_element_type=jnp.float32,
        ).astype(jnp.bfloat16)
        for block in range(rows // 2 // per):
            mine_ref[by_dom(core, block, per), :] = part[block * per : (block + 1) * per, :]


def pack_kernel(per, place_ref, row_0, row_1, mine_ref, packed_ref, stage, sems):
    rows, half = stage.shape[0], row_0.shape[1]
    size = rows // 2
    copies = []

    def send(source, target):
        copies.append(pltpu.make_async_copy(source, target, sems.at[len(copies)]))
        copies[-1].start()

    for to, start, wide in pieces(True):
        send(mine_ref.at[:, pl.ds(start, wide)], packed_ref.at[:, pl.ds(to, wide)])
    line = lax.broadcasted_iota(jnp.int32, (16, 128), 0)
    lane = lax.broadcasted_iota(jnp.int32, (16, 128), 1)
    ids = []
    for core, row in enumerate((row_0, row_1)):
        total = jnp.zeros((size, 128), jnp.float32)
        for n, lines in enumerate((place_ref[:, core * size : (core + 1) * size], row[size:, :size])):
            spread = ((lane == line + 2 * n) & (line < 2)).astype(jnp.bfloat16)
            total += lax.dot_general(
                lines, spread, (((0,), (0,)), ((), ())), preferred_element_type=jnp.float32
            )
        ids.append(total.astype(jnp.bfloat16))
    chips = size // per
    for part in range(2):
        for block in range(part * chips // 2, (part + 1) * chips // 2):
            span = slice(block * per, (block + 1) * per)
            for core, row in enumerate((row_0, row_1)):
                at = by_dom(core, block, per)
                stage[at, :half] = row[span, :]
                stage[at, half:] = ids[core][span, :]
        some = pl.ds(part * size, size)
        for n, (to, start, wide) in enumerate(pieces(False)):
            wide += 128 if n == len(WIDTHS) - 1 else 0
            send(stage.at[some, pl.ds(start, wide)], packed_ref.at[some, pl.ds(to, wide)])
    for copy in copies:
        copy.wait()


def place_kernel(arrived_ref, token, *outs):
    rows = arrived_ref.shape[0]
    total = sum(out.shape[1] for out in outs)
    line = lax.broadcasted_iota(jnp.int32, (16, 128), 0)
    lane = lax.broadcasted_iota(jnp.int32, (16, 128), 1)
    spread = ((lane == line) & (line < 4)).astype(jnp.bfloat16)
    outs[0][rows:, :rows] = lax.dot_general(
        spread, arrived_ref[:, total:], (((1,), (1,)), ((), ())), preferred_element_type=jnp.float32
    ).astype(jnp.bfloat16)
    if outs[0].shape[1] > rows:
        outs[0][rows:, rows:] = jnp.zeros((16, outs[0].shape[1] - rows), jnp.bfloat16)
    start = 0
    for out in outs:
        out[:rows, :] = arrived_ref[:, start : start + out.shape[1]]
        start += out.shape[1]


def dense_kernel(list_ref, count_ref, weight_ref, dense_ref, scale_ref, token_ref, held, sems):
    blocks, _, size, _ = weight_ref.shape
    dom, z = lax.axis_index("dom"), lax.axis_index("grp")
    loads = [pltpu.make_async_copy(weight_ref.at[b], held.at[b], sems.at[b]) for b in range(blocks)]
    for load in loads:
        load.start()
    for b in range(blocks):
        dense_ref[pl.ds(b * size, size), :] = jnp.zeros((size, dense_ref.shape[1]), dense_ref.dtype)
    for b in range(blocks):
        span = pl.ds(b * size, size)
        loads[b].wait()

        def put(k, total):
            block = held[b, k]
            target = list_ref[b, k]
            column = steps_of(dom, z, target // blocks) * blocks + target % blocks
            start = pl.multiple_of(column * size, size)
            dense_ref[span, pl.ds(start, size)] = block
            return total + block.astype(jnp.float32)

        total = lax.fori_loop(0, count_ref[b], put, jnp.zeros((size, size), jnp.float32))
        degree = jnp.sum(total, axis=1, keepdims=True)
        scale_ref[span, :] = jnp.broadcast_to((1.0 - MIX) * lax.rsqrt(degree), (size, 128))
    token_ref[...] = jnp.zeros(token_ref.shape, token_ref.dtype)


def steps_of(dom, z, q):
    odd = dom % 2 == 1
    rx, fx = jnp.where(odd, 3, 1), jnp.where(odd, 1, 3)
    step = q ^ z
    return jnp.where(step == 0, 0, jnp.where(step == rx, 1, jnp.where(step == fx, 2, 3)))


def pick_kernel(rows_ref, *refs):
    pick_ref = refs[-1]
    nodes, size = pick_ref.shape[1:]
    dom, z = lax.axis_index("dom"), lax.axis_index("grp")
    coded = rows_ref[pl.ds(size, 16), :size].astype(jnp.float32).astype(jnp.int32)
    for k in range(2):
        p = coded[2 * k : 2 * k + 1, :] * 64 + coded[2 * k + 1 : 2 * k + 2, :]
        spot = steps_of(dom, z, p // size) * size + p % size
        for n in range(nodes // size):
            node = lax.broadcasted_iota(jnp.int32, (size, size), 0) + n * size
            pick_ref[k, pl.ds(n * size, size), :] = (node == spot).astype(jnp.bfloat16)


def part_kernel(pick_ref, near_ref, part_ref):
    size, width = pick_ref.shape[2], part_ref.shape[1]
    for n in range(part_ref.shape[0] // size):
        at = pl.ds(n * size, size)
        total = jnp.dot(pick_ref[0, at, :], near_ref[:size, :width], preferred_element_type=jnp.float32)
        total += jnp.dot(pick_ref[1, at, :], near_ref[:size, width:], preferred_element_type=jnp.float32)
        part_ref[at, :] = total.astype(jnp.bfloat16)


def first_kernel(dense_a, dense_b, scale_a, scale_b, pick_ref, part_ref, far_ref, base_ref, hidden_ref, panel):
    size = dense_a.shape[0]
    width = part_ref.shape[1]
    for n in range(panel.shape[0] // size):
        at = pl.ds(n * size, size)
        total = jnp.dot(pick_ref[0, at, :], far_ref[:size, :width], preferred_element_type=jnp.float32)
        total += jnp.dot(pick_ref[1, at, :], far_ref[:size, width:], preferred_element_type=jnp.float32)
        panel[at, :] = part_ref[at, :] + total.astype(jnp.bfloat16)
    for n, (dense, scale) in enumerate(((dense_a, scale_a), (dense_b, scale_b))):
        at = pl.ds(n * size, size)
        total = jnp.dot(dense[...], panel[...], preferred_element_type=jnp.float32)
        base = panel[at, :]
        base_ref[at, :] = base
        hidden_ref[at, :] = (MIX * base.astype(jnp.float32) + total * scale[:, 0:1]).astype(jnp.bfloat16)


def half_kernel(dense_a, dense_b, hidden_ref, total_ref):
    size = dense_a.shape[0]
    depth = hidden_ref.shape[0]
    for n, dense in enumerate((dense_a, dense_b)):
        total_ref[pl.ds(n * size, size), :] = jnp.dot(
            dense[:, :depth], hidden_ref[...], preferred_element_type=jnp.float32
        )


def finish(dense, scale, total_ref, hidden_ref, base_ref, at, out):
    depth = hidden_ref.shape[0]
    total = total_ref[at, :] + jnp.dot(dense[:, depth:], hidden_ref[...], preferred_element_type=jnp.float32)
    out[...] = (MIX * base_ref[at, :].astype(jnp.float32) + total * scale[:, 0:1]).astype(jnp.bfloat16)


def side_kernel(row, dense, scale, total_ref, hidden_ref, base_ref, after, out_ref):
    size = dense.shape[0]
    finish(dense, scale, total_ref, hidden_ref, base_ref, pl.ds(row * size, size), out_ref)


def move_halves(pieces, side, out_ref, sems):
    part = pieces[0].shape[1]
    copies = []
    for n, piece in enumerate(pieces):
        start = pl.multiple_of((side * len(pieces) + n) * part, part)
        copies.append(pltpu.make_async_copy(piece, out_ref.at[:, pl.ds(start, part)], sems.at[n]))
    for copy in copies:
        copy.start()
    for copy in copies:
        copy.wait()


def hold_kernel(sent_ref, after_0, after_1, back_ref):
    back_ref[...] = sent_ref[...]


def keep_kernel(keep_0, keep_1, out_ref, sems):
    dom, z = lax.axis_index("dom"), lax.axis_index("grp")
    move_halves((keep_0, keep_1), half_of(dom % 2 == 1, z), out_ref, sems)


def join_kernel(early_0, late_0, got_1, _, out_ref, sems):
    dom, z = lax.axis_index("dom"), lax.axis_index("grp")
    side = 1 - half_of(dom % 2 == 1, z)

    @pl.when(dom % 2 == 0)
    def _():
        move_halves((early_0, got_1), side, out_ref, sems)

    @pl.when(dom % 2 == 1)
    def _():
        move_halves((late_0, got_1), side, out_ref, sems)


def row_step(core):
    return 1 if core == 0 else 3


def shards(doms, depth, encoded, owner_of, nbr_blocks, nbr_count, edge_weights):
    f32, bf16, i32 = jnp.float32, jnp.bfloat16, jnp.int32
    rows, width = encoded.shape
    half = width // 2
    blocks, slots, size, _ = edge_weights.shape
    nodes = rows * depth
    devices = [(d, q) for d in range(doms) for q in range(depth)]
    row_pairs = [(d * depth + q, d * depth + (q ^ row_step(d % 2))) for d, q in devices]
    col_pairs = [(d * depth + q, d * depth + (q ^ row_step(1 - d % 2))) for d, q in devices]

    def to_row(a):
        return lax.ppermute(a, AXES, row_pairs)

    def to_col(a):
        return lax.ppermute(a, AXES, col_pairs)

    def to_row_of(core, a):
        return lax.ppermute(a, AXES, [(d * depth + q, d * depth + (q ^ row_step(core))) for d, q in devices])

    far_blocks, far_count = to_row(nbr_blocks), to_row(nbr_count)

    def dense_of(lists, count, weights, limit, work=0):
        return kernel_call(
            dense_kernel,
            (
                jax.ShapeDtypeStruct((blocks * size, nodes), bf16),
                jax.ShapeDtypeStruct((blocks * size, 128), f32),
                jax.ShapeDtypeStruct((8, 128), f32),
            ),
            [SMEM, SMEM, ANY],
            work,
            8 << 20,
            scratch=[pltpu.VMEM(weights.shape, bf16), pltpu.SemaphoreType.DMA((blocks,))],
            limit=limit,
        )(lists, count, weights)

    held = pltpu.VMEM((2, rows, half), f32)
    other = jax.ShapeDtypeStruct((rows // 2 + 16, half), bf16)
    other_0, other_1, pick, place = kernel_call(
        functools.partial(sort_kernel, doms),
        (other, other, jax.ShapeDtypeStruct((rows, rows), bf16), jax.ShapeDtypeStruct((16, rows), bf16)),
        [ANY, ANY],
        2 * rows * rows * half,
        4 << 20,
        scratch=[held, pltpu.VMEM((1, rows), i32), pltpu.SemaphoreType.DMA((3,))],
        limit=58,
    )(owner_of.reshape(1, rows), encoded)
    row_0, row_1 = to_row_of(0, other_0), to_row_of(1, other_1)
    per = rows // doms
    mine = kernel_call(
        functools.partial(mine_kernel, per),
        jax.ShapeDtypeStruct((rows, half), bf16),
        [ANY, VMEM],
        2 * rows * rows * half,
        4 << 20,
        scratch=[held, pltpu.SemaphoreType.DMA((2,))],
        limit=50,
    )(encoded, pick)
    sent_weights, mine, far_blocks, far_count = lax.optimization_barrier(
        (edge_weights, mine, far_blocks, far_count)
    )
    far_weights = to_row(sent_weights)
    packed = pl.pallas_call(
        functools.partial(pack_kernel, per),
        out_shape=jax.ShapeDtypeStruct((rows, width + 128), bf16),
        in_specs=[VMEM] * 3 + [ANY],
        out_specs=ANY,
        scratch_shapes=[pltpu.VMEM((rows, half + 128), bf16), pltpu.SemaphoreType.DMA((3 * len(WIDTHS),))],
        compiler_params=pltpu.CompilerParams(vmem_limit_bytes=10 << 20),
        cost_estimate=pl.CostEstimate(flops=1 << 20, bytes_accessed=2 << 20, transcendentals=0),
    )(place, row_0, row_1, mine)

    packed = lax.all_to_all(packed, "dom", 0, 0, tiled=True)
    dense_a, scale_a, token_a = dense_of(nbr_blocks, nbr_count, edge_weights, 50, 40_000_000_000)
    near_rows = kernel_call(
        place_kernel,
        tuple(jax.ShapeDtypeStruct((rows + (16 if c == 0 else 0), 2 * w), bf16) for c, w in enumerate(WIDTHS)),
        [VMEM, ANY],
        1 << 20,
        1 << 20,
    )(packed, token_a)
    far_rows = [to_col(a) for a in near_rows]

    dense_b, scale_b, token_b = dense_of(far_blocks, far_count, far_weights, 10)

    def picks_of(first_rows, *after):
        return kernel_call(
            pick_kernel,
            jax.ShapeDtypeStruct((2, nodes, rows), bf16),
            [VMEM] + [ANY] * len(after),
            1 << 20,
            4 << 20,
        )(first_rows, *after)

    near_picks = picks_of(near_rows[0], token_a)
    placed = [
        kernel_call(
            part_kernel,
            jax.ShapeDtypeStruct((nodes, part), bf16),
            [VMEM] * 2,
            4 * nodes * rows * part,
            4 << 20,
        )(near_picks, near_rows[c])
        for c, part in enumerate(WIDTHS)
    ]
    far_picks = picks_of(far_rows[0], token_b, *placed)

    mine_n = 2 * rows
    steps = []
    for c, part in enumerate(WIDTHS):
        base, hidden = kernel_call(
            first_kernel,
            (jax.ShapeDtypeStruct((mine_n, part), bf16), jax.ShapeDtypeStruct((mine_n, part), bf16)),
            [VMEM] * 7,
            4 * nodes * rows * part + 2 * mine_n * nodes * part,
            4 << 20,
            scratch=[pltpu.VMEM((nodes, part), bf16)],
        )(dense_a, dense_b, scale_a, scale_b, far_picks, placed[c], far_rows[c])
        far_hidden = to_col(hidden)
        running = kernel_call(
            half_kernel,
            jax.ShapeDtypeStruct((mine_n, part), f32),
            [VMEM] * 3,
            2 * mine_n * mine_n * part,
            4 << 20,
        )(dense_a, dense_b, hidden)
        steps.append((running, far_hidden, base))

    part = WIDTHS[0]
    out_shape = jax.ShapeDtypeStruct((rows, part), bf16)
    work = 2 * rows * mine_n * part
    def side(row, step, after):
        dense, scale = ((dense_a, scale_a), (dense_b, scale_b))[row]
        return kernel_call(functools.partial(side_kernel, row), out_shape, [VMEM] * 5 + [ANY], work, 2 << 20)(
            dense, scale, *steps[step], after
        )

    send_0 = side(1, 0, steps[1][0])
    send_1 = side(1, 1, send_0)
    keep_0 = side(0, 0, send_1)
    keep_1 = side(0, 1, send_1)
    kept, sent = [keep_0, keep_1], [send_0, send_1]

    def to_row_on(core, a):
        return lax.ppermute(a, AXES, [(p, q) for p, q in row_pairs if p // depth % 2 == core])

    early_0 = to_row_on(0, sent[0])
    got_1 = to_row(sent[1])
    whole = jax.ShapeDtypeStruct((rows, width), bf16)
    held_back = kernel_call(hold_kernel, out_shape, [VMEM, ANY, ANY], 0, 1 << 19)(sent[0], early_0, sent[1])
    late_0 = to_row_on(1, held_back)
    half_done = pl.pallas_call(
        keep_kernel,
        out_shape=whole,
        in_specs=[VMEM] * 2,
        out_specs=ANY,
        scratch_shapes=[pltpu.SemaphoreType.DMA((2,))],
        compiler_params=pltpu.CompilerParams(vmem_limit_bytes=8 << 20),
    )(*kept)
    return pl.pallas_call(
        join_kernel,
        out_shape=whole,
        in_specs=[VMEM] * 3 + [ANY],
        out_specs=ANY,
        input_output_aliases={3: 0},
        scratch_shapes=[pltpu.SemaphoreType.DMA((2,))],
        compiler_params=pltpu.CompilerParams(vmem_limit_bytes=8 << 20),
    )(early_0, late_0, got_1, half_done)


def solution(mesh):
    return jax.shard_map(
        functools.partial(shards, mesh.shape["dom"], mesh.shape["grp"]),
        mesh=mesh,
        in_specs=(P(AXES, None), P(AXES), P(AXES, None), P(AXES), P(AXES, None, None, None)),
        out_specs=P(AXES, None),
        check_vma=False,
    )
```
